32 devices in a mesh: dp: 16 (over z, x, core), mp: 2 (over y).
Axes of the slice: x: 2, y: 2, z: 4, core: 2. Of those that a mesh axis runs over, the one named last changes fastest.
Arguments:
- tokens: bfloat16 [32768, 1024], P(('dp', 'mp')), may hold values from -6 to 6
- first_values: bfloat16 [32768, 1024], P('dp', 'mp'), may hold values from -6 to 6
- lengths: int32 [16], P('dp'), may hold values from 128 to 2048, as said below
- cotangent: bfloat16 [32768, 1024], P(('dp', 'mp')), may hold values from -6 to 6
- w_qkv: float32 [1024, 3, 1024], P(None, None, 'mp'), may hold values from -0.1875 to 0.1875
- w_out: float32 [1024, 1024], P('mp'), may hold values from -4 to 4
- w_gateup: float32 [1024, 2, 2816], P(None, None, 'mp'), may hold values from -0.1875 to 0.1875
- w_down: float32 [2816, 1024], P('mp'), may hold values from -0.109375 to 0.109375
- gains: float32 [2, 1024], replicated, may hold values from 0.4 to 1.8
- moment_qkv: float32 [1024, 3, 1024], P('dp', None, 'mp'), may hold values from -3 to 3
- moment_out: float32 [1024, 1024], P('mp', 'dp'), may hold values from -0.15625 to 0.15625
- moment_gateup: float32 [1024, 2, 2816], P('dp', None, 'mp'), may hold values from -1.25 to 1.25
- moment_down: float32 [2816, 1024], P('mp', 'dp'), may hold values from -2.5 to 2.5
- moment_gains: float32 [2, 1024], replicated, may hold values from -2.5 to 2.5
- average_qkv: float32 [1024, 3, 1024], P('dp', None, 'mp'), may hold values from -0.1875 to 0.1875
- average_out: float32 [1024, 1024], P('mp', 'dp'), may hold values from -12 to 12
- average_gateup: float32 [1024, 2, 2816], P('dp', None, 'mp'), may hold values from -0.1875 to 0.1875
- average_down: float32 [2816, 1024], P('mp', 'dp'), may hold values from -0.109375 to 0.109375
- average_gains: float32 [2, 1024], replicated, may hold values from 0.5 to 1.5
Outputs:
- output: bfloat16 [32768, 1024], P(('dp', 'mp'))
- input_grad: float32 [32768, 1024], P(('dp', 'mp'))
- first_values_grad: float32 [32768, 1024], P('dp', 'mp')
- qkv_grad: float32 [1024, 3, 1024], P('dp', None, 'mp')
- qkv_moment: float32 [1024, 3, 1024], P('dp', None, 'mp')
- qkv_average: float32 [1024, 3, 1024], P('dp', None, 'mp')
- qkv_weight: float32 [1024, 3, 1024], P('dp', None, 'mp')
- out_grad: float32 [1024, 1024], P('mp', 'dp')
- out_moment: float32 [1024, 1024], P('mp', 'dp')
- out_average: float32 [1024, 1024], P('mp', 'dp')
- out_weight: float32 [1024, 1024], P('mp', 'dp')
- gateup_grad: float32 [1024, 2, 2816], P('dp', None, 'mp')
- gateup_moment: float32 [1024, 2, 2816], P('dp', None, 'mp')
- gateup_average: float32 [1024, 2, 2816], P('dp', None, 'mp')
- gateup_weight: float32 [1024, 2, 2816], P('dp', None, 'mp')
- down_grad: float32 [2816, 1024], P('mp', 'dp')
- down_moment: float32 [2816, 1024], P('mp', 'dp')
- down_average: float32 [2816, 1024], P('mp', 'dp')
- down_weight: float32 [2816, 1024], P('mp', 'dp')
- gains_grad: float32 [2, 1024], replicated
- gains_moment: float32 [2, 1024], replicated
- gains_average: float32 [2, 1024], replicated
- gains_new: float32 [2, 1024], replicated
The draws below stay inside these ranges and needn't reach their ends.
Inputs may be any that keep to these rules, and one draw needn't show every extreme that they name: `lengths`: valid tokens of each of the 16 slots; some slot holds 2048 and some holds exactly 128.
All inputs are finite; a program needn't handle non-finite values.
Results may differ from the reference program's by a relative error of at most 0.014.
Values may be sent and summed in bfloat16 or wider, within the bound.
No kernel may reach another device: no remote copies, remote signals or barrier semaphores. Data moves between devices by JAX's collectives and lax.ppermute only.
A program may use at most 320 MiB of HBM per device.

```python
import math
import jax
import jax.numpy as jnp
from jax import lax

D = 1024
HEADS = 16
HEAD_DIM = 64
FF = 2816
SEQ = 2048
MIN_LEN = 128
SLOTS_DEV = 1
SLOTS = 16
TOKENS = 32768
N_DP = 16


def draw_lengths(key, part):
    key = jax.random.fold_in(key, 11)
    key_first, key_second, key_long, key_short = jax.random.split(key, 4)
    length_range = SEQ - MIN_LEN + 1
    first_draw = jax.random.randint(key_first, (SLOTS,), 0, length_range)
    second_draw = jax.random.randint(key_second, (SLOTS,), 0, length_range)
    skewed = MIN_LEN + first_draw * second_draw // length_range
    longest = jax.random.randint(key_long, (), 0, SLOTS)
    shortest = (longest + 1 + jax.random.randint(key_short, (), 0, SLOTS - 1)) % SLOTS
    positions = jnp.arange(SLOTS)
    result = jnp.where(positions == longest, SEQ, jnp.where(positions == shortest, MIN_LEN, skewed))
    return result.astype(jnp.int32)


def draw_gains(key, part):
    key = jax.random.fold_in(key, 12)
    noise = jax.random.uniform(key, (2, D), jnp.float32, -1.0, 1.0)
    ramp = 0.5 + jnp.arange(D, dtype=jnp.float32) / (D - 1)
    return ramp[None, :] * (1.0 + 0.2 * noise)


def steps_of(own_key, dims, cuts, smallest, top_value):
    def one(position, shards_of):
        draws = jax.random.uniform(jax.random.fold_in(jax.random.fold_in(own_key, 6), position), (shards_of,), jnp.float32, smallest / len(cuts), top_value / len(cuts))
        return jnp.repeat(jnp.exp(draws), dims[position] // shards_of).reshape((-1,) + (1,) * (len(dims) - position - 1))

    factor_of = one(*cuts[0])
    for cut in cuts[1:]:
        factor_of = factor_of * one(*cut)
    return factor_of


def normal_values(stream_key, shape, deviation, reach, shards=(), kind=jnp.bfloat16):
    values = jax.random.normal(stream_key, shape, jnp.float32) * deviation
    if len(shards) > 0:
        values = steps_of(stream_key, shape, shards, -0.22, 0.18) * values
    return jnp.clip(values, min=-reach, max=reach).astype(kind)


def setup_inputs(seed: int = 0) -> dict:
    key_of = jax.random.split(jax.random.key(seed), 20)
    return {
        "tokens": normal_values(key_of[0], (TOKENS, D), 1.0, 6.0, ((0, 32),)),
        "first_values": normal_values(key_of[1], (TOKENS, D), 1.0, 6.0, ((0, 16), (1, 2))),
        "lengths": draw_lengths(jax.random.fold_in(key_of[19], 71), 0),
        "cotangent": normal_values(key_of[3], (TOKENS, D), 1.0, 6.0, ((0, 32),)),
        "w_qkv": normal_values(key_of[4], (D, 3, D), D ** -0.5, 0.1875, ((2, 2),), jnp.float32),
        "w_out": normal_values(key_of[5], (D, D), (max(D * 4 // SEQ, 1)) ** -0.5, 4.0, ((0, 2),), jnp.float32),
        "w_gateup": normal_values(key_of[6], (D, 2, FF), D ** -0.5, 0.1875, ((2, 2),), jnp.float32),
        "w_down": normal_values(key_of[7], (FF, D), FF ** -0.5, 0.109375, ((0, 2),), jnp.float32),
        "gains": draw_gains(jax.random.fold_in(key_of[19], 71), 0),
        "moment_qkv": normal_values(key_of[9], (D, 3, D), 0.5, 3.0, ((0, 16), (2, 2)), jnp.float32),
        "moment_out": normal_values(key_of[10], (D, D), 0.025, 0.15625, ((0, 2), (1, 16)), jnp.float32),
        "moment_gateup": normal_values(key_of[11], (D, 2, FF), 0.2, 1.25, ((0, 16), (2, 2)), jnp.float32),
        "moment_down": normal_values(key_of[12], (FF, D), 0.4, 2.5, ((0, 2), (1, 16)), jnp.float32),
        "moment_gains": normal_values(key_of[13], (2, D), 0.4, 2.5, (), jnp.float32),
        "average_qkv": normal_values(key_of[14], (D, 3, D), D ** -0.5, 0.1875, ((0, 16), (2, 2)), jnp.float32),
        "average_out": normal_values(key_of[15], (D, D), (3.0 / max(D * 4 // SEQ, 1) ** 0.5), 12.0, ((0, 2), (1, 16)), jnp.float32),
        "average_gateup": normal_values(key_of[16], (D, 2, FF), D ** -0.5, 0.1875, ((0, 16), (2, 2)), jnp.float32),
        "average_down": normal_values(key_of[17], (FF, D), FF ** -0.5, 0.109375, ((0, 2), (1, 16)), jnp.float32),
        "average_gains": jnp.clip(jax.random.uniform(key_of[18], (2, D), jnp.float32, 0.5, 1.5), 0.5, 1.5),
    }


EPS = 1e-06
NEG_BIG = -1e+30
HALF = 0.5
MOMENTUM = 0.5
AVERAGE_DECAY = 0.5
RATE_QKV = 0.05
RATE_OUT = 20.0
RATE_GATEUP = 0.12
RATE_DOWN = 0.04
RATE_GAINS = 0.6
HIGH = lax.Precision.HIGHEST

@jax.custom_vjp
def low(v):
    return lax.optimization_barrier(v.astype(jnp.bfloat16)).astype(jnp.float32)

@jax.custom_vjp
def low_back(v):
    return v

def low_keep(v):
    return (low(v), None)

def low_pass(kept, grad):
    return (grad,)

def back_keep(v):
    return (v, None)

def back_low(kept, grad):
    return (low(grad),)
low.defvjp(low_keep, low_pass)
low_back.defvjp(back_keep, back_low)

def rms_norm(values, gain):
    return values * lax.rsqrt(lax.optimization_barrier(jnp.mean(values * values, axis=-1, keepdims=True)) + EPS) * gain

def rope_tables(length, head_size):
    half_size = head_size // 2
    freqs = jnp.power(10000.0, -2.0 * jnp.arange(half_size, dtype=jnp.float32) / head_size)
    angles = jnp.arange(length, dtype=jnp.float32)[:, None] * freqs[None, :]
    return (jnp.cos(angles)[:, None, :], jnp.sin(angles)[:, None, :])

def rotate(values, cosine, sine):
    half_size = values.shape[-1] // 2
    first_half = values[..., :half_size]
    second_half = values[..., half_size:]
    return jnp.concatenate([first_half * cosine - second_half * sine, second_half * cosine + first_half * sine], axis=-1)

def attend_slot(queries, keys, values, length):
    block_len = min(512, SEQ)
    blocks = SEQ // block_len
    scale = 1.0 / math.sqrt(HEAD_DIM)

    def per_block(item):
        query_block, start = item
        scores = jnp.einsum('qhd,khd->hqk', query_block, keys, precision=HIGH) * scale
        scores = low_back(scores)
        query_pos = start + jnp.arange(block_len, dtype=jnp.int32)
        key_pos = jnp.arange(SEQ, dtype=jnp.int32)
        allowed = (key_pos[None, :] <= query_pos[:, None]) & (key_pos[None, :] < length)
        scores = jnp.where(allowed[None], scores, NEG_BIG)
        probs = jax.nn.softmax(scores, axis=-1)
        return jnp.einsum('hqk,khd->qhd', low(probs), values, precision=HIGH)
    starts = jnp.arange(blocks, dtype=jnp.int32) * block_len
    mixed = lax.map(jax.checkpoint(per_block), (queries.reshape(blocks, block_len, HEADS, HEAD_DIM), starts))
    return mixed.reshape(SEQ, D)

def forward(params, x_group, first_group, lens_group):
    w_qkv, w_out, w_gateup, w_down, gains = params
    n_one = low(rms_norm(x_group, gains[0]))
    qkv = jnp.einsum('gsd,dc->gsc', n_one, low(w_qkv).reshape(D, 3 * D), precision=HIGH)
    qkv = low_back(qkv).reshape(SLOTS_DEV, SEQ, 3, HEADS, HEAD_DIM)
    cosine, sine = rope_tables(SEQ, HEAD_DIM)
    queries = low(rotate(qkv[:, :, 0], cosine, sine))
    keys = low(rotate(qkv[:, :, 1], cosine, sine))
    values = low(HALF * qkv[:, :, 2] + HALF * first_group.reshape(SLOTS_DEV, SEQ, HEADS, HEAD_DIM))
    mixed = lax.map(lambda item: attend_slot(item[0], item[1], item[2], item[3]), (queries, keys, values, lens_group))
    mixed = low(low_back(mixed))
    projected = low_back(jnp.einsum('gsc,cd->gsd', mixed, low(w_out), precision=HIGH))
    resid = x_group + projected
    n_two = low(rms_norm(resid, gains[1]))
    gateup = low_back(jnp.einsum('gsd,dc->gsc', n_two, low(w_gateup).reshape(D, 2 * FF), precision=HIGH))
    gate_val = gateup[..., :FF]
    up_val = gateup[..., FF:]
    hidden = low(jax.nn.silu(gate_val) * up_val)
    return resid + jnp.einsum('gsf,fd->gsd', hidden, low(w_down), precision=HIGH)

def nesterov(grad, weight, moment, average, rate):
    moment_new = MOMENTUM * moment + grad
    weight_new = weight - rate * (grad + MOMENTUM * moment_new)
    average_new = AVERAGE_DECAY * average + (1.0 - AVERAGE_DECAY) * weight_new
    return (grad, moment_new, average_new, weight_new)

def reference(tokens, first_values, lengths, cotangent, w_qkv, w_out, w_gateup, w_down, gains, moment_qkv, moment_out, moment_gateup, moment_down, moment_gains, average_qkv, average_out, average_gateup, average_down, average_gains):
    params = (w_qkv, w_out, w_gateup, w_down, gains)
    x_all = tokens.astype(jnp.float32).reshape(N_DP, SLOTS_DEV, SEQ, D)
    first_all = first_values.astype(jnp.float32).reshape(N_DP, SLOTS_DEV, SEQ, D)
    grads_all = cotangent.astype(jnp.float32).reshape(N_DP, SLOTS_DEV, SEQ, D)
    lens_all = lengths.reshape(N_DP, SLOTS_DEV)
    zeros = jax.tree.map(jnp.zeros_like, params)

    def group_step(total, item):
        x_group, first_group, grad_group, lens_group = item
        valid = (jnp.arange(SEQ, dtype=jnp.int32)[None, :] < lens_group[:, None]).astype(jnp.float32)
        result, pull = jax.vjp(lambda p, a, b: forward(p, a, b, lens_group), params, x_group, first_group)
        grad_params, grad_x, grad_first = pull(grad_group * valid[..., None])
        total = jax.tree.map(lambda acc, new: acc + new, total, grad_params)
        return (total, (result.astype(jnp.bfloat16), grad_x, grad_first))
    total, (results, grad_x, grad_first) = lax.scan(group_step, zeros, (x_all, first_all, grads_all, lens_all))
    root_count = math.sqrt(TOKENS)
    g_qkv, g_out, g_gateup, g_down, g_gains = jax.tree.map(lambda g: g / root_count, total)
    qkv_set = nesterov(g_qkv, w_qkv, moment_qkv, average_qkv, RATE_QKV)
    out_set = nesterov(g_out, w_out, moment_out, average_out, RATE_OUT)
    gateup_set = nesterov(g_gateup, w_gateup, moment_gateup, average_gateup, RATE_GATEUP)
    down_set = nesterov(g_down, w_down, moment_down, average_down, RATE_DOWN)
    gains_set = nesterov(g_gains, gains, moment_gains, average_gains, RATE_GAINS)
    return (results.reshape(TOKENS, D), grad_x.reshape(TOKENS, D), grad_first.reshape(TOKENS, D), qkv_set[0], qkv_set[1], qkv_set[2], qkv_set[3], out_set[0], out_set[1], out_set[2], out_set[3], gateup_set[0], gateup_set[1], gateup_set[2], gateup_set[3], down_set[0], down_set[1], down_set[2], down_set[3], gains_set[0], gains_set[1], gains_set[2], gains_set[3])
```

```python
import functools
import math

import jax
import jax.numpy as jnp
from jax import lax
from jax.experimental import pallas as pl
from jax.experimental.pallas import tpu as pltpu
from jax.sharding import PartitionSpec as P

HEAD_DIM = 64


EPS = 1e-06
NEG_BIG = -1e30
HALF = 0.5
MOMENTUM = 0.5
AVERAGE_DECAY = 0.5
RATE_QKV = 0.05
RATE_OUT = 20.0
RATE_GATEUP = 0.12
RATE_DOWN = 0.04
RATE_GAINS = 0.6


def normalize(values, gain):
    inverse = lax.rsqrt(jnp.mean(values * values, axis=-1, keepdims=True) + EPS)
    unit = values * inverse
    return (unit * gain, unit, inverse)


def norm_back(grad_norm, gain, unit, inverse):
    scaled = grad_norm * gain
    return inverse * (scaled - unit * jnp.mean(scaled * unit, axis=-1, keepdims=True))


def rope_tables(length, head_size):
    half_size = head_size // 2
    freqs = jnp.power(10000.0, -2.0 * jnp.arange(half_size, dtype=jnp.float32) / head_size)
    angles = jnp.arange(length, dtype=jnp.float32)[:, None] * freqs[None, :]
    return (jnp.cos(angles)[:, None, :], jnp.sin(angles)[:, None, :])


def rotate(values, cosine, sine):
    half_size = values.shape[-1] // 2
    first_half = values[..., :half_size]
    second_half = values[..., half_size:]
    return jnp.concatenate(
        [first_half * cosine - second_half * sine, second_half * cosine + first_half * sine],
        axis=-1,
    )


def unrotate(grads, cosine, sine):
    half_size = grads.shape[-1] // 2
    first_half = grads[..., :half_size]
    second_half = grads[..., half_size:]
    return jnp.concatenate(
        [first_half * cosine + second_half * sine, second_half * cosine - first_half * sine],
        axis=-1,
    )


def dot_last(left, right):
    return lax.dot_general(
        left, right, (((1,), (1,)), ((), ())), preferred_element_type=jnp.float32
    )


def dot_first(left, right):
    return lax.dot_general(
        left, right, (((0,), (0,)), ((), ())), preferred_element_type=jnp.float32
    )


def block_scores(query_block, keys, start, length, scale):
    block_len = query_block.shape[0]
    key_len = keys.shape[0]
    scores = (
        jnp.einsum("qhd,khd->hqk", query_block, keys, preferred_element_type=jnp.float32) * scale
    )
    query_pos = start + jnp.arange(block_len, dtype=jnp.int32)
    key_pos = jnp.arange(key_len, dtype=jnp.int32)
    allowed = (key_pos[None, :] <= query_pos[:, None]) & (key_pos[None, :] < length)
    return jnp.where(allowed[None], scores, NEG_BIG)


def attend_forward(queries, keys, values, lengths):
    slot_count, slot_len, heads_here, head_size = queries.shape
    block_len = min(512, slot_len)
    blocks = slot_len // block_len
    scale = 1.0 / math.sqrt(head_size)
    starts = jnp.arange(blocks, dtype=jnp.int32) * block_len

    def per_slot(item):
        slot_queries, slot_keys, slot_values, length = item

        def per_block(inner):
            query_block, start = inner
            scores = block_scores(query_block, slot_keys, start, length, scale)
            peak = jnp.max(scores, axis=-1, keepdims=True)
            raw_weights = jnp.exp(scores - peak)
            total = jnp.sum(raw_weights, axis=-1, keepdims=True)
            probs = raw_weights / total
            mixed = jnp.einsum(
                "hqk,khd->qhd",
                probs.astype(jnp.bfloat16),
                slot_values,
                preferred_element_type=jnp.float32,
            )
            return (mixed, (peak + jnp.log(total))[..., 0])

        mixed, log_totals = lax.map(
            per_block, (slot_queries.reshape(blocks, block_len, heads_here, head_size), starts)
        )
        return (mixed.reshape(slot_len, heads_here, head_size), log_totals)

    return lax.map(per_slot, (queries, keys, values, lengths))


def attend_backward(queries, keys, values, lengths, grad_mixed, log_totals):
    slot_count, slot_len, heads_here, head_size = queries.shape
    block_len = min(512, slot_len)
    blocks = slot_len // block_len
    scale = 1.0 / math.sqrt(head_size)
    starts = jnp.arange(blocks, dtype=jnp.int32) * block_len

    def per_slot(item):
        slot_queries, slot_keys, slot_values, length, slot_grads, slot_totals = item

        def per_block(carry, inner):
            key_grad, value_grad = carry
            query_block, grad_block, total_block, start = inner
            scores = block_scores(query_block, slot_keys, start, length, scale)
            probs = jnp.exp(scores - total_block[..., None])
            prob_grad = jnp.einsum(
                "qhd,khd->hqk", grad_block, slot_values, preferred_element_type=jnp.float32
            )
            center = jnp.sum(probs * prob_grad, axis=-1, keepdims=True)
            score_grad = (probs * (prob_grad - center)).astype(jnp.bfloat16)
            query_grad = (
                jnp.einsum(
                    "hqk,khd->qhd", score_grad, slot_keys, preferred_element_type=jnp.float32
                )
                * scale
            )
            key_grad = (
                key_grad
                + jnp.einsum(
                    "hqk,qhd->khd", score_grad, query_block, preferred_element_type=jnp.float32
                )
                * scale
            )
            value_grad = value_grad + jnp.einsum(
                "hqk,qhd->khd",
                probs.astype(jnp.bfloat16),
                grad_block,
                preferred_element_type=jnp.float32,
            )
            return ((key_grad, value_grad), query_grad)

        empty = jnp.zeros((slot_len, heads_here, head_size), jnp.float32)
        shaped_queries = slot_queries.reshape(blocks, block_len, heads_here, head_size)
        shaped_grads = slot_grads.reshape(blocks, block_len, heads_here, head_size)
        (key_grad, value_grad), query_grad = lax.scan(
            per_block, (empty, empty), (shaped_queries, shaped_grads, slot_totals, starts)
        )
        return (query_grad.reshape(slot_len, heads_here, head_size), key_grad, value_grad)

    return lax.map(per_slot, (queries, keys, values, lengths, grad_mixed, log_totals))


def row_valid(lengths, slot_len, start, count):
    index = start + jnp.arange(count, dtype=jnp.int32)
    slot_of = index // slot_len
    place = index % slot_len
    slot_ids = jnp.arange(lengths.shape[0], dtype=jnp.int32)
    limit = jnp.sum(jnp.where(slot_of[:, None] == slot_ids[None, :], lengths[None, :], 0), axis=1)
    return (place < limit).astype(jnp.float32)


def nesterov(grad, weight, moment, average, rate):
    moment_new = MOMENTUM * moment + grad
    weight_new = weight - rate * (grad + MOMENTUM * moment_new)
    average_new = AVERAGE_DECAY * average + (1.0 - AVERAGE_DECAY) * weight_new
    return (grad, moment_new, average_new, weight_new)


def shards_any(
    tokens,
    first_values,
    lengths,
    cotangent,
    w_qkv,
    w_out,
    w_gateup,
    w_down,
    gains,
    moment_qkv,
    moment_out,
    moment_gateup,
    moment_down,
    moment_gains,
    average_qkv,
    average_out,
    average_gateup,
    average_down,
    average_gains,
):
    local_rows, model = tokens.shape
    mp_count = lax.axis_size("mp")
    dp_count = lax.axis_size("dp")
    mp_index = lax.axis_index("mp")
    dp_index = lax.axis_index("dp")
    slot_count = lengths.shape[0]
    group_rows = local_rows * mp_count
    slot_len = group_rows // slot_count
    head_cols = w_qkv.shape[2]
    hidden_cols = w_gateup.shape[2]
    heads_here = head_cols // HEAD_DIM
    row_start = mp_index * local_rows
    all_tokens = group_rows * dp_count
    root_count = math.sqrt(all_tokens)
    qkv_bf = w_qkv.astype(jnp.bfloat16).reshape(model, 3 * head_cols)
    out_bf = w_out.astype(jnp.bfloat16)
    gateup_bf = w_gateup.astype(jnp.bfloat16).reshape(model, 2 * hidden_cols)
    down_bf = w_down.astype(jnp.bfloat16)
    gain_one = gains[0]
    gain_two = gains[1]
    valid_local = row_valid(lengths, slot_len, row_start, local_rows)
    x_local = tokens.astype(jnp.float32)
    x_group = lax.all_gather(tokens, "mp", axis=0, tiled=True).astype(jnp.float32)
    norm_one, unit_one, inverse_one = normalize(x_group, gain_one)
    norm_one_bf = norm_one.astype(jnp.bfloat16)
    qkv = jnp.dot(norm_one_bf, qkv_bf, preferred_element_type=jnp.float32)
    qkv = qkv.reshape(slot_count, slot_len, 3, heads_here, HEAD_DIM)
    cosine, sine = rope_tables(slot_len, HEAD_DIM)
    queries = rotate(qkv[:, :, 0], cosine, sine).astype(jnp.bfloat16)
    keys = rotate(qkv[:, :, 1], cosine, sine).astype(jnp.bfloat16)
    first_shaped = first_values.astype(jnp.float32).reshape(
        slot_count, slot_len, heads_here, HEAD_DIM
    )
    values = (HALF * qkv[:, :, 2] + HALF * first_shaped).astype(jnp.bfloat16)
    mixed, log_totals = attend_forward(queries, keys, values, lengths)
    mixed_bf = mixed.reshape(group_rows, head_cols).astype(jnp.bfloat16)
    resid_local = x_local + lax.psum_scatter(
        jnp.dot(mixed_bf, out_bf, preferred_element_type=jnp.float32),
        "mp",
        scatter_dimension=0,
        tiled=True,
    )
    norm_two_local, unit_two, inverse_two = normalize(resid_local, gain_two)
    norm_two_bf = lax.all_gather(norm_two_local.astype(jnp.bfloat16), "mp", axis=0, tiled=True)
    gateup = jnp.dot(norm_two_bf, gateup_bf, preferred_element_type=jnp.float32)
    gate_val = gateup[:, :hidden_cols]
    up_val = gateup[:, hidden_cols:]
    sigmoid_gate = jax.nn.sigmoid(gate_val)
    silu_gate = gate_val * sigmoid_gate
    hidden_bf = (silu_gate * up_val).astype(jnp.bfloat16)
    result_local = resid_local + lax.psum_scatter(
        jnp.dot(hidden_bf, down_bf, preferred_element_type=jnp.float32),
        "mp",
        scatter_dimension=0,
        tiled=True,
    )
    output = result_local.astype(jnp.bfloat16)
    grad_local = (cotangent.astype(jnp.float32) * valid_local[:, None]).astype(jnp.bfloat16)
    grad_group = lax.all_gather(grad_local, "mp", axis=0, tiled=True)
    grad_down = dot_first(hidden_bf, grad_group)
    grad_hidden = dot_last(grad_group, down_bf)
    grad_gate = grad_hidden * up_val * sigmoid_gate * (1.0 + gate_val * (1.0 - sigmoid_gate))
    grad_up = grad_hidden * silu_gate
    grad_gateup_bf = jnp.concatenate([grad_gate, grad_up], axis=1).astype(jnp.bfloat16)
    grad_gateup = dot_first(norm_two_bf, grad_gateup_bf)
    grad_norm_two = lax.psum_scatter(
        dot_last(grad_gateup_bf, gateup_bf), "mp", scatter_dimension=0, tiled=True
    )
    grad_resid_local = grad_local.astype(jnp.float32) + norm_back(
        grad_norm_two, gain_two, unit_two, inverse_two
    )
    gain_two_grad = jnp.sum(grad_norm_two * unit_two, axis=0)
    grad_resid_bf = lax.all_gather(grad_resid_local.astype(jnp.bfloat16), "mp", axis=0, tiled=True)
    grad_out = dot_first(mixed_bf, grad_resid_bf)
    grad_mixed = dot_last(grad_resid_bf, out_bf).astype(jnp.bfloat16)
    grad_mixed = grad_mixed.reshape(slot_count, slot_len, heads_here, HEAD_DIM)
    query_grad, key_grad, value_grad = attend_backward(
        queries, keys, values, lengths, grad_mixed, log_totals
    )
    first_values_grad = (HALF * value_grad).reshape(group_rows, head_cols)
    grad_qkv_bf = jnp.stack(
        [unrotate(query_grad, cosine, sine), unrotate(key_grad, cosine, sine), HALF * value_grad],
        axis=2,
    )
    grad_qkv_bf = grad_qkv_bf.reshape(group_rows, 3 * head_cols).astype(jnp.bfloat16)
    grad_qkv = dot_first(norm_one_bf, grad_qkv_bf)
    unit_local = lax.dynamic_slice_in_dim(unit_one, row_start, local_rows, 0)
    inverse_local = lax.dynamic_slice_in_dim(inverse_one, row_start, local_rows, 0)
    grad_norm_one = lax.psum_scatter(
        dot_last(grad_qkv_bf, qkv_bf).astype(jnp.bfloat16), "mp", scatter_dimension=0, tiled=True
    ).astype(jnp.float32)
    input_grad = grad_resid_local + norm_back(grad_norm_one, gain_one, unit_local, inverse_local)
    gain_one_grad = jnp.sum(grad_norm_one * unit_local, axis=0)
    sum_qkv, sum_out, sum_gateup, sum_down = (
        lax.psum_scatter(
            grad_qkv.reshape(model, 3, head_cols), "dp", scatter_dimension=0, tiled=True
        ),
        lax.psum_scatter(grad_out, "dp", scatter_dimension=1, tiled=True),
        lax.psum_scatter(
            grad_gateup.reshape(model, 2, hidden_cols), "dp", scatter_dimension=0, tiled=True
        ),
        lax.psum_scatter(grad_down, "dp", scatter_dimension=1, tiled=True),
    )
    gain_sum = lax.psum(jnp.stack([gain_one_grad, gain_two_grad], axis=0), ("dp", "mp"))
    share = model // dp_count
    own_qkv = lax.dynamic_slice_in_dim(w_qkv, dp_index * share, share, 0)
    own_out = lax.dynamic_slice_in_dim(w_out, dp_index * share, share, 1)
    own_gateup = lax.dynamic_slice_in_dim(w_gateup, dp_index * share, share, 0)
    own_down = lax.dynamic_slice_in_dim(w_down, dp_index * share, share, 1)
    qkv_set = nesterov(sum_qkv / root_count, own_qkv, moment_qkv, average_qkv, RATE_QKV)
    out_set = nesterov(sum_out / root_count, own_out, moment_out, average_out, RATE_OUT)
    gateup_set = nesterov(
        sum_gateup / root_count, own_gateup, moment_gateup, average_gateup, RATE_GATEUP
    )
    down_set = nesterov(sum_down / root_count, own_down, moment_down, average_down, RATE_DOWN)
    gains_set = nesterov(gain_sum / root_count, gains, moment_gains, average_gains, RATE_GAINS)
    return (
        output,
        input_grad,
        first_values_grad,
        qkv_set[0],
        qkv_set[1],
        qkv_set[2],
        qkv_set[3],
        out_set[0],
        out_set[1],
        out_set[2],
        out_set[3],
        gateup_set[0],
        gateup_set[1],
        gateup_set[2],
        gateup_set[3],
        down_set[0],
        down_set[1],
        down_set[2],
        down_set[3],
        gains_set[0],
        gains_set[1],
        gains_set[2],
        gains_set[3],
    )


F32 = jnp.float32
BF16 = jnp.bfloat16
LANES = 128
BLK = 256
PARTS = 3
SWAP = ((0, 1), (1, 0))
VMEM_MIB = 60


def nt(left, right):
    return lax.dot_general(left, right, (((1,), (1,)), ((), ())), preferred_element_type=F32)


def nn(left, right):
    return lax.dot_general(left, right, (((1,), (0,)), ((), ())), preferred_element_type=F32)


def tn(left, right):
    return lax.dot_general(left, right, (((0,), (0,)), ((), ())), preferred_element_type=F32)


def lane_of(rows):
    return lax.broadcasted_iota(jnp.int32, (rows, LANES), 1)


def params(mib):
    return pltpu.CompilerParams(vmem_limit_bytes=mib * 2**20)


def cost(flops, moved, exps=0):
    return pl.CostEstimate(flops=int(flops), bytes_accessed=int(moved), transcendentals=int(exps))


def partner_lanes(pair):
    lane = lane_of(pair.shape[0])
    return jnp.where((lane % HEAD_DIM) < HEAD_DIM // 2, pltpu.roll(pair, LANES - 32, 1), pltpu.roll(pair, 32, 1))


def pair_tables(length):
    cosine, sine = rope_tables(length, HEAD_DIM)
    cosine, sine = cosine[:, 0, :], sine[:, 0, :]
    wide_cos = jnp.concatenate([cosine] * 4, axis=1)
    wide_sin = jnp.concatenate([-sine, sine, -sine, sine], axis=1)
    return wide_cos, wide_sin


def qkv_kernel(base_ref, x_ref, first_ref, gain_ref, w_ref, cos_ref, sin_ref, *refs):
    n_ref, q_ref, k_ref, v_ref = refs[-4:]
    x = x_ref[...].astype(F32)
    inverse = lax.rsqrt(jnp.mean(x * x, axis=-1, keepdims=True) + EPS)
    norm = ((x * inverse) * gain_ref[...]).astype(BF16)
    n_ref[...] = norm
    cosine, sine = cos_ref[...], sin_ref[...]
    for part, out in ((0, q_ref), (1, k_ref)):
        flat = nn(norm, w_ref[part])
        for c in range(flat.shape[1] // LANES):
            pair = flat[:, c * LANES : (c + 1) * LANES]
            turned = (pair * cosine + partner_lanes(pair) * sine).astype(BF16)
            if part == 0:
                turned = turned * jnp.asarray(0.125, BF16)
            out[:, c * LANES : (c + 1) * LANES] = turned
    v_ref[...] = (HALF * nn(norm, w_ref[2]) + HALF * first_ref[...].astype(F32)).astype(BF16)


def project_qkv(base, x, first, gain, w, cosine, sine, before):
    rows, model = x.shape
    slot_len, cols = first.shape
    here = lambda i, b: (i, 0)
    there = lambda i, b: (b[0] + i, 0)
    outs = (
        jax.ShapeDtypeStruct((slot_len, model), BF16),
        *(jax.ShapeDtypeStruct((slot_len, cols), BF16) for _ in range(3)),
    )
    before = () if before is None else tuple(before)
    return pl.pallas_call(
        qkv_kernel,
        out_shape=outs,
        grid_spec=pltpu.PrefetchScalarGridSpec(
            num_scalar_prefetch=1,
            grid=(rows // BLK,),
            in_specs=[
                pl.BlockSpec((BLK, model), here),
                pl.BlockSpec((BLK, cols), there),
                pl.BlockSpec((1, model), lambda i, b: (0, 0)),
                pl.BlockSpec((PARTS, model, cols), lambda i, b: (0, 0, 0)),
                pl.BlockSpec((BLK, LANES), there),
                pl.BlockSpec((BLK, LANES), there),
                *(pl.BlockSpec(memory_space=pl.ANY) for _ in before),
            ],
            out_specs=[pl.BlockSpec((BLK, o.shape[1]), there) for o in outs],
        ),
        input_output_aliases={7 + n: n for n in range(len(before))},
        compiler_params=params(VMEM_MIB),
        cost_estimate=cost(2 * rows * model * cols * 3, 10e6),
        name="project_qkv",
    )(base, x, first, gain, w, cosine, sine, *before)


def attend_fwd_kernel(len_ref, q_ref, k_ref, v_ref, *refs):
    o_ref, lse_ref, ka_ref, va_ref, mask_ref = refs[-5:]
    block = pl.program_id(0)
    slot_len = k_ref.shape[0]

    @pl.when(block == 0)
    def _():
        row = lax.broadcasted_iota(jnp.int32, (slot_len, LANES), 0)
        lane = lane_of(slot_len)
        bias = jnp.where(row < len_ref[0], 0.0, NEG_BIG).astype(BF16)
        for head in (0, 1):
            mine = (lane // HEAD_DIM) == head
            spot = HEAD_DIM * (1 - head)
            ka_ref[head] = jnp.where(mine, k_ref[...], jnp.where(lane == spot, bias, jnp.zeros_like(bias)))
            va_ref[head] = jnp.where(mine, v_ref[...], jnp.ones_like(bias))
        query = lax.broadcasted_iota(jnp.int32, (BLK, BLK), 0)
        key = lax.broadcasted_iota(jnp.int32, (BLK, BLK), 1)
        mask_ref[...] = jnp.where(key <= query, 0.0, NEG_BIG)

    lane = lane_of(BLK)
    low = lane < HEAD_DIM
    for count in range(slot_len // BLK):

        @pl.when(block == count)
        def _():
            q = q_ref[...]
            outs, peaks = [], []
            for head in (0, 1):
                spot = HEAD_DIM * (1 - head)
                one = jnp.where(lane == spot, 1.0, 0.0).astype(BF16)
                scored = jnp.where((lane // HEAD_DIM) == head, q, one)
                scores = []
                for j in range(count + 1):
                    s = nt(scored, ka_ref[head, pl.ds(j * BLK, BLK), :])
                    scores.append(s + mask_ref[...] if j == count else s)
                top = scores[0]
                for s in scores[1:]:
                    top = jnp.maximum(top, s)
                peak = jnp.max(top, axis=1, keepdims=True)
                acc = None
                for j, s in enumerate(scores):
                    p = jnp.exp(s - peak).astype(BF16)
                    term = nn(p, va_ref[head, pl.ds(j * BLK, BLK), :])
                    acc = term if acc is None else acc + term
                outs.append(acc)
                peaks.append(peak)
            total = pltpu.roll(jnp.where(low, outs[1], outs[0]), HEAD_DIM, 1)
            o_ref[...] = (jnp.where(low, outs[0], outs[1]) / total).astype(BF16)
            lse_ref[...] = jnp.where(low, peaks[0], peaks[1]) + jnp.log(total)


def attend_pair(pair, length, q, k, v, before):
    slot_len, cols = q.shape
    blocks = slot_len // BLK
    row = pl.BlockSpec((BLK, LANES), lambda i, n: (i, pair))
    full = pl.BlockSpec((slot_len, LANES), lambda i, n: (0, pair))
    before = () if before is None else tuple(before)
    return pl.pallas_call(
        attend_fwd_kernel,
        out_shape=(
            jax.ShapeDtypeStruct((slot_len, cols), BF16),
            jax.ShapeDtypeStruct((slot_len, cols), F32),
        ),
        grid_spec=pltpu.PrefetchScalarGridSpec(
            num_scalar_prefetch=1,
            grid=(blocks,),
            in_specs=[row, full, full] + [pl.BlockSpec(memory_space=pl.ANY) for _ in before],
            out_specs=[row, row],
            scratch_shapes=[
                pltpu.VMEM((2, slot_len, LANES), BF16),
                pltpu.VMEM((2, slot_len, LANES), BF16),
                pltpu.VMEM((BLK, BLK), F32),
            ],
        ),
        input_output_aliases={4 + n: n for n in range(len(before))},
        compiler_params=params(VMEM_MIB),
        cost_estimate=cost(2 * 2 * slot_len * slot_len * 256, 3e6),
        name="attend_pair",
    )(length, q, k, v, *before)


def split3(x):
    high = x.astype(BF16)
    rest = x - high.astype(F32)
    mid = rest.astype(BF16)
    return high, mid, (rest - mid.astype(F32)).astype(BF16)


def attend_back_kernel(len_ref, q_ref, k_ref, v_ref, do_ref, o_ref, lse_ref, cos_ref, sin_ref, *refs):
    fv_ref, grad_ref, send_ref, qa, ka, va, da, qz, kz, dz, mask_ref, dq_acc = refs[-12:]
    slot_len = k_ref.shape[0]
    blocks = slot_len // BLK
    lane = lane_of(slot_len)
    low = lane < HEAD_DIM
    row = lax.broadcasted_iota(jnp.int32, (slot_len, LANES), 0)
    bias = jnp.where(row < len_ref[0], 0.0, NEG_BIG).astype(BF16)
    zero = jnp.zeros_like(bias)
    minus = jnp.full_like(bias, -1.0)
    prod = do_ref[...].astype(F32) * o_ref[...].astype(F32)
    center_low = jnp.sum(jnp.where(low, prod, 0.0), axis=1, keepdims=True)
    center_high = jnp.sum(jnp.where(low, 0.0, prod), axis=1, keepdims=True)
    centers = split3(jnp.where(low, center_high, center_low))
    totals = split3(pltpu.roll(lse_ref[...], HEAD_DIM, 1))

    def place(head, items):
        out = zero
        for n, item in enumerate(items):
            out = jnp.where(lane == HEAD_DIM * (1 - head) + n, item, out)
        return out

    for head in (0, 1):
        mine = (lane // HEAD_DIM) == head
        qa[head] = jnp.where(mine, q_ref[...], place(head, [-minus, *totals]))
        ka[head] = jnp.where(mine, k_ref[...], place(head, [bias, minus, minus, minus]))
        da[head] = jnp.where(mine, do_ref[...], place(head, centers))
        va[head] = jnp.where(mine, v_ref[...], place(head, [minus, minus, minus]))
        qz[head] = jnp.where(mine, q_ref[...], zero)
        kz[head] = jnp.where(mine, k_ref[...], zero)
        dz[head] = jnp.where(mine, do_ref[...], zero)
    key = lax.broadcasted_iota(jnp.int32, (BLK, BLK), 0)
    query = lax.broadcasted_iota(jnp.int32, (BLK, BLK), 1)
    mask_ref[...] = jnp.where(key <= query, 0.0, NEG_BIG)
    dq_acc[...] = jnp.zeros_like(dq_acc)

    def unturn(grad, rows):
        return grad * cos_ref[rows, :] - partner_lanes(grad) * sin_ref[rows, :]

    for j in range(blocks):
        keys = pl.ds(j * BLK, BLK)
        dk = dv = None
        for i in range(j, blocks):
            queries = pl.ds(i * BLK, BLK)
            dq = None
            for head in (0, 1):
                s = nt(ka[head, keys, :], qa[head, queries, :])
                if i == j:
                    s = s + mask_ref[...]
                p = jnp.exp(s)
                ds = (p * nt(va[head, keys, :], da[head, queries, :])).astype(BF16)
                term = nn(p.astype(BF16), dz[head, queries, :])
                dv = term if dv is None else dv + term
                term = nn(ds, qz[head, queries, :])
                dk = term if dk is None else dk + term
                term = tn(ds, kz[head, keys, :])
                dq = term if dq is None else dq + term
            dq_acc[queries, :] += dq
        half_dv = HALF * dv
        fv_ref[keys, :] = half_dv
        grad_ref[keys, 2 * LANES : 3 * LANES] = half_dv.astype(BF16)
        grad_ref[keys, LANES : 2 * LANES] = unturn(dk, keys).astype(BF16)
    for i in range(blocks):
        queries = pl.ds(i * BLK, BLK)
        grad_ref[queries, 0:LANES] = unturn(dq_acc[queries, :] * 0.125, queries).astype(BF16)
    send_ref[...] = grad_ref[pl.ds(pl.multiple_of(len_ref[1] * BLK, BLK), send_ref.shape[0]), :]


def attend_back_pair(pair, length, q, k, v, do, o, lse, cosine, sine, before):
    slot_len, cols = q.shape
    full = pl.BlockSpec((slot_len, LANES), lambda i, n: (0, pair))
    own = pl.BlockSpec((slot_len, LANES), lambda i, n: (0, 0))
    before = () if before is None else tuple(before)
    both = pltpu.VMEM((2, slot_len, LANES), BF16)
    wide = PARTS * LANES
    return pl.pallas_call(
        attend_back_kernel,
        out_shape=(
            jax.ShapeDtypeStruct((slot_len, cols), F32),
            jax.ShapeDtypeStruct((slot_len, PARTS * cols), BF16),
            jax.ShapeDtypeStruct((slot_len // 2, wide), BF16),
        ),
        grid_spec=pltpu.PrefetchScalarGridSpec(
            num_scalar_prefetch=1,
            grid=(1,),
            in_specs=[full, full, full, own, full, full, own, own]
            + [pl.BlockSpec(memory_space=pl.ANY) for _ in before],
            out_specs=[
                full,
                pl.BlockSpec((slot_len, wide), lambda i, n: (0, pair)),
                pl.BlockSpec((slot_len // 2, wide), lambda i, n: (0, 0)),
            ],
            scratch_shapes=[both] * 7
            + [pltpu.VMEM((BLK, BLK), F32), pltpu.VMEM((slot_len, LANES), F32)],
        ),
        input_output_aliases={9 + n: n for n in range(len(before))},
        compiler_params=params(VMEM_MIB),
        cost_estimate=cost(5 * 2 * slot_len * slot_len * 256, 6e6),
        name="attend_back_pair",
    )(length, q, k, v, do, o, lse, cosine, sine, *before)


def resid_kernel(base_ref, x_ref, gain_ref, w_own_ref, w_far_ref, own_ref, *refs):
    own = own_ref[...]
    far = jnp.concatenate([r[...] for r in refs[:-3]], axis=1)
    h_ref, n_ref, o_ref = refs[-3:]
    h = x_ref[...].astype(F32) + (nn(own, w_own_ref[...]) + nn(far, w_far_ref[...]))
    inverse = lax.rsqrt(jnp.mean(h * h, axis=-1, keepdims=True) + EPS)
    h_ref[...] = h
    n_ref[...] = ((h * inverse) * gain_ref[...]).astype(BF16)
    cols = own.shape[1]
    o_ref[:, :cols] = far
    o_ref[:, cols:] = own


def resid_rows(base, x, gain, w_own, w_far, own, far):
    rows, model = x.shape
    cols = w_own.shape[0]
    wide = pl.BlockSpec((BLK, model), lambda i, b: (i, 0))
    fixed = pl.BlockSpec((cols, model), lambda i, b: (0, 0))
    return pl.pallas_call(
        resid_kernel,
        out_shape=(
            jax.ShapeDtypeStruct((rows, model), F32),
            jax.ShapeDtypeStruct((rows, model), BF16),
            jax.ShapeDtypeStruct((rows, 2 * cols), BF16),
        ),
        grid_spec=pltpu.PrefetchScalarGridSpec(
            num_scalar_prefetch=1,
            grid=(rows // BLK,),
            in_specs=[
                wide,
                pl.BlockSpec((1, model), lambda i, b: (0, 0)),
                fixed,
                fixed,
                pl.BlockSpec((BLK, cols), lambda i, b: (b[0] + i, 0)),
                *(pl.BlockSpec((BLK, f.shape[1]), lambda i, b: (i, 0)) for f in far),
            ],
            out_specs=[wide, wide, pl.BlockSpec((BLK, 2 * cols), lambda i, b: (i, 0))],
        ),
        compiler_params=params(VMEM_MIB),
        cost_estimate=cost(2 * rows * model * cols * 2, 14e6),
        name="resid_rows",
    )(base, x, gain, w_own, w_far, own, *far)


def interleave_kernel(w_ref, out_ref):
    for run in range(w_ref.shape[2] // LANES):
        for side in (0, 1):
            spot = (2 * run + side) * LANES
            out_ref[:, spot : spot + LANES] = w_ref[:, side, run * LANES : (run + 1) * LANES].astype(BF16)


def interleave(w):
    model, sides, hidden = w.shape
    return pl.pallas_call(
        interleave_kernel,
        out_shape=jax.ShapeDtypeStruct((model, sides * hidden), BF16),
        grid=(model // 128,),
        in_specs=[pl.BlockSpec((128, sides, hidden), lambda i: (i, 0, 0))],
        out_specs=pl.BlockSpec((128, sides * hidden), lambda i: (i, 0)),
        compiler_params=params(VMEM_MIB),
        cost_estimate=cost(0, 6 * w.size),
        name="interleave",
    )(w)


def halve_rows(grad, core, x, keep, send):
    rows = grad.shape[0] // 16
    block = lambda z, i, c: grad[(z * 4 + i * 2 + c) * rows : (z * 4 + i * 2 + c + 1) * rows]
    for i in (0, 1):
        for z in range(4):
            spot = pl.ds((i * 4 + z) * rows, rows)
            same = [jnp.where(x == 0, block(z, i, c), block(z, 1 - i, c)) for c in (0, 1)]
            keep[spot, :] = jnp.where(core == 0, same[0], same[1])
            send[spot, :] = jnp.where(core == 0, same[1], same[0])


def runs(block, count, of, which):
    return jnp.concatenate(
        [block[:, (of * i + which) * LANES : (of * i + which + 1) * LANES] for i in range(count)], axis=1
    )


def swiglu_kernel(place_ref, n_ref, dy_ref, wgu_ref, wd_ref, y_ref, dn_ref, keep_ref, send_ref, y_acc, dn_acc):
    step = pl.program_id(0)
    last = pl.num_programs(0) - 1
    core, x = place_ref[0], place_ref[1]

    def work(count, first):
        n = n_ref[...]
        dy = dy_ref[...]
        wgu, wd = wgu_ref[:, : 2 * count * LANES], wd_ref[: count * LANES, :]
        both = nn(n, wgu)
        gate, up = runs(both, count, 2, 0), runs(both, count, 2, 1)
        sig = jax.nn.sigmoid(gate)
        silu = gate * sig
        hid = (silu * up).astype(BF16)
        dhid = nt(dy, wd)
        dgate = (dhid * up * sig * (1.0 + gate * (1.0 - sig))).astype(BF16)
        dup = (dhid * silu).astype(BF16)
        dgu = jnp.concatenate(
            [d[:, i * LANES : (i + 1) * LANES] for i in range(count) for d in (dgate, dup)], axis=1
        )
        y = nn(hid, wd)
        dn = nt(dgu, wgu)
        if first:
            y_acc[...] = y
            dn_acc[...] = dn
        else:
            y_acc[...] += y
            dn_acc[...] += dn
        grad_gu = tn(n, dgu).astype(BF16)
        grad_d = tn(dy, hid).astype(BF16)
        for i in range(count):
            for part, grad in enumerate((grad_gu[:, 2 * i * LANES : (2 * i + 2) * LANES],
                                         grad_d[:, i * LANES : (i + 1) * LANES])):
                spot = slice((3 * i + 2 * part) * LANES, (3 * i + 2 * part) * LANES + grad.shape[1])
                halve_rows(grad, core, x, keep_ref.at[:, spot], send_ref.at[:, spot])

    @pl.when(step == 0)
    def _():
        work(2, True)

    @pl.when((step > 0) & (step < last))
    def _():
        work(2, False)

    @pl.when(step == last)
    def _():
        work(1, False)
        y_ref[...] = y_acc[...].astype(BF16)
        dn_ref[...] = dn_acc[...].astype(BF16)


def swiglu_half(place, n, dy, wgu, wd, width):
    rows, model = n.shape
    hidden = wd.shape[0]
    tile = 256
    steps = -(-hidden // tile)
    held = pl.BlockSpec((rows, model), lambda t, p: (0, 0))
    grads = pl.BlockSpec((model // 2, 3 * tile), lambda t, p: (0, t))
    return pl.pallas_call(
        swiglu_kernel,
        out_shape=(
            *(jax.ShapeDtypeStruct((rows, model), BF16) for _ in range(2)),
            *(jax.ShapeDtypeStruct((model // 2, width), BF16) for _ in range(2)),
        ),
        grid_spec=pltpu.PrefetchScalarGridSpec(
            num_scalar_prefetch=1,
            grid=(steps,),
            in_specs=[
                held,
                held,
                pl.BlockSpec((model, 2 * tile), lambda t, p: (0, t)),
                pl.BlockSpec((tile, model), lambda t, p: (t, 0)),
            ],
            out_specs=[held, held, grads, grads],
            scratch_shapes=[pltpu.VMEM((rows, model), F32)] * 2,
        ),
        compiler_params=params(VMEM_MIB),
        cost_estimate=cost(9 * 2 * rows * model * hidden, 36e6, rows * hidden),
        name="swiglu_half",
    )(place, n, dy, wgu, wd)


def grad_out_kernel(place_ref, dhb_ref, o_ref, keep_in, send_in, keep_ref, send_ref):
    del keep_in, send_in
    grad = tn(dhb_ref[...], o_ref[...]).astype(BF16)
    halve_rows(grad, place_ref[0], place_ref[1], keep_ref, send_ref)


def grad_out_into(place, dhb, o_cat, keep, send, start):
    rows, model = dhb.shape
    tile = 384
    out = pl.BlockSpec((model // 2, tile), lambda t, p: (0, start // tile + t))
    return pl.pallas_call(
        grad_out_kernel,
        out_shape=[jax.ShapeDtypeStruct(a.shape, a.dtype) for a in (keep, send)],
        grid_spec=pltpu.PrefetchScalarGridSpec(
            num_scalar_prefetch=1,
            grid=(-(-o_cat.shape[1] // tile),),
            in_specs=[
                pl.BlockSpec((rows, model), lambda t, p: (0, 0)),
                pl.BlockSpec((rows, tile), lambda t, p: (0, t)),
                pl.BlockSpec(memory_space=pl.ANY),
                pl.BlockSpec(memory_space=pl.ANY),
            ],
            out_specs=[out, out],
        ),
        input_output_aliases={3: 0, 4: 1},
        compiler_params=params(VMEM_MIB),
        cost_estimate=cost(2 * rows * model * o_cat.shape[1], 7e6),
        name="grad_out",
    )(place, dhb, o_cat, keep, send)


def grad_qkv_kernel(place_ref, n_ref, dqkv_ref, w_ref, keep_ref, send_ref, t_ref):
    grad = tn(n_ref[...], dqkv_ref[...])
    term = None
    for part in range(PARTS):
        piece = grad[:, part * LANES : (part + 1) * LANES] * w_ref[part].astype(F32)
        term = piece if term is None else term + piece

    @pl.when(pl.program_id(0) == 0)
    def _():
        t_ref[...] = term

    @pl.when(pl.program_id(0) > 0)
    def _():
        t_ref[...] += term

    halve_rows(grad.astype(BF16), place_ref[0], place_ref[1], keep_ref, send_ref)


def grad_qkv_of(place, norm, dqkv, w):
    slot_len, model = norm.shape
    tile = PARTS * LANES
    out = pl.BlockSpec((model // 2, tile), lambda t, p: (0, t))
    return pl.pallas_call(
        grad_qkv_kernel,
        out_shape=(
            *(jax.ShapeDtypeStruct((model // 2, dqkv.shape[1]), BF16) for _ in range(2)),
            jax.ShapeDtypeStruct((model, LANES), F32),
        ),
        grid_spec=pltpu.PrefetchScalarGridSpec(
            num_scalar_prefetch=1,
            grid=(dqkv.shape[1] // tile,),
            in_specs=[
                pl.BlockSpec((slot_len, model), lambda t, p: (0, 0)),
                pl.BlockSpec((slot_len, tile), lambda t, p: (0, t)),
                pl.BlockSpec((PARTS, model, LANES), lambda t, p: (0, 0, t)),
            ],
            out_specs=[out, out, pl.BlockSpec((model, LANES), lambda t, p: (0, 0))],
        ),
        compiler_params=params(VMEM_MIB),
        cost_estimate=cost(2 * slot_len * model * dqkv.shape[1], 14e6),
        name="grad_qkv",
    )(place, norm, dqkv, w)


def after_kernel(h_ref, y1_ref, y2_ref, d1_ref, d2_ref, dy_ref, gain_ref, w_own_ref, w_far_ref,
                 out_ref, dh_ref, dhb_ref, own_ref, far_ref, t_ref):
    h = h_ref[...]
    out_ref[...] = (h + (y1_ref[...].astype(F32) + y2_ref[...].astype(F32))).astype(BF16)
    inverse = lax.rsqrt(jnp.mean(h * h, axis=-1, keepdims=True) + EPS)
    unit = h * inverse
    dn = d1_ref[...].astype(F32) + d2_ref[...].astype(F32)
    e = dn * gain_ref[...]
    dh = dy_ref[...].astype(F32) + inverse * (e - unit * jnp.mean(e * unit, axis=-1, keepdims=True))
    dh_ref[...] = dh
    dhb = dh.astype(BF16)
    dhb_ref[...] = dhb
    own_ref[...] = nt(dhb, w_own_ref[...]).astype(BF16)
    far_ref[...] = nt(dhb, w_far_ref[...]).astype(BF16)

    @pl.when(pl.program_id(0) == 0)
    def _():
        t_ref[...] = jnp.zeros_like(t_ref)

    t_ref[...] += jnp.sum(dn * unit, axis=0, keepdims=True)


def after_rows(h, y1, y2, d1, d2, dy, gain, w_own, w_far):
    rows, model = h.shape
    cols = w_own.shape[0]
    wide = pl.BlockSpec((BLK, model), lambda i: (i, 0))
    fixed = pl.BlockSpec((cols, model), lambda i: (0, 0))
    slim = pl.BlockSpec((BLK, cols), lambda i: (i, 0))
    one = pl.BlockSpec((1, model), lambda i: (0, 0))
    return pl.pallas_call(
        after_kernel,
        out_shape=(
            jax.ShapeDtypeStruct((rows, model), BF16),
            jax.ShapeDtypeStruct((rows, model), F32),
            jax.ShapeDtypeStruct((rows, model), BF16),
            jax.ShapeDtypeStruct((rows, cols), BF16),
            jax.ShapeDtypeStruct((rows, cols), BF16),
            jax.ShapeDtypeStruct((1, model), F32),
        ),
        grid=(rows // BLK,),
        in_specs=[wide] * 6 + [one, fixed, fixed],
        out_specs=[wide, wide, wide, slim, slim, one],
        compiler_params=params(VMEM_MIB),
        cost_estimate=cost(2 * rows * model * cols * 2, 36e6),
        name="after_rows",
    )(h, y1, y2, d1, d2, dy, gain, w_own, w_far)


def input_kernel(base_ref, x_ref, dh_ref, gain_ref, w_own_ref, w_far_ref, *refs):
    out_ref = refs[-1]
    dn = None
    for weights, grads in ((w_own_ref, refs[:1]), (w_far_ref, refs[1:-1])):
        flat = jnp.concatenate([g[...] for g in grads], axis=1)
        for part in range(PARTS):
            term = nt(runs(flat, flat.shape[1] // (PARTS * LANES), PARTS, part), weights[part])
            dn = term if dn is None else dn + term
    x = x_ref[...].astype(F32)
    inverse = lax.rsqrt(jnp.mean(x * x, axis=-1, keepdims=True) + EPS)
    unit = x * inverse
    e = dn * gain_ref[...]
    out_ref[...] = dh_ref[...] + inverse * (e - unit * jnp.mean(e * unit, axis=-1, keepdims=True))


def input_rows(base, x, dh, gain, w_own, w_far, own, far):
    rows, model = x.shape
    cols = w_own.shape[2]
    wide = pl.BlockSpec((BLK, model), lambda i, b: (i, 0))
    fixed = pl.BlockSpec((PARTS, model, cols), lambda i, b: (0, 0, 0))
    return pl.pallas_call(
        input_kernel,
        out_shape=jax.ShapeDtypeStruct((rows, model), F32),
        grid_spec=pltpu.PrefetchScalarGridSpec(
            num_scalar_prefetch=1,
            grid=(rows // BLK,),
            in_specs=[wide, wide, pl.BlockSpec((1, model), lambda i, b: (0, 0)), fixed, fixed]
            + [pl.BlockSpec((BLK, own.shape[1]), lambda i, b: (b[0] + i, 0))]
            + [pl.BlockSpec((BLK, f.shape[1]), lambda i, b: (i, 0)) for f in far],
            out_specs=wide,
        ),
        compiler_params=params(VMEM_MIB),
        cost_estimate=cost(2 * rows * model * cols * 6, 20e6),
        name="input_rows",
    )(base, x, dh, gain, w_own, w_far, own, *far)


def step_of(sum_grad, weight, moment, average, rate, root_count):
    return nesterov(sum_grad / root_count, weight, moment, average, rate)


def own_columns(place, wide):
    turned = wide.T
    half = turned.shape[0] // 2
    return jnp.where(place == 0, turned[:half], turned[half:])


def step_mlp_kernel(root_count, place_ref, sum_ref, got_ref, wgu_ref, mgu_ref, agu_ref, wd_ref, md_ref, ad_ref, *outs):
    total = sum_ref[...] + got_ref[...].astype(F32)
    count = total.shape[1] // (3 * LANES)
    for side in (0, 1):
        grads = step_of(runs(total, count, 3, side), wgu_ref[:, side, :], mgu_ref[:, side, :],
                        agu_ref[:, side, :], RATE_GATEUP, root_count)
        for out, value in zip(outs[:4], grads):
            out[:, side, :] = value
    weight = own_columns(place_ref[1], wd_ref[...])
    grads = step_of(runs(total, count, 3, 2), weight, md_ref[...], ad_ref[...], RATE_DOWN, root_count)
    for out, value in zip(outs[4:], grads):
        out[...] = value


def step_mlp(dp_index, root_count, total, got, w_gateup, m_gu, a_gu, w_down, m_d, a_d):
    place = jnp.stack([dp_index, dp_index % 2, dp_index // 2]).astype(jnp.int32)
    share, sides, hidden = m_gu.shape
    cols = total.shape[1]
    gu = pl.BlockSpec((share, sides, hidden), lambda i, p: (0, 0, 0))
    d = pl.BlockSpec((share, hidden), lambda i, p: (0, 0))
    return pl.pallas_call(
        functools.partial(step_mlp_kernel, root_count),
        out_shape=(
            *(jax.ShapeDtypeStruct(m_gu.shape, F32) for _ in range(4)),
            *(jax.ShapeDtypeStruct((share, hidden), F32) for _ in range(4)),
        ),
        grid_spec=pltpu.PrefetchScalarGridSpec(
            num_scalar_prefetch=1,
            grid=(1,),
            in_specs=[
                pl.BlockSpec((share, cols), lambda i, p: (0, 0)),
                pl.BlockSpec((share, cols), lambda i, p: (0, 0)),
                pl.BlockSpec((share, sides, hidden), lambda i, p: (p[0], 0, 0)),
                gu,
                gu,
                pl.BlockSpec((hidden, LANES), lambda i, p: (0, p[2])),
                d,
                d,
            ],
            out_specs=[gu] * 4 + [d] * 4,
        ),
        compiler_params=params(VMEM_MIB),
        cost_estimate=cost(0, 14e6),
        name="step_mlp",
    )(place, total, got, w_gateup, m_gu, a_gu, w_down, m_d, a_d)


def step_attention_kernel(root_count, place_ref, sum_ref, own_ref, got_ref, wq_ref, mq_ref, aq_ref, wo_ref, mo_ref, ao_ref, *outs):
    total = sum_ref[...]
    count = total.shape[1] // (PARTS * LANES)
    for part in range(PARTS):
        grads = step_of(runs(total, count, PARTS, part), wq_ref[part], mq_ref[part], aq_ref[part],
                        RATE_QKV, root_count)
        for out, value in zip(outs[:4], grads):
            out[part] = value
    weight = own_columns(place_ref[1], wo_ref[...])
    grads = step_of(own_ref[...] + got_ref[...].astype(F32), weight, mo_ref[...], ao_ref[...],
                    RATE_OUT, root_count)
    for out, value in zip(outs[4:], grads):
        out[...] = value


def step_attention(dp_index, root_count, total, own, got, w_qkv, m_q, a_q, w_out, m_o, a_o):
    place = jnp.stack([dp_index, dp_index % 2, dp_index // 2]).astype(jnp.int32)
    parts, share, cols = m_q.shape
    q = pl.BlockSpec((parts, share, cols), lambda i, p: (0, 0, 0))
    o = pl.BlockSpec((share, cols), lambda i, p: (0, 0))
    return pl.pallas_call(
        functools.partial(step_attention_kernel, root_count),
        out_shape=(
            *(jax.ShapeDtypeStruct(m_q.shape, F32) for _ in range(4)),
            *(jax.ShapeDtypeStruct((share, cols), F32) for _ in range(4)),
        ),
        grid_spec=pltpu.PrefetchScalarGridSpec(
            num_scalar_prefetch=1,
            grid=(1,),
            in_specs=[
                pl.BlockSpec((share, parts * cols), lambda i, p: (0, 0)),
                o,
                o,
                pl.BlockSpec((parts, share, cols), lambda i, p: (0, p[0], 0)),
                q,
                q,
                pl.BlockSpec((cols, LANES), lambda i, p: (0, p[2])),
                o,
                o,
            ],
            out_specs=[q] * 4 + [o] * 4,
        ),
        compiler_params=params(VMEM_MIB),
        cost_estimate=cost(0, 6e6),
        name="step_attention",
    )(place, total, own, got, w_qkv, m_q, a_q, w_out, m_o, a_o)


def dp_pairs(move):
    return tuple((i, move(i)) for i in range(16))


CORE = dp_pairs(lambda i: i ^ 1)
CROSS = dp_pairs(lambda i: i ^ 2)
NEAR = tuple(
    tuple((i, i ^ flip) for i in range(32)) for flip in (1, 2, 3)
)
ALONG = tuple(dp_pairs(lambda i, step=step: (i + 4 * step) % 16) for step in (1, 2, 3))


def move(x, pairs):
    return lax.ppermute(x, "dp", pairs)


def add(left, right):
    return left.astype(F32) + right.astype(F32)


def after_core(keep, got):
    half = keep.shape[0] // 2
    here = add(keep[:half], got[:half]).astype(BF16)
    away = add(keep[half:], got[half:]).astype(BF16)
    return here, away


def after_cross(here, got, z):
    total = add(here, got)
    rows = here.shape[0] // 4
    block = lambda step: lax.dynamic_slice_in_dim(total, lax.rem(z + step, 4) * rows, rows, 0)
    return block(0), tuple(block(step).astype(BF16) for step in (1, 2, 3))


def after_along(mine, got):
    for piece in got:
        mine = mine + piece.astype(F32)
    return mine


def tie(values, *others):
    return lax.optimization_barrier((values, others))[0]


def shards_pair(
    tokens,
    first_values,
    lengths,
    cotangent,
    w_qkv,
    w_out,
    w_gateup,
    w_down,
    gains,
    moment_qkv,
    moment_out,
    moment_gateup,
    moment_down,
    moment_gains,
    average_qkv,
    average_out,
    average_gateup,
    average_down,
    average_gains,
):
    rows, model = tokens.shape
    mp_index = lax.axis_index("mp")
    dp_index = lax.axis_index("dp")
    dp_count = lax.axis_size("dp")
    z, core = dp_index // 4, dp_index % 2
    place = jnp.stack([core, (dp_index // 2) % 2]).astype(jnp.int32)
    slot_len = 2 * rows
    head_cols = w_qkv.shape[2]
    hidden = w_gateup.shape[2]
    pairs = head_cols // LANES
    root_count = math.sqrt(slot_len * dp_count)
    row_start = mp_index * rows
    far_start = (1 - mp_index) * rows
    gain_one, gain_two = gains[0:1], gains[1:2]

    def swap(x):
        return lax.ppermute(x, "mp", SWAP)

    def chunk(x):
        part = x.shape[0] // dp_count
        return lax.dynamic_slice_in_dim(x, dp_index * part, part, 0)

    def gather(x):
        return lax.all_gather(x, "dp", axis=0, tiled=True)

    out_bf = w_out.astype(BF16)
    out_chunk = swap(chunk(w_out).astype(BF16))
    far_tokens = swap(tie(tokens, out_chunk))
    out_far = gather(out_chunk)
    qkv_bf = w_qkv.transpose(1, 0, 2).astype(BF16)
    gateup_bf = interleave(w_gateup)
    down_bf = w_down.astype(BF16)
    cosine, sine = pair_tables(slot_len)
    block_of = lambda start: (start // BLK).astype(jnp.int32)
    base, far_base = block_of(row_start).reshape(1), block_of(far_start).reshape(1)
    own_part = project_qkv(base, tokens, first_values, gain_one, qkv_bf, cosine, sine, None)
    place_row = row_start + jnp.arange(rows, dtype=jnp.int32)
    dy = jnp.where((place_row < lengths[0])[:, None], cotangent, jnp.zeros_like(cotangent))
    far_tokens, own_part, gateup_bf, down_bf, dy, out_far = lax.optimization_barrier(
        (far_tokens, own_part, gateup_bf, down_bf, dy, out_far)
    )
    gateup_chunk = swap(chunk(gateup_bf))
    down_chunk = swap(tie(chunk(down_bf), gateup_chunk))
    qkv_chunk = swap(tie(chunk(qkv_bf.reshape(PARTS * model, head_cols)), down_chunk))

    norm_one, q, k, v = project_qkv(
        far_base, far_tokens, first_values, gain_one, qkv_bf, cosine, sine, own_part
    )
    q, gateup_chunk, down_chunk, qkv_chunk = lax.optimization_barrier(
        (q, gateup_chunk, down_chunk, qkv_chunk)
    )
    gateup_far = gather(gateup_chunk)
    down_far = gather(tie(down_chunk, gateup_far))
    qkv_far = gather(tie(qkv_chunk, down_far)).reshape(PARTS, model, head_cols)

    mixed = None
    o_far = []
    for pair in range(pairs):
        lanes = slice(pair * LANES, (pair + 1) * LANES)
        mixed = attend_pair(pair, lengths, q, k, v, mixed)
        if pair == pairs - 2:
            piece = lax.dynamic_slice_in_dim(mixed[0][:, : lanes.stop], far_start, rows, 0)
            piece, mixed = lax.optimization_barrier((piece, mixed))
            o_far.append(swap(piece))
        if pair == pairs - 1:
            o_far.append(swap(lax.dynamic_slice_in_dim(mixed[0][:, lanes], far_start, rows, 0)))
    o_all, lse_all = mixed
    h, norm_two, o_cat = resid_rows(base, tokens, gain_two, out_bf, out_far, o_all, o_far)

    runs_width = 3 * hidden
    norm_two, gateup_far = lax.optimization_barrier((norm_two, gateup_far))
    y_own, dn_own, keep_own, send_own = swiglu_half(place, norm_two, dy, gateup_bf, down_bf, runs_width)
    got_own = move(send_own, CORE)
    far_width = runs_width + 3 * 384
    (norm_two, gateup_far, down_far) = tie((norm_two, gateup_far, down_far), y_own)
    y_far, dn_far, keep_far, send_far = swiglu_half(place, norm_two, dy, gateup_far, down_far, far_width)
    here_own, away_own = after_core(keep_own, tie(got_own, y_far))
    got_own = move(away_own, CROSS)
    y_far = tie(y_far, away_own)
    output, dh, dhb, do_own, do_far, gain_two_part = after_rows(
        h, y_own, y_far, dn_own, dn_far, dy, gain_two, out_bf, out_far
    )
    theirs = [swap(do_far[:, :LANES]), swap(do_far[:, LANES:])]
    keep_far, send_far = grad_out_into(place, dhb, o_cat, keep_far, send_far, runs_width)
    got_far = move(send_far, CORE)

    theirs, qkv_far = lax.optimization_barrier((theirs, qkv_far))
    back = None
    dqkv_far = []
    far_place = jnp.concatenate([lengths, far_base])
    for pair in range(pairs):
        lanes = slice(pair * LANES, (pair + 1) * LANES)
        mine = do_own[:, lanes]
        other = theirs[0] if pair == 0 else theirs[1][:, (pair - 1) * LANES : pair * LANES]
        if pair == 1:
            here_far, away_far = after_core(keep_far, tie(got_far, back))
            got_far = move(away_far, CROSS)
            other = tie(other, away_far)
        if pair == 2:
            mine_own, blocks_own = after_cross(here_own, tie(got_own, back), z)
            got_own = tuple(move(b, p) for b, p in zip(blocks_own, ALONG))
            other, dqkv_far[0] = lax.optimization_barrier((tie(other, blocks_own, mine_own), dqkv_far[0]))
        if pair == 3:
            mine_far, blocks_far = after_cross(here_far, tie(got_far, back), z)
            got_far = tuple(move(b, p) for b, p in zip(blocks_far, ALONG))
            other, dqkv_far[1] = lax.optimization_barrier((tie(other, blocks_far, mine_far), dqkv_far[1]))
        low = jnp.where(mp_index == 0, mine, other)
        high = jnp.where(mp_index == 0, other, mine)
        do = jnp.concatenate([low, high], axis=0)
        first_grad, dqkv, away = attend_back_pair(
            pair, far_place, q, k, v, do, o_all, lse_all, cosine, sine, back
        )
        back = (first_grad, dqkv)
        dqkv_far.append(swap(away))

    dqkv, dqkv_far[2], got_own = lax.optimization_barrier((dqkv, dqkv_far[2], got_own))
    sum_own = after_along(mine_own, got_own)
    keep_qkv, send_qkv, gain_one_lanes = grad_qkv_of(place, norm_one, dqkv, qkv_bf)
    got_qkv = move(send_qkv, CORE)
    gain_one_part = jnp.sum(gain_one_lanes, axis=1) / gains[0]
    parts = jnp.stack([gain_one_part, gain_two_part[0]], axis=0)
    near = [lax.ppermute(parts, ("dp", "mp"), p) for p in NEAR]
    got_qkv, near = lax.optimization_barrier((got_qkv, near))
    here_qkv, away_qkv = after_core(keep_qkv, got_qkv)
    got_qkv = move(away_qkv, CROSS)
    parts = after_along(parts, near)
    cross = move(parts, CROSS)
    input_grad = input_rows(
        base, tokens, tie(dh, away_qkv, parts), gain_one, qkv_bf, qkv_far, dqkv, dqkv_far
    )
    got_qkv, cross, got_far = tie((got_qkv, cross, got_far), input_grad)
    mine_qkv, blocks_qkv = after_cross(here_qkv, got_qkv, z)
    got_qkv = tuple(move(b, p) for b, p in zip(blocks_qkv, ALONG))
    parts = parts + cross
    along = [move(parts, p) for p in ALONG]
    sum_far = after_along(mine_far, got_far)
    cut = runs_width + head_cols
    got_swap = swap(sum_far[:, :cut].astype(BF16))

    gateup_down = step_mlp(
        dp_index, root_count, tie(sum_own, blocks_qkv, parts), got_swap[:, :runs_width], w_gateup,
        moment_gateup, average_gateup, w_down, moment_down.T, average_down.T,
    )
    got_qkv, along = tie((got_qkv, along), gateup_down[0])
    gain_sum = after_along(parts, along)
    sum_qkv = after_along(mine_qkv, got_qkv)
    turn = lambda x: x.transpose(1, 0, 2)
    qkv_out = step_attention(
        dp_index, root_count, sum_qkv, sum_far[:, cut : cut + head_cols], got_swap[:, runs_width:],
        turn(w_qkv), turn(moment_qkv), turn(average_qkv), w_out, moment_out.T, average_out.T,
    )
    gains_set = nesterov(gain_sum / root_count, gains, moment_gains, average_gains, RATE_GAINS)
    return (
        output,
        input_grad,
        first_grad,
        *(turn(x) for x in qkv_out[:4]),
        *(x.T for x in qkv_out[4:]),
        *gateup_down[:4],
        *(x.T for x in gateup_down[4:]),
        *gains_set,
    )


def solution(mesh):
    placed = (
        P(("dp", "mp"), None),
        P("dp", "mp"),
        P("dp"),
        P(("dp", "mp"), None),
        P(None, None, "mp"),
        P("mp", None),
        P(None, None, "mp"),
        P("mp", None),
        P(),
        P("dp", None, "mp"),
        P("mp", "dp"),
        P("dp", None, "mp"),
        P("mp", "dp"),
        P(),
        P("dp", None, "mp"),
        P("mp", "dp"),
        P("dp", None, "mp"),
        P("mp", "dp"),
        P(),
    )
    return jax.shard_map(
        shards_pair if (mesh.shape["dp"], mesh.shape["mp"]) == (16, 2) else shards_any,
        mesh=mesh,
        in_specs=placed,
        out_specs=(
            P(("dp", "mp"), None),
            P(("dp", "mp"), None),
            P("dp", "mp"),
            P("dp", None, "mp"),
            P("dp", None, "mp"),
            P("dp", None, "mp"),
            P("dp", None, "mp"),
            P("mp", "dp"),
            P("mp", "dp"),
            P("mp", "dp"),
            P("mp", "dp"),
            P("dp", None, "mp"),
            P("dp", None, "mp"),
            P("dp", None, "mp"),
            P("dp", None, "mp"),
            P("mp", "dp"),
            P("mp", "dp"),
            P("mp", "dp"),
            P("mp", "dp"),
            P(),
            P(),
            P(),
            P(),
        ),
        check_vma=False,
    )
```

```python
import functools
import math

import jax
import jax.numpy as jnp
from jax import lax
from jax.experimental import pallas as pl
from jax.experimental.pallas import tpu as pltpu
from jax.sharding import PartitionSpec as P

HEAD_DIM = 64


EPS = 1e-06
NEG_BIG = -1e30
HALF = 0.5
MOMENTUM = 0.5
AVERAGE_DECAY = 0.5
RATE_QKV = 0.05
RATE_OUT = 20.0
RATE_GATEUP = 0.12
RATE_DOWN = 0.04
RATE_GAINS = 0.6


def normalize(values, gain):
    inverse = lax.rsqrt(jnp.mean(values * values, axis=-1, keepdims=True) + EPS)
    unit = values * inverse
    return (unit * gain, unit, inverse)


def norm_back(grad_norm, gain, unit, inverse):
    scaled = grad_norm * gain
    return inverse * (scaled - unit * jnp.mean(scaled * unit, axis=-1, keepdims=True))


def rope_tables(length, head_size):
    half_size = head_size // 2
    freqs = jnp.power(10000.0, -2.0 * jnp.arange(half_size, dtype=jnp.float32) / head_size)
    angles = jnp.arange(length, dtype=jnp.float32)[:, None] * freqs[None, :]
    return (jnp.cos(angles)[:, None, :], jnp.sin(angles)[:, None, :])


def rotate(values, cosine, sine):
    half_size = values.shape[-1] // 2
    first_half = values[..., :half_size]
    second_half = values[..., half_size:]
    return jnp.concatenate(
        [first_half * cosine - second_half * sine, second_half * cosine + first_half * sine],
        axis=-1,
    )


def unrotate(grads, cosine, sine):
    half_size = grads.shape[-1] // 2
    first_half = grads[..., :half_size]
    second_half = grads[..., half_size:]
    return jnp.concatenate(
        [first_half * cosine + second_half * sine, second_half * cosine - first_half * sine],
        axis=-1,
    )


def dot_last(left, right):
    return lax.dot_general(
        left, right, (((1,), (1,)), ((), ())), preferred_element_type=jnp.float32
    )


def dot_first(left, right):
    return lax.dot_general(
        left, right, (((0,), (0,)), ((), ())), preferred_element_type=jnp.float32
    )


def block_scores(query_block, keys, start, length, scale):
    block_len = query_block.shape[0]
    key_len = keys.shape[0]
    scores = (
        jnp.einsum("qhd,khd->hqk", query_block, keys, preferred_element_type=jnp.float32) * scale
    )
    query_pos = start + jnp.arange(block_len, dtype=jnp.int32)
    key_pos = jnp.arange(key_len, dtype=jnp.int32)
    allowed = (key_pos[None, :] <= query_pos[:, None]) & (key_pos[None, :] < length)
    return jnp.where(allowed[None], scores, NEG_BIG)


def attend_forward(queries, keys, values, lengths):
    slot_count, slot_len, heads_here, head_size = queries.shape
    block_len = min(512, slot_len)
    blocks = slot_len // block_len
    scale = 1.0 / math.sqrt(head_size)
    starts = jnp.arange(blocks, dtype=jnp.int32) * block_len

    def per_slot(item):
        slot_queries, slot_keys, slot_values, length = item

        def per_block(inner):
            query_block, start = inner
            scores = block_scores(query_block, slot_keys, start, length, scale)
            peak = jnp.max(scores, axis=-1, keepdims=True)
            raw_weights = jnp.exp(scores - peak)
            total = jnp.sum(raw_weights, axis=-1, keepdims=True)
            probs = raw_weights / total
            mixed = jnp.einsum(
                "hqk,khd->qhd",
                probs.astype(jnp.bfloat16),
                slot_values,
                preferred_element_type=jnp.float32,
            )
            return (mixed, (peak + jnp.log(total))[..., 0])

        mixed, log_totals = lax.map(
            per_block, (slot_queries.reshape(blocks, block_len, heads_here, head_size), starts)
        )
        return (mixed.reshape(slot_len, heads_here, head_size), log_totals)

    return lax.map(per_slot, (queries, keys, values, lengths))


def attend_backward(queries, keys, values, lengths, grad_mixed, log_totals):
    slot_count, slot_len, heads_here, head_size = queries.shape
    block_len = min(512, slot_len)
    blocks = slot_len // block_len
    scale = 1.0 / math.sqrt(head_size)
    starts = jnp.arange(blocks, dtype=jnp.int32) * block_len

    def per_slot(item):
        slot_queries, slot_keys, slot_values, length, slot_grads, slot_totals = item

        def per_block(carry, inner):
            key_grad, value_grad = carry
            query_block, grad_block, total_block, start = inner
            scores = block_scores(query_block, slot_keys, start, length, scale)
            probs = jnp.exp(scores - total_block[..., None])
            prob_grad = jnp.einsum(
                "qhd,khd->hqk", grad_block, slot_values, preferred_element_type=jnp.float32
            )
            center = jnp.sum(probs * prob_grad, axis=-1, keepdims=True)
            score_grad = (probs * (prob_grad - center)).astype(jnp.bfloat16)
            query_grad = (
                jnp.einsum(
                    "hqk,khd->qhd", score_grad, slot_keys, preferred_element_type=jnp.float32
                )
                * scale
            )
            key_grad = (
                key_grad
                + jnp.einsum(
                    "hqk,qhd->khd", score_grad, query_block, preferred_element_type=jnp.float32
                )
                * scale
            )
            value_grad = value_grad + jnp.einsum(
                "hqk,qhd->khd",
                probs.astype(jnp.bfloat16),
                grad_block,
                preferred_element_type=jnp.float32,
            )
            return ((key_grad, value_grad), query_grad)

        empty = jnp.zeros((slot_len, heads_here, head_size), jnp.float32)
        shaped_queries = slot_queries.reshape(blocks, block_len, heads_here, head_size)
        shaped_grads = slot_grads.reshape(blocks, block_len, heads_here, head_size)
        (key_grad, value_grad), query_grad = lax.scan(
            per_block, (empty, empty), (shaped_queries, shaped_grads, slot_totals, starts)
        )
        return (query_grad.reshape(slot_len, heads_here, head_size), key_grad, value_grad)

    return lax.map(per_slot, (queries, keys, values, lengths, grad_mixed, log_totals))


def row_valid(lengths, slot_len, start, count):
    index = start + jnp.arange(count, dtype=jnp.int32)
    slot_of = index // slot_len
    place = index % slot_len
    slot_ids = jnp.arange(lengths.shape[0], dtype=jnp.int32)
    limit = jnp.sum(jnp.where(slot_of[:, None] == slot_ids[None, :], lengths[None, :], 0), axis=1)
    return (place < limit).astype(jnp.float32)


def nesterov(grad, weight, moment, average, rate):
    moment_new = MOMENTUM * moment + grad
    weight_new = weight - rate * (grad + MOMENTUM * moment_new)
    average_new = AVERAGE_DECAY * average + (1.0 - AVERAGE_DECAY) * weight_new
    return (grad, moment_new, average_new, weight_new)


def shards_any(
    tokens,
    first_values,
    lengths,
    cotangent,
    w_qkv,
    w_out,
    w_gateup,
    w_down,
    gains,
    moment_qkv,
    moment_out,
    moment_gateup,
    moment_down,
    moment_gains,
    average_qkv,
    average_out,
    average_gateup,
    average_down,
    average_gains,
):
    local_rows, model = tokens.shape
    mp_count = lax.axis_size("mp")
    dp_count = lax.axis_size("dp")
    mp_index = lax.axis_index("mp")
    dp_index = lax.axis_index("dp")
    slot_count = lengths.shape[0]
    group_rows = local_rows * mp_count
    slot_len = group_rows // slot_count
    head_cols = w_qkv.shape[2]
    hidden_cols = w_gateup.shape[2]
    heads_here = head_cols // HEAD_DIM
    row_start = mp_index * local_rows
    all_tokens = group_rows * dp_count
    root_count = math.sqrt(all_tokens)
    qkv_bf = w_qkv.astype(jnp.bfloat16).reshape(model, 3 * head_cols)
    out_bf = w_out.astype(jnp.bfloat16)
    gateup_bf = w_gateup.astype(jnp.bfloat16).reshape(model, 2 * hidden_cols)
    down_bf = w_down.astype(jnp.bfloat16)
    gain_one = gains[0]
    gain_two = gains[1]
    valid_local = row_valid(lengths, slot_len, row_start, local_rows)
    x_local = tokens.astype(jnp.float32)
    x_group = lax.all_gather(tokens, "mp", axis=0, tiled=True).astype(jnp.float32)
    norm_one, unit_one, inverse_one = normalize(x_group, gain_one)
    norm_one_bf = norm_one.astype(jnp.bfloat16)
    qkv = jnp.dot(norm_one_bf, qkv_bf, preferred_element_type=jnp.float32)
    qkv = qkv.reshape(slot_count, slot_len, 3, heads_here, HEAD_DIM)
    cosine, sine = rope_tables(slot_len, HEAD_DIM)
    queries = rotate(qkv[:, :, 0], cosine, sine).astype(jnp.bfloat16)
    keys = rotate(qkv[:, :, 1], cosine, sine).astype(jnp.bfloat16)
    first_shaped = first_values.astype(jnp.float32).reshape(
        slot_count, slot_len, heads_here, HEAD_DIM
    )
    values = (HALF * qkv[:, :, 2] + HALF * first_shaped).astype(jnp.bfloat16)
    mixed, log_totals = attend_forward(queries, keys, values, lengths)
    mixed_bf = mixed.reshape(group_rows, head_cols).astype(jnp.bfloat16)
    resid_local = x_local + lax.psum_scatter(
        jnp.dot(mixed_bf, out_bf, preferred_element_type=jnp.float32),
        "mp",
        scatter_dimension=0,
        tiled=True,
    )
    norm_two_local, unit_two, inverse_two = normalize(resid_local, gain_two)
    norm_two_bf = lax.all_gather(norm_two_local.astype(jnp.bfloat16), "mp", axis=0, tiled=True)
    gateup = jnp.dot(norm_two_bf, gateup_bf, preferred_element_type=jnp.float32)
    gate_val = gateup[:, :hidden_cols]
    up_val = gateup[:, hidden_cols:]
    sigmoid_gate = jax.nn.sigmoid(gate_val)
    silu_gate = gate_val * sigmoid_gate
    hidden_bf = (silu_gate * up_val).astype(jnp.bfloat16)
    result_local = resid_local + lax.psum_scatter(
        jnp.dot(hidden_bf, down_bf, preferred_element_type=jnp.float32),
        "mp",
        scatter_dimension=0,
        tiled=True,
    )
    output = result_local.astype(jnp.bfloat16)
    grad_local = (cotangent.astype(jnp.float32) * valid_local[:, None]).astype(jnp.bfloat16)
    grad_group = lax.all_gather(grad_local, "mp", axis=0, tiled=True)
    grad_down = dot_first(hidden_bf, grad_group)
    grad_hidden = dot_last(grad_group, down_bf)
    grad_gate = grad_hidden * up_val * sigmoid_gate * (1.0 + gate_val * (1.0 - sigmoid_gate))
    grad_up = grad_hidden * silu_gate
    grad_gateup_bf = jnp.concatenate([grad_gate, grad_up], axis=1).astype(jnp.bfloat16)
    grad_gateup = dot_first(norm_two_bf, grad_gateup_bf)
    grad_norm_two = lax.psum_scatter(
        dot_last(grad_gateup_bf, gateup_bf), "mp", scatter_dimension=0, tiled=True
    )
    grad_resid_local = grad_local.astype(jnp.float32) + norm_back(
        grad_norm_two, gain_two, unit_two, inverse_two
    )
    gain_two_grad = jnp.sum(grad_norm_two * unit_two, axis=0)
    grad_resid_bf = lax.all_gather(grad_resid_local.astype(jnp.bfloat16), "mp", axis=0, tiled=True)
    grad_out = dot_first(mixed_bf, grad_resid_bf)
    grad_mixed = dot_last(grad_resid_bf, out_bf).astype(jnp.bfloat16)
    grad_mixed = grad_mixed.reshape(slot_count, slot_len, heads_here, HEAD_DIM)
    query_grad, key_grad, value_grad = attend_backward(
        queries, keys, values, lengths, grad_mixed, log_totals
    )
    first_values_grad = (HALF * value_grad).reshape(group_rows, head_cols)
    grad_qkv_bf = jnp.stack(
        [unrotate(query_grad, cosine, sine), unrotate(key_grad, cosine, sine), HALF * value_grad],
        axis=2,
    )
    grad_qkv_bf = grad_qkv_bf.reshape(group_rows, 3 * head_cols).astype(jnp.bfloat16)
    grad_qkv = dot_first(norm_one_bf, grad_qkv_bf)
    unit_local = lax.dynamic_slice_in_dim(unit_one, row_start, local_rows, 0)
    inverse_local = lax.dynamic_slice_in_dim(inverse_one, row_start, local_rows, 0)
    grad_norm_one = lax.psum_scatter(
        dot_last(grad_qkv_bf, qkv_bf).astype(jnp.bfloat16), "mp", scatter_dimension=0, tiled=True
    ).astype(jnp.float32)
    input_grad = grad_resid_local + norm_back(grad_norm_one, gain_one, unit_local, inverse_local)
    gain_one_grad = jnp.sum(grad_norm_one * unit_local, axis=0)
    sum_qkv, sum_out, sum_gateup, sum_down = (
        lax.psum_scatter(
            grad_qkv.reshape(model, 3, head_cols), "dp", scatter_dimension=0, tiled=True
        ),
        lax.psum_scatter(grad_out, "dp", scatter_dimension=1, tiled=True),
        lax.psum_scatter(
            grad_gateup.reshape(model, 2, hidden_cols), "dp", scatter_dimension=0, tiled=True
        ),
        lax.psum_scatter(grad_down, "dp", scatter_dimension=1, tiled=True),
    )
    gain_sum = lax.psum(jnp.stack([gain_one_grad, gain_two_grad], axis=0), ("dp", "mp"))
    share = model // dp_count
    own_qkv = lax.dynamic_slice_in_dim(w_qkv, dp_index * share, share, 0)
    own_out = lax.dynamic_slice_in_dim(w_out, dp_index * share, share, 1)
    own_gateup = lax.dynamic_slice_in_dim(w_gateup, dp_index * share, share, 0)
    own_down = lax.dynamic_slice_in_dim(w_down, dp_index * share, share, 1)
    qkv_set = nesterov(sum_qkv / root_count, own_qkv, moment_qkv, average_qkv, RATE_QKV)
    out_set = nesterov(sum_out / root_count, own_out, moment_out, average_out, RATE_OUT)
    gateup_set = nesterov(
        sum_gateup / root_count, own_gateup, moment_gateup, average_gateup, RATE_GATEUP
    )
    down_set = nesterov(sum_down / root_count, own_down, moment_down, average_down, RATE_DOWN)
    gains_set = nesterov(gain_sum / root_count, gains, moment_gains, average_gains, RATE_GAINS)
    return (
        output,
        input_grad,
        first_values_grad,
        qkv_set[0],
        qkv_set[1],
        qkv_set[2],
        qkv_set[3],
        out_set[0],
        out_set[1],
        out_set[2],
        out_set[3],
        gateup_set[0],
        gateup_set[1],
        gateup_set[2],
        gateup_set[3],
        down_set[0],
        down_set[1],
        down_set[2],
        down_set[3],
        gains_set[0],
        gains_set[1],
        gains_set[2],
        gains_set[3],
    )


F32 = jnp.float32
BF16 = jnp.bfloat16
LANES = 128
BLK = 256
PARTS = 3
SWAP = ((0, 1), (1, 0))
VMEM_MIB = 60


def nt(left, right):
    return lax.dot_general(left, right, (((1,), (1,)), ((), ())), preferred_element_type=F32)


def nn(left, right):
    return lax.dot_general(left, right, (((1,), (0,)), ((), ())), preferred_element_type=F32)


def tn(left, right):
    return lax.dot_general(left, right, (((0,), (0,)), ((), ())), preferred_element_type=F32)


def lane_of(rows):
    return lax.broadcasted_iota(jnp.int32, (rows, LANES), 1)


def params(mib):
    return pltpu.CompilerParams(vmem_limit_bytes=mib * 2**20)


def cost(flops, moved, exps=0):
    return pl.CostEstimate(flops=int(flops), bytes_accessed=int(moved), transcendentals=int(exps))


def partner_lanes(pair):
    lane = lane_of(pair.shape[0])
    return jnp.where((lane % HEAD_DIM) < HEAD_DIM // 2, pltpu.roll(pair, LANES - 32, 1), pltpu.roll(pair, 32, 1))


def pair_tables(length):
    cosine, sine = rope_tables(length, HEAD_DIM)
    cosine, sine = cosine[:, 0, :], sine[:, 0, :]
    wide_cos = jnp.concatenate([cosine] * 4, axis=1)
    wide_sin = jnp.concatenate([-sine, sine, -sine, sine], axis=1)
    return wide_cos, wide_sin


def qkv_kernel(base_ref, x_ref, first_ref, gain_ref, w_ref, cos_ref, sin_ref, *refs):
    n_ref, q_ref, k_ref, v_ref = refs[-4:]
    x = x_ref[...].astype(F32)
    inverse = lax.rsqrt(jnp.mean(x * x, axis=-1, keepdims=True) + EPS)
    norm = ((x * inverse) * gain_ref[...]).astype(BF16)
    n_ref[...] = norm
    cosine, sine = cos_ref[...], sin_ref[...]
    for part, out in ((0, q_ref), (1, k_ref)):
        flat = nn(norm, w_ref[:, part * q_ref.shape[1] : (part + 1) * q_ref.shape[1]])
        for c in range(flat.shape[1] // LANES):
            pair = flat[:, c * LANES : (c + 1) * LANES]
            turned = (pair * cosine + partner_lanes(pair) * sine).astype(BF16)
            if part == 0:
                turned = turned * jnp.asarray(0.125, BF16)
            out[:, c * LANES : (c + 1) * LANES] = turned
    v_ref[...] = (HALF * nn(norm, w_ref[:, 2 * q_ref.shape[1] :]) + HALF * first_ref[...].astype(F32)).astype(BF16)


def project_qkv(base, x, first, gain, w, cosine, sine, before):
    rows, model = x.shape
    slot_len, cols = first.shape
    here = lambda i, b: (i, 0)
    there = lambda i, b: (b[0] + i, 0)
    outs = (
        jax.ShapeDtypeStruct((slot_len, model), BF16),
        *(jax.ShapeDtypeStruct((slot_len, cols), BF16) for _ in range(3)),
    )
    before = () if before is None else tuple(before)
    return pl.pallas_call(
        qkv_kernel,
        out_shape=outs,
        grid_spec=pltpu.PrefetchScalarGridSpec(
            num_scalar_prefetch=1,
            grid=(rows // BLK,),
            in_specs=[
                pl.BlockSpec((BLK, model), here),
                pl.BlockSpec((BLK, cols), there),
                pl.BlockSpec((1, model), lambda i, b: (0, 0)),
                pl.BlockSpec((model, PARTS * cols), lambda i, b: (0, 0)),
                pl.BlockSpec((BLK, LANES), there),
                pl.BlockSpec((BLK, LANES), there),
                *(pl.BlockSpec(memory_space=pl.ANY) for _ in before),
            ],
            out_specs=[pl.BlockSpec((BLK, o.shape[1]), there) for o in outs],
        ),
        input_output_aliases={7 + n: n for n in range(len(before))},
        compiler_params=params(VMEM_MIB),
        cost_estimate=cost(2 * rows * model * cols * 3, 10e6),
        name="project_qkv",
    )(base, x, first, gain, w, cosine, sine, *before)


SAFE_SCORE = 60.0


def spare(head):
    return HEAD_DIM * (1 - head)


def own_lanes(lane, head):
    return (lane // HEAD_DIM) == head


def length_bias(slot_len, length):
    row = lax.broadcasted_iota(jnp.int32, (slot_len, LANES), 0)
    return jnp.where(row < length, 0.0, NEG_BIG).astype(BF16)


def causal_bias(mask_ref, query_axis):
    query = lax.broadcasted_iota(jnp.int32, (BLK, BLK), query_axis)
    key = lax.broadcasted_iota(jnp.int32, (BLK, BLK), 1 - query_axis)
    mask_ref[...] = jnp.where(key <= query, 0.0, NEG_BIG)


def largest_square(pair, both):
    flat = pair.astype(F32)
    return jnp.max(nn((flat * flat).astype(BF16), both))


def attend_fwd_kernel(scalar_ref, q_ref, k_ref, v_ref, *refs):
    o_ref, lse_ref, send_ref, ka, va, mask_ref = refs[-6:]
    slot_len = k_ref.shape[0]
    lane = lane_of(slot_len)
    bias = length_bias(slot_len, scalar_ref[0])
    for head in (0, 1):
        mine = own_lanes(lane, head)
        extra = jnp.where(lane == spare(head), bias, jnp.zeros_like(bias))
        ka[head] = jnp.where(mine, k_ref[...], extra)
        va[head] = jnp.where(mine, v_ref[...], jnp.ones_like(bias))
    causal_bias(mask_ref, 0)
    side = lambda axis: lax.broadcasted_iota(jnp.int32, (LANES, LANES), axis) // HEAD_DIM
    both = jnp.where(side(0) == side(1), 1.0, 0.0).astype(BF16)
    reach = largest_square(q_ref[...], both) * largest_square(k_ref[...], both)

    def rows_of(shifted):
        low = lane_of(BLK) < HEAD_DIM
        for i in range(slot_len // BLK):
            queries, seen = pl.ds(i * BLK, BLK), pl.ds(0, (i + 1) * BLK)
            before = i * BLK
            q = q_ref[queries, :]
            outs, peaks = [], []
            for head in (0, 1):
                one = jnp.where(lane_of(BLK) == spare(head), 1.0, 0.0).astype(BF16)
                scores = nt(jnp.where(own_lanes(lane_of(BLK), head), q, one), ka[head, seen, :])
                last = scores[:, before:] + mask_ref[...]
                scores = last if i == 0 else jnp.concatenate([scores[:, :before], last], axis=1)
                if shifted:
                    peak = jnp.max(scores, axis=1, keepdims=True)
                    scores = scores - peak
                    peaks.append(peak)
                outs.append(nn(jnp.exp(scores).astype(BF16), va[head, seen, :]))
            total = pltpu.roll(jnp.where(low, outs[1], outs[0]), HEAD_DIM, 1)
            o_ref[queries, :] = (jnp.where(low, outs[0], outs[1]) / total).astype(BF16)
            shift = jnp.where(low, peaks[0], peaks[1]) if shifted else 0.0
            lse_ref[queries, :] = shift + jnp.log(total)

    small = reach < (0.9 * SAFE_SCORE) ** 2

    @pl.when(small)
    def _():
        rows_of(False)

    @pl.when(jnp.logical_not(small))
    def _():
        rows_of(True)

    half = send_ref.shape[0]
    send_ref[...] = o_ref[pl.ds(pl.multiple_of(scalar_ref[1] * half, half), half), :]


def attend_pairs(first, count, scalars, q, k, v, before):
    slot_len, cols = q.shape
    full = pl.BlockSpec((slot_len, LANES), lambda p, n: (0, first + p))
    before = () if before is None else tuple(before)
    both = pltpu.VMEM((2, slot_len, LANES), BF16)
    return pl.pallas_call(
        attend_fwd_kernel,
        out_shape=(
            jax.ShapeDtypeStruct((slot_len, cols), BF16),
            jax.ShapeDtypeStruct((slot_len, cols), F32),
            jax.ShapeDtypeStruct((slot_len // 2, count * LANES), BF16),
        ),
        grid_spec=pltpu.PrefetchScalarGridSpec(
            num_scalar_prefetch=1,
            grid=(count,),
            in_specs=[full] * 3 + [pl.BlockSpec(memory_space=pl.ANY) for _ in before],
            out_specs=[full, full, pl.BlockSpec((slot_len // 2, LANES), lambda p, n: (0, p))],
            scratch_shapes=[both, both, pltpu.VMEM((BLK, BLK), F32)],
        ),
        input_output_aliases={4 + n: n for n in range(len(before))},
        compiler_params=params(VMEM_MIB),
        cost_estimate=cost(count * 2 * 2 * slot_len * slot_len * 256, 3e6 * count),
        name="attend_pairs",
    )(scalars, q, k, v, *before)


def split3(x):
    high = x.astype(BF16)
    rest = x - high.astype(F32)
    mid = rest.astype(BF16)
    return high, mid, (rest - mid.astype(F32)).astype(BF16)


def attend_back_kernel(scalar_ref, q_ref, k_ref, v_ref, o_ref, lse_ref, mine_ref, theirs_ref, cos_ref, sin_ref, *refs):
    fv_ref, grad_ref, send_ref, ka, va, kz, do_ref, mask_ref, dk_ref, dv_ref = refs[-10:]
    slot_len = k_ref.shape[0]
    half = slot_len // 2
    far_rows = pl.ds(pl.multiple_of(scalar_ref[1] * half, half), half)
    do_ref[pl.ds(pl.multiple_of((1 - scalar_ref[1]) * half, half), half), :] = mine_ref[...]
    do_ref[far_rows, :] = theirs_ref[...]
    lane = lane_of(slot_len)
    bias = length_bias(slot_len, scalar_ref[0])
    zero, minus = jnp.zeros_like(bias), jnp.full_like(bias, -1.0)
    for head in (0, 1):
        mine, at = own_lanes(lane, head), spare(head)
        ones = jnp.where((lane > at) & (lane < at + 4), minus, zero)
        ka[head] = jnp.where(mine, k_ref[...], jnp.where(lane == at, bias, ones))
        va[head] = jnp.where(mine, v_ref[...], ones)
        kz[head] = jnp.where(mine, k_ref[...], zero)
    causal_bias(mask_ref, 1)
    lane = lane_of(BLK)
    low = lane < HEAD_DIM
    zero = jnp.zeros((BLK, LANES), BF16)

    def unturn(grad, rows):
        return grad * cos_ref[rows, :] - partner_lanes(grad) * sin_ref[rows, :]

    for i in range(slot_len // BLK):
        queries, seen = pl.ds(i * BLK, BLK), pl.ds(0, (i + 1) * BLK)
        before = i * BLK
        q, do = q_ref[queries, :], do_ref[queries, :]
        prod = do.astype(F32) * o_ref[queries, :].astype(F32)
        center_low = jnp.sum(jnp.where(low, prod, 0.0), axis=1, keepdims=True)
        center_high = jnp.sum(jnp.where(low, 0.0, prod), axis=1, keepdims=True)
        centers = split3(jnp.where(low, center_high, center_low))
        totals = split3(pltpu.roll(lse_ref[queries, :], HEAD_DIM, 1))
        dq = dk = dv = None
        for head in (0, 1):
            mine = own_lanes(lane, head)

            def place(block, items):
                out = zero
                for n, item in enumerate(items):
                    out = jnp.where(lane == spare(head) + n, item, out)
                return jnp.where(mine, block, out)

            s = nt(ka[head, seen, :], place(q, [jnp.ones_like(zero), *totals]))
            last = s[before:] + mask_ref[...]
            p = jnp.exp(last if i == 0 else jnp.concatenate([s[:before], last], axis=0))
            ds = (p * nt(va[head, seen, :], place(do, [zero, *centers]))).astype(BF16)
            term = nn(p.astype(BF16), jnp.where(mine, do, zero))
            dv = term if dv is None else dv + term
            term = nn(ds, jnp.where(mine, q, zero))
            dk = term if dk is None else dk + term
            term = tn(ds, kz[head, seen, :])
            dq = term if dq is None else dq + term
        if i > 0:
            dv_ref[pl.ds(0, before), :] += dv[:before]
            dk_ref[pl.ds(0, before), :] += dk[:before]
        dv_ref[queries, :] = dv[before:]
        dk_ref[queries, :] = dk[before:]
        grad_ref[queries, 0:LANES] = unturn(dq * 0.125, queries).astype(BF16)
    for i in range(slot_len // BLK):
        keys = pl.ds(i * BLK, BLK)
        half_dv = HALF * dv_ref[keys, :]
        fv_ref[keys, :] = half_dv
        grad_ref[keys, 2 * LANES : 3 * LANES] = half_dv.astype(BF16)
        grad_ref[keys, LANES : 2 * LANES] = unturn(dk_ref[keys, :], keys).astype(BF16)
    send_ref[...] = grad_ref[far_rows, :]


def attend_back_pairs(first, count, scalars, q, k, v, o, lse, mine, theirs, cosine, sine, before):
    slot_len, cols = q.shape
    full = pl.BlockSpec((slot_len, LANES), lambda p, n: (0, first + p))
    own = pl.BlockSpec((slot_len, LANES), lambda p, n: (0, 0))
    before = () if before is None else tuple(before)
    both = pltpu.VMEM((2, slot_len, LANES), BF16)
    acc = pltpu.VMEM((slot_len, LANES), F32)
    wide = PARTS * LANES
    return pl.pallas_call(
        attend_back_kernel,
        out_shape=(
            jax.ShapeDtypeStruct((slot_len, cols), F32),
            jax.ShapeDtypeStruct((slot_len, PARTS * cols), BF16),
            jax.ShapeDtypeStruct((slot_len // 2, count * wide), BF16),
        ),
        grid_spec=pltpu.PrefetchScalarGridSpec(
            num_scalar_prefetch=1,
            grid=(count,),
            in_specs=[full] * 5
            + [
                pl.BlockSpec((slot_len // 2, LANES), lambda p, n: (0, first + p)),
                pl.BlockSpec((slot_len // 2, LANES), lambda p, n: (0, p)),
                own,
                own,
            ]
            + [pl.BlockSpec(memory_space=pl.ANY) for _ in before],
            out_specs=[
                full,
                pl.BlockSpec((slot_len, wide), lambda p, n: (0, first + p)),
                pl.BlockSpec((slot_len // 2, wide), lambda p, n: (0, p)),
            ],
            scratch_shapes=[both, both, both, pltpu.VMEM((slot_len, LANES), BF16),
                            pltpu.VMEM((BLK, BLK), F32), acc, acc],
        ),
        input_output_aliases={10 + n: n for n in range(len(before))},
        compiler_params=params(VMEM_MIB),
        cost_estimate=cost(count * (40 if first > 1 else 10) * slot_len * slot_len * 256, 6e6 * count),
        name="attend_back_pairs",
    )(scalars, q, k, v, o, lse, mine, theirs, cosine, sine, *before)


def resid_kernel(base_ref, x_ref, gain_ref, w_own_ref, w_far_ref, own_ref, *refs):
    own = own_ref[...]
    far = jnp.concatenate([r[...] for r in refs[:-3]], axis=1)
    h_ref, n_ref, o_ref = refs[-3:]
    h = x_ref[...].astype(F32) + (nn(own, w_own_ref[...]) + nn(far, w_far_ref[...]))
    inverse = lax.rsqrt(jnp.mean(h * h, axis=-1, keepdims=True) + EPS)
    h_ref[...] = h.astype(BF16)
    n_ref[...] = ((h * inverse) * gain_ref[...]).astype(BF16)
    cols = own.shape[1]
    o_ref[:, :cols] = far
    o_ref[:, cols:] = own


def resid_rows(base, x, gain, w_own, w_far, own, far):
    rows, model = x.shape
    cols = w_own.shape[0]
    wide = pl.BlockSpec((BLK, model), lambda i, b: (i, 0))
    fixed = pl.BlockSpec((cols, model), lambda i, b: (0, 0))
    return pl.pallas_call(
        resid_kernel,
        out_shape=(
            jax.ShapeDtypeStruct((rows, model), BF16),
            jax.ShapeDtypeStruct((rows, model), BF16),
            jax.ShapeDtypeStruct((rows, 2 * cols), BF16),
        ),
        grid_spec=pltpu.PrefetchScalarGridSpec(
            num_scalar_prefetch=1,
            grid=(rows // BLK,),
            in_specs=[
                wide,
                pl.BlockSpec((1, model), lambda i, b: (0, 0)),
                fixed,
                fixed,
                pl.BlockSpec((BLK, cols), lambda i, b: (b[0] + i, 0)),
                *(pl.BlockSpec((BLK, f.shape[1]), lambda i, b: (i, 0)) for f in far),
            ],
            out_specs=[wide, wide, pl.BlockSpec((BLK, 2 * cols), lambda i, b: (i, 0))],
        ),
        compiler_params=params(VMEM_MIB),
        cost_estimate=cost(2 * rows * model * cols * 2, 14e6),
        name="resid_rows",
    )(base, x, gain, w_own, w_far, own, *far)


def weave_kernel(q_ref, gu_ref, d_ref, out_ref):
    cols = q_ref.shape[2]
    for part in range(PARTS):
        out_ref[:, part * cols : (part + 1) * cols] = q_ref[part].astype(BF16)
    down = d_ref[...].T
    for run in range(gu_ref.shape[2] // LANES):
        lanes = slice(run * LANES, (run + 1) * LANES)
        for part, piece in enumerate((gu_ref[:, 0, lanes], gu_ref[:, 1, lanes], down[:, lanes])):
            spot = PARTS * cols + (3 * run + part) * LANES
            out_ref[:, spot : spot + LANES] = piece.astype(BF16)


def weave(w_qkv, w_gateup, w_down):
    parts, model, cols = w_qkv.shape
    sides, hidden = w_gateup.shape[1:]
    rows = 128
    wide = parts * cols + 3 * hidden
    return pl.pallas_call(
        weave_kernel,
        out_shape=jax.ShapeDtypeStruct((model, wide), BF16),
        grid=(model // rows,),
        in_specs=[
            pl.BlockSpec((parts, rows, cols), lambda i: (0, i, 0)),
            pl.BlockSpec((rows, sides, hidden), lambda i: (i, 0, 0)),
            pl.BlockSpec((hidden, rows), lambda i: (0, i)),
        ],
        out_specs=pl.BlockSpec((rows, wide), lambda i: (i, 0)),
        compiler_params=params(VMEM_MIB),
        cost_estimate=cost(0, 6 * model * wide),
        name="weave",
    )(w_qkv, w_gateup, w_down)


def halve_rows(grad, core, x, keep, send):
    rows = grad.shape[0] // 16
    block = lambda z, i, c: grad[(z * 4 + i * 2 + c) * rows : (z * 4 + i * 2 + c + 1) * rows]
    for i in (0, 1):
        for z in range(4):
            spot = pl.ds((i * 4 + z) * rows, rows)
            same = [jnp.where(x == 0, block(z, i, c), block(z, 1 - i, c)) for c in (0, 1)]
            keep[spot, :] = jnp.where(core == 0, same[0], same[1])
            send[spot, :] = jnp.where(core == 0, same[1], same[0])


def runs(block, count, of, which):
    return jnp.concatenate(
        [block[:, (of * i + which) * LANES : (of * i + which + 1) * LANES] for i in range(count)], axis=1
    )


def swiglu_kernel(halved, place_ref, n_ref, dy_ref, w_ref, y_ref, dn_ref, *refs):
    y_acc, dn_acc = refs[-2:]
    step = pl.program_id(0)
    last = pl.num_programs(0) - 1

    def work(count, first):
        n = n_ref[...]
        dy = dy_ref[...]
        run = lambda i: w_ref[:, i * LANES : (i + 1) * LANES]
        wgu = jnp.concatenate([run(3 * i + j) for i in range(count) for j in (0, 1)], axis=1)
        wd = jnp.concatenate([run(3 * i + 2) for i in range(count)], axis=1)
        both = nn(n, wgu)
        gate, up = runs(both, count, 2, 0), runs(both, count, 2, 1)
        sig = jax.nn.sigmoid(gate)
        silu = gate * sig
        hid = (silu * up).astype(BF16)
        dhid = nn(dy, wd)
        dgate = (dhid * up * sig * (1.0 + gate * (1.0 - sig))).astype(BF16)
        dup = (dhid * silu).astype(BF16)
        dgu = jnp.concatenate(
            [d[:, i * LANES : (i + 1) * LANES] for i in range(count) for d in (dgate, dup)], axis=1
        )
        y = nt(hid, wd)
        dn = nt(dgu, wgu)
        if first:
            y_acc[...] = y
            dn_acc[...] = dn
        else:
            y_acc[...] += y
            dn_acc[...] += dn
        grad_gu = tn(n, dgu).astype(BF16)
        grad_d = tn(dy, hid).astype(BF16)
        for i in range(count):
            for part, grad in enumerate((grad_gu[:, 2 * i * LANES : (2 * i + 2) * LANES],
                                         grad_d[:, i * LANES : (i + 1) * LANES])):
                start = (3 * i + 2 * part) * LANES
                spot = slice(start, start + grad.shape[1])
                if halved:
                    halve_rows(grad, place_ref[0], place_ref[1], refs[0].at[:, spot], refs[1].at[:, spot])
                else:
                    refs[0][:, spot] = grad

    @pl.when(step == 0)
    def _():
        work(2, True)

    @pl.when((step > 0) & (step < last))
    def _():
        work(2, False)

    @pl.when(step == last)
    def _():
        work(1, False)
        y_ref[...] = y_acc[...].astype(BF16)
        dn_ref[...] = dn_acc[...].astype(BF16)


def swiglu_half(place, n, dy, w, first, width=None):
    rows, model = n.shape
    tile = 256
    skip = first // (3 * tile)
    hidden = (w.shape[1] - first) // 3
    held = pl.BlockSpec((rows, model), lambda t, p: (0, 0))
    cols = pl.BlockSpec((model, 3 * tile), lambda t, p: (0, t))
    source = pl.BlockSpec((model, 3 * tile), lambda t, p: (0, skip + t))
    half = pl.BlockSpec((model // 2, 3 * tile), lambda t, p: (0, t))
    grads = [(model, 3 * hidden)] if width is None else [(model // 2, width)] * 2
    return pl.pallas_call(
        functools.partial(swiglu_kernel, width is not None),
        out_shape=(
            *(jax.ShapeDtypeStruct((rows, model), BF16) for _ in range(2)),
            *(jax.ShapeDtypeStruct(g, BF16) for g in grads),
        ),
        grid_spec=pltpu.PrefetchScalarGridSpec(
            num_scalar_prefetch=1,
            grid=(-(-hidden // tile),),
            in_specs=[held, held, source],
            out_specs=[held, held] + ([cols] if width is None else [half, half]),
            scratch_shapes=[pltpu.VMEM((rows, model), F32)] * 2,
        ),
        compiler_params=params(VMEM_MIB),
        cost_estimate=cost(9 * 2 * rows * model * hidden, 36e6, rows * hidden),
        name="swiglu_half",
    )(place, n, dy, w)


def grad_out_kernel(place_ref, dhb_ref, o_ref, keep_ref, send_ref):
    grad = tn(dhb_ref[...], o_ref[...]).astype(BF16)
    halve_rows(grad, place_ref[0], place_ref[1], keep_ref, send_ref)


def grad_out_of(place, dhb, o_cat):
    rows, model = dhb.shape
    tile = 512
    out = pl.BlockSpec((model // 2, tile), lambda t, p: (0, t))
    return pl.pallas_call(
        grad_out_kernel,
        out_shape=[jax.ShapeDtypeStruct((model // 2, o_cat.shape[1]), BF16)] * 2,
        grid_spec=pltpu.PrefetchScalarGridSpec(
            num_scalar_prefetch=1,
            grid=(o_cat.shape[1] // tile,),
            in_specs=[
                pl.BlockSpec((rows, model), lambda t, p: (0, 0)),
                pl.BlockSpec((rows, tile), lambda t, p: (0, t)),
            ],
            out_specs=[out, out],
        ),
        compiler_params=params(VMEM_MIB),
        cost_estimate=cost(2 * rows * model * o_cat.shape[1], 7e6),
        name="grad_out",
    )(place, dhb, o_cat)


def grad_qkv_kernel(place_ref, n_ref, dqkv_ref, *refs):
    keep_ref, send_ref, t_ref = refs[PARTS:]
    grad = tn(n_ref[...], dqkv_ref[...])
    term = None
    for i in range(grad.shape[1] // LANES):
        weight = refs[i % PARTS][:, (i // PARTS) * LANES : (i // PARTS + 1) * LANES]
        piece = grad[:, i * LANES : (i + 1) * LANES] * weight.astype(F32)
        term = piece if term is None else term + piece

    @pl.when(pl.program_id(0) == 0)
    def _():
        t_ref[...] = term

    @pl.when(pl.program_id(0) > 0)
    def _():
        t_ref[...] += term

    halve_rows(grad.astype(BF16), place_ref[0], place_ref[1], keep_ref, send_ref)


def grad_qkv_of(place, norm, dqkv, w):
    slot_len, model = norm.shape
    pairs = 2
    tile = pairs * PARTS * LANES
    steps = dqkv.shape[1] // tile
    out = pl.BlockSpec((model // 2, tile), lambda t, p: (0, t))
    return pl.pallas_call(
        grad_qkv_kernel,
        out_shape=(
            *(jax.ShapeDtypeStruct((model // 2, dqkv.shape[1]), BF16) for _ in range(2)),
            jax.ShapeDtypeStruct((model, LANES), F32),
        ),
        grid_spec=pltpu.PrefetchScalarGridSpec(
            num_scalar_prefetch=1,
            grid=(steps,),
            in_specs=[
                pl.BlockSpec((slot_len, model), lambda t, p: (0, 0)),
                pl.BlockSpec((slot_len, tile), lambda t, p: (0, t)),
                *(
                    pl.BlockSpec((model, pairs * LANES), lambda t, p, part=part: (0, part * steps + t))
                    for part in range(PARTS)
                ),
            ],
            out_specs=[out, out, pl.BlockSpec((model, LANES), lambda t, p: (0, 0))],
        ),
        compiler_params=params(VMEM_MIB),
        cost_estimate=cost(8 * slot_len * model * dqkv.shape[1], 14e6),
        name="grad_qkv",
    )(place, norm, dqkv, *[w] * PARTS)


def after_kernel(h_ref, y1_ref, y2_ref, d1_ref, d2_ref, dy_ref, gain_ref, w_own_ref, w_far_ref,
                 out_ref, dhb_ref, own_ref, far_ref, t_ref):
    h = h_ref[...].astype(F32)
    out_ref[...] = (h + (y1_ref[...].astype(F32) + y2_ref[...].astype(F32))).astype(BF16)
    inverse = lax.rsqrt(jnp.mean(h * h, axis=-1, keepdims=True) + EPS)
    unit = h * inverse
    dn = d1_ref[...].astype(F32) + d2_ref[...].astype(F32)
    e = dn * gain_ref[...]
    dh = dy_ref[...].astype(F32) + inverse * (e - unit * jnp.mean(e * unit, axis=-1, keepdims=True))
    dhb = dh.astype(BF16)
    dhb_ref[...] = dhb
    own_ref[...] = nt(dhb, w_own_ref[...]).astype(BF16)
    far_ref[...] = nt(dhb, w_far_ref[...]).astype(BF16)

    @pl.when(pl.program_id(0) == 0)
    def _():
        t_ref[...] = jnp.zeros_like(t_ref)

    t_ref[...] += jnp.sum(dn * unit, axis=0, keepdims=True)


def after_rows(h, y1, y2, d1, d2, dy, gain, w_own, w_far):
    rows, model = h.shape
    cols = w_own.shape[0]
    wide = pl.BlockSpec((BLK, model), lambda i: (i, 0))
    fixed = pl.BlockSpec((cols, model), lambda i: (0, 0))
    slim = pl.BlockSpec((BLK, cols), lambda i: (i, 0))
    one = pl.BlockSpec((1, model), lambda i: (0, 0))
    return pl.pallas_call(
        after_kernel,
        out_shape=(
            jax.ShapeDtypeStruct((rows, model), BF16),
            jax.ShapeDtypeStruct((rows, model), BF16),
            jax.ShapeDtypeStruct((rows, cols), BF16),
            jax.ShapeDtypeStruct((rows, cols), BF16),
            jax.ShapeDtypeStruct((1, model), F32),
        ),
        grid=(rows // BLK,),
        in_specs=[wide] * 6 + [one, fixed, fixed],
        out_specs=[wide, wide, slim, slim, one],
        compiler_params=params(VMEM_MIB),
        cost_estimate=cost(2 * rows * model * cols * 2, 36e6),
        name="after_rows",
    )(h, y1, y2, d1, d2, dy, gain, w_own, w_far)


def input_kernel(base_ref, x_ref, dh_ref, gain_ref, w_own_ref, w_far_ref, *refs):
    out_ref = refs[-1]
    dn = None
    for weights, grads in ((w_own_ref, refs[:1]), (w_far_ref, refs[1:-1])):
        flat = jnp.concatenate([g[...] for g in grads], axis=1)
        count = flat.shape[1] // (PARTS * LANES)
        lanes = jnp.concatenate([runs(flat, count, PARTS, part) for part in range(PARTS)], axis=1)
        term = nt(lanes, weights[...])
        dn = term if dn is None else dn + term
    x = x_ref[...].astype(F32)
    inverse = lax.rsqrt(jnp.mean(x * x, axis=-1, keepdims=True) + EPS)
    unit = x * inverse
    e = dn * gain_ref[...]
    out_ref[...] = dh_ref[...].astype(F32) + inverse * (e - unit * jnp.mean(e * unit, axis=-1, keepdims=True))


def input_rows(base, x, dh, gain, w_own, w_far, own, far):
    rows, model = x.shape
    cols = own.shape[1] // PARTS
    wide = pl.BlockSpec((BLK, model), lambda i, b: (i, 0))
    fixed = pl.BlockSpec((model, PARTS * cols), lambda i, b: (0, 0))
    return pl.pallas_call(
        input_kernel,
        out_shape=jax.ShapeDtypeStruct((rows, model), F32),
        grid_spec=pltpu.PrefetchScalarGridSpec(
            num_scalar_prefetch=1,
            grid=(rows // BLK,),
            in_specs=[wide, wide, pl.BlockSpec((1, model), lambda i, b: (0, 0)), fixed, fixed]
            + [pl.BlockSpec((BLK, own.shape[1]), lambda i, b: (b[0] + i, 0))]
            + [pl.BlockSpec((BLK, f.shape[1]), lambda i, b: (i, 0)) for f in far],
            out_specs=wide,
        ),
        compiler_params=params(VMEM_MIB),
        cost_estimate=cost(8 * rows * model * cols * 6, 20e6),
        name="input_rows",
    )(base, x, dh, gain, w_own, w_far, own, *far)


def step_of(sum_grad, weight, moment, average, rate, root_count):
    return nesterov(sum_grad / root_count, weight, moment, average, rate)


def own_columns(place, wide):
    turned = wide.T
    half = turned.shape[0] // 2
    return jnp.where(place == 0, turned[:half], turned[half:])


def step_mlp_kernel(root_count, place_ref, sum_ref, got_ref, wgu_ref, mgu_ref, agu_ref, wd_ref, md_ref, ad_ref, *outs):
    total = sum_ref[...].astype(F32) + got_ref[...].astype(F32)
    count = total.shape[1] // (3 * LANES)
    for side in (0, 1):
        grads = step_of(runs(total, count, 3, side), wgu_ref[:, side, :], mgu_ref[:, side, :],
                        agu_ref[:, side, :], RATE_GATEUP, root_count)
        for out, value in zip(outs[:4], grads):
            out[:, side, :] = value
    weight = own_columns(place_ref[1], wd_ref[...])
    grads = step_of(runs(total, count, 3, 2), weight, md_ref[...], ad_ref[...], RATE_DOWN, root_count)
    for out, value in zip(outs[4:], grads):
        out[...] = value


def step_mlp(dp_index, root_count, total, got, w_gateup, m_gu, a_gu, w_down, m_d, a_d):
    place = jnp.stack([dp_index, dp_index % 2, dp_index // 2]).astype(jnp.int32)
    share, sides, hidden = m_gu.shape
    cols = total.shape[1]
    gu = pl.BlockSpec((share, sides, hidden), lambda i, p: (0, 0, 0))
    d = pl.BlockSpec((share, hidden), lambda i, p: (0, 0))
    return pl.pallas_call(
        functools.partial(step_mlp_kernel, root_count),
        out_shape=(
            *(jax.ShapeDtypeStruct(m_gu.shape, F32) for _ in range(4)),
            *(jax.ShapeDtypeStruct((share, hidden), F32) for _ in range(4)),
        ),
        grid_spec=pltpu.PrefetchScalarGridSpec(
            num_scalar_prefetch=1,
            grid=(1,),
            in_specs=[
                pl.BlockSpec((share, cols), lambda i, p: (0, 0)),
                pl.BlockSpec((share, cols), lambda i, p: (0, 0)),
                pl.BlockSpec((share, sides, hidden), lambda i, p: (p[0], 0, 0)),
                gu,
                gu,
                pl.BlockSpec((hidden, LANES), lambda i, p: (0, p[2])),
                d,
                d,
            ],
            out_specs=[gu] * 4 + [d] * 4,
        ),
        compiler_params=params(VMEM_MIB),
        cost_estimate=cost(0, 14e6),
        name="step_mlp",
    )(place, total, got, w_gateup, m_gu, a_gu, w_down, m_d, a_d)


def step_attention_kernel(root_count, place_ref, sum_ref, own_ref, got_ref, wq_ref, mq_ref, aq_ref, wo_ref, mo_ref, ao_ref, *outs):
    total = sum_ref[...]
    count = total.shape[1] // (PARTS * LANES)
    for part in range(PARTS):
        grads = step_of(runs(total, count, PARTS, part), wq_ref[part], mq_ref[part], aq_ref[part],
                        RATE_QKV, root_count)
        for out, value in zip(outs[:4], grads):
            out[part] = value
    weight = own_columns(place_ref[1], wo_ref[...])
    grads = step_of(own_ref[...].astype(F32) + got_ref[...].astype(F32), weight, mo_ref[...], ao_ref[...],
                    RATE_OUT, root_count)
    for out, value in zip(outs[4:], grads):
        out[...] = value


def step_attention(dp_index, root_count, total, own, got, w_qkv, m_q, a_q, w_out, m_o, a_o):
    place = jnp.stack([dp_index, dp_index % 2, dp_index // 2]).astype(jnp.int32)
    parts, share, cols = m_q.shape
    q = pl.BlockSpec((parts, share, cols), lambda i, p: (0, 0, 0))
    o = pl.BlockSpec((share, cols), lambda i, p: (0, 0))
    return pl.pallas_call(
        functools.partial(step_attention_kernel, root_count),
        out_shape=(
            *(jax.ShapeDtypeStruct(m_q.shape, F32) for _ in range(4)),
            *(jax.ShapeDtypeStruct((share, cols), F32) for _ in range(4)),
        ),
        grid_spec=pltpu.PrefetchScalarGridSpec(
            num_scalar_prefetch=1,
            grid=(1,),
            in_specs=[
                pl.BlockSpec((share, parts * cols), lambda i, p: (0, 0)),
                o,
                o,
                pl.BlockSpec((parts, share, cols), lambda i, p: (0, p[0], 0)),
                q,
                q,
                pl.BlockSpec((cols, LANES), lambda i, p: (0, p[2])),
                o,
                o,
            ],
            out_specs=[q] * 4 + [o] * 4,
        ),
        compiler_params=params(VMEM_MIB),
        cost_estimate=cost(0, 6e6),
        name="step_attention",
    )(place, total, own, got, w_qkv, m_q, a_q, w_out, m_o, a_o)


def dp_pairs(move):
    return tuple((i, move(i)) for i in range(16))


CORE = dp_pairs(lambda i: i ^ 1)
CROSS = dp_pairs(lambda i: i ^ 2)
Z_LINES = tuple(tuple(z * 4 + i for z in range(4)) for i in range(4))
NEAR = tuple(
    tuple((i, i ^ flip) for i in range(32)) for flip in (1, 2, 3)
)
ALONG = tuple(dp_pairs(lambda i, step=step: (i + 4 * step) % 16) for step in (1, 2, 3))


def move(x, pairs):
    return lax.ppermute(x, "dp", pairs)


def add(left, right):
    return left.astype(F32) + right.astype(F32)


def after_core(keep, got):
    half = keep.shape[0] // 2
    here = add(keep[:half], got[:half]).astype(BF16)
    away = add(keep[half:], got[half:]).astype(BF16)
    return here, away


def after_cross(here, got, z):
    total = add(here, got)
    rows = here.shape[0] // 4
    block = lambda step: lax.dynamic_slice_in_dim(total, lax.rem(z + step, 4) * rows, rows, 0)
    return block(0), tuple(block(step).astype(BF16) for step in (1, 2, 3))


def after_along(mine, got):
    for piece in got:
        mine = mine + piece.astype(F32)
    return mine


def tie(values, *others):
    return lax.optimization_barrier((values, others))[0]


def shards_pair(
    tokens,
    first_values,
    lengths,
    cotangent,
    w_qkv,
    w_out,
    w_gateup,
    w_down,
    gains,
    moment_qkv,
    moment_out,
    moment_gateup,
    moment_down,
    moment_gains,
    average_qkv,
    average_out,
    average_gateup,
    average_down,
    average_gains,
):
    rows, model = tokens.shape
    mp_index = lax.axis_index("mp")
    dp_index = lax.axis_index("dp")
    dp_count = lax.axis_size("dp")
    z, core = dp_index // 4, dp_index % 2
    place = jnp.stack([core, (dp_index // 2) % 2]).astype(jnp.int32)
    slot_len = 2 * rows
    head_cols = w_qkv.shape[2]
    hidden = w_gateup.shape[2]
    pairs = head_cols // LANES
    root_count = math.sqrt(slot_len * dp_count)
    row_start = mp_index * rows
    far_start = (1 - mp_index) * rows
    gain_one, gain_two = gains[0:1], gains[1:2]

    def swap(x):
        return lax.ppermute(x, "mp", SWAP)

    def chunk(x):
        part = x.shape[0] // dp_count
        return lax.dynamic_slice_in_dim(x, dp_index * part, part, 0)

    def gather(x):
        return lax.all_gather(x, "dp", axis=0, tiled=True)

    far_tokens = swap(tokens)
    out_bf = w_out.astype(BF16)
    woven = weave(w_qkv.transpose(1, 0, 2), w_gateup, w_down)
    cosine, sine = pair_tables(slot_len)
    block_of = lambda start: (start // BLK).astype(jnp.int32)
    base, far_base = block_of(row_start).reshape(1), block_of(far_start).reshape(1)
    own_part = project_qkv(base, tokens, first_values, gain_one, woven, cosine, sine, None)
    place_row = row_start + jnp.arange(rows, dtype=jnp.int32)
    dy = jnp.where((place_row < lengths[0])[:, None], cotangent, jnp.zeros_like(cotangent))
    far_tokens, own_part, woven, dy, out_bf = lax.optimization_barrier(
        (far_tokens, own_part, woven, dy, out_bf)
    )
    woven_chunk = swap(chunk(woven))
    norm_one, q, k, v = project_qkv(
        far_base, far_tokens, first_values, gain_one, woven, cosine, sine, own_part
    )
    q, woven_chunk = lax.optimization_barrier((q, woven_chunk))
    woven_far = gather(woven_chunk)
    out_far = swap(tie(out_bf, woven_chunk))

    scalars = jnp.concatenate([lengths, (1 - mp_index).reshape(1).astype(jnp.int32)])
    early = pairs - 1
    o_all, lse_all, away = attend_pairs(0, early, scalars, q, k, v, None)
    o_far = [swap(away)]
    o_all, lse_all, away = attend_pairs(early, pairs - early, scalars, q, k, v, (o_all, lse_all))
    o_far.append(swap(away))
    h, norm_two, o_cat = resid_rows(base, tokens, gain_two, out_bf, out_far, o_all, o_far)

    y_own, dn_own, grads_own = swiglu_half(place, norm_two, dy, woven, PARTS * head_cols)
    sum_own = lax.psum_scatter(grads_own, "dp", scatter_dimension=0, tiled=True)
    norm_two, woven_far = tie((norm_two, woven_far), y_own)
    y_far, dn_far, keep_far, send_far = swiglu_half(
        place, norm_two, dy, woven_far, PARTS * head_cols, 3 * hidden
    )
    got_far = move(send_far, CORE)
    output, dhb, do_own, do_far, gain_two_part = after_rows(
        h, y_own, y_far, dn_own, dn_far, dy, gain_two, out_bf, out_far
    )
    theirs = [swap(do_far[:, :LANES])]
    theirs.append(swap(tie(do_far, theirs[0])[:, LANES:]))
    keep_out, send_out = grad_out_of(place, dhb, o_cat)
    here_far, away_far = after_core(keep_far, tie(got_far, keep_out))
    got_far = move(away_far, CROSS)
    got_out = move(send_out, CORE)

    dqkv_far = []

    def back(first, count, theirs, before):
        first_grad, dqkv, away = attend_back_pairs(
            first, count, scalars, q, k, v, o_all, lse_all, do_own, theirs, cosine, sine, before
        )
        dqkv_far.append(swap(away))
        return first_grad, dqkv

    done = back(0, 1, tie(theirs[0], keep_out, away_far), None)
    here_out, away_out = after_core(keep_out, tie(got_out, done))
    got_out = move(away_out, CROSS)
    done = back(1, pairs - 2, tie(theirs[1], away_out), done)
    done, dqkv_far[0] = lax.optimization_barrier((done, dqkv_far[0]))
    total_far = jnp.concatenate(
        [add(here_far, tie(got_far, done)), add(here_out, tie(got_out, done))], axis=1
    ).astype(BF16)
    sum_far = lax.psum_scatter(
        tie(total_far, sum_own), "dp", scatter_dimension=0, tiled=True, axis_index_groups=Z_LINES
    )
    last, sum_own = lax.optimization_barrier((tie(theirs[1], total_far), sum_own))
    first_grad, dqkv = back(pairs - 1, 1, last[:, (pairs - 2) * LANES :], done)

    keep_qkv, send_qkv, gain_one_lanes = grad_qkv_of(place, norm_one, dqkv, woven)
    got_qkv = move(send_qkv, CORE)
    gain_one_part = jnp.sum(gain_one_lanes, axis=1) / gains[0]
    parts = jnp.stack([gain_one_part, gain_two_part[0]], axis=0)
    near = [lax.ppermute(parts, ("dp", "mp"), p) for p in NEAR]
    got_qkv, near, dqkv_far[1] = lax.optimization_barrier((got_qkv, near, dqkv_far[1]))
    here_qkv, away_qkv = after_core(keep_qkv, got_qkv)
    got_qkv = move(away_qkv, CROSS)
    parts = after_along(parts, near)
    cross = move(parts, CROSS)
    input_grad = input_rows(
        base, tokens, tie(dhb, away_qkv, parts), gain_one, woven, woven_far, dqkv, dqkv_far
    )
    got_qkv, cross, sum_far = tie((got_qkv, cross, sum_far), input_grad)
    cut = 3 * hidden
    got_swap = swap(sum_far[:, : cut + head_cols])
    mine_qkv, blocks_qkv = after_cross(here_qkv, got_qkv, z)
    got_qkv = tuple(move(b, p) for b, p in zip(blocks_qkv, ALONG))
    parts = parts + cross
    along = [move(parts, p) for p in ALONG]

    gateup_down = step_mlp(
        dp_index, root_count, tie(sum_own, blocks_qkv, parts), got_swap[:, :cut], w_gateup,
        moment_gateup, average_gateup, w_down, moment_down.T, average_down.T,
    )
    got_qkv, along = tie((got_qkv, along), gateup_down[0])
    gain_sum = after_along(parts, along)
    sum_qkv = after_along(mine_qkv, got_qkv)
    turn = lambda x: x.transpose(1, 0, 2)
    qkv_out = step_attention(
        dp_index, root_count, sum_qkv, sum_far[:, cut + head_cols :], got_swap[:, cut:],
        turn(w_qkv), turn(moment_qkv), turn(average_qkv), w_out, moment_out.T, average_out.T,
    )
    gains_set = nesterov(gain_sum / root_count, gains, moment_gains, average_gains, RATE_GAINS)
    return (
        output,
        input_grad,
        first_grad,
        *(turn(x) for x in qkv_out[:4]),
        *(x.T for x in qkv_out[4:]),
        *gateup_down[:4],
        *(x.T for x in gateup_down[4:]),
        *gains_set,
    )


def solution(mesh):
    placed = (
        P(("dp", "mp"), None),
        P("dp", "mp"),
        P("dp"),
        P(("dp", "mp"), None),
        P(None, None, "mp"),
        P("mp", None),
        P(None, None, "mp"),
        P("mp", None),
        P(),
        P("dp", None, "mp"),
        P("mp", "dp"),
        P("dp", None, "mp"),
        P("mp", "dp"),
        P(),
        P("dp", None, "mp"),
        P("mp", "dp"),
        P("dp", None, "mp"),
        P("mp", "dp"),
        P(),
    )
    return jax.shard_map(
        shards_pair if (mesh.shape["dp"], mesh.shape["mp"]) == (16, 2) else shards_any,
        mesh=mesh,
        in_specs=placed,
        out_specs=(
            P(("dp", "mp"), None),
            P(("dp", "mp"), None),
            P("dp", "mp"),
            P("dp", None, "mp"),
            P("dp", None, "mp"),
            P("dp", None, "mp"),
            P("dp", None, "mp"),
            P("mp", "dp"),
            P("mp", "dp"),
            P("mp", "dp"),
            P("mp", "dp"),
            P("dp", None, "mp"),
            P("dp", None, "mp"),
            P("dp", None, "mp"),
            P("dp", None, "mp"),
            P("mp", "dp"),
            P("mp", "dp"),
            P("mp", "dp"),
            P("mp", "dp"),
            P(),
            P(),
            P(),
            P(),
        ),
        check_vma=False,
    )
```

```python
import functools
import math

import jax
import jax.numpy as jnp
from jax import lax
from jax.experimental import pallas as pl
from jax.experimental.pallas import tpu as pltpu
from jax.sharding import PartitionSpec as P

HEAD_DIM = 64


EPS = 1e-06
NEG_BIG = -1e30
HALF = 0.5
MOMENTUM = 0.5
AVERAGE_DECAY = 0.5
RATE_QKV = 0.05
RATE_OUT = 20.0
RATE_GATEUP = 0.12
RATE_DOWN = 0.04
RATE_GAINS = 0.6


def normalize(values, gain):
    inverse = lax.rsqrt(jnp.mean(values * values, axis=-1, keepdims=True) + EPS)
    unit = values * inverse
    return (unit * gain, unit, inverse)


def norm_back(grad_norm, gain, unit, inverse):
    scaled = grad_norm * gain
    return inverse * (scaled - unit * jnp.mean(scaled * unit, axis=-1, keepdims=True))


def rope_tables(length, head_size):
    half_size = head_size // 2
    freqs = jnp.power(10000.0, -2.0 * jnp.arange(half_size, dtype=jnp.float32) / head_size)
    angles = jnp.arange(length, dtype=jnp.float32)[:, None] * freqs[None, :]
    return (jnp.cos(angles)[:, None, :], jnp.sin(angles)[:, None, :])


def rotate(values, cosine, sine):
    half_size = values.shape[-1] // 2
    first_half = values[..., :half_size]
    second_half = values[..., half_size:]
    return jnp.concatenate(
        [first_half * cosine - second_half * sine, second_half * cosine + first_half * sine],
        axis=-1,
    )


def unrotate(grads, cosine, sine):
    half_size = grads.shape[-1] // 2
    first_half = grads[..., :half_size]
    second_half = grads[..., half_size:]
    return jnp.concatenate(
        [first_half * cosine + second_half * sine, second_half * cosine - first_half * sine],
        axis=-1,
    )


def dot_last(left, right):
    return lax.dot_general(
        left, right, (((1,), (1,)), ((), ())), preferred_element_type=jnp.float32
    )


def dot_first(left, right):
    return lax.dot_general(
        left, right, (((0,), (0,)), ((), ())), preferred_element_type=jnp.float32
    )


def block_scores(query_block, keys, start, length, scale):
    block_len = query_block.shape[0]
    key_len = keys.shape[0]
    scores = (
        jnp.einsum("qhd,khd->hqk", query_block, keys, preferred_element_type=jnp.float32) * scale
    )
    query_pos = start + jnp.arange(block_len, dtype=jnp.int32)
    key_pos = jnp.arange(key_len, dtype=jnp.int32)
    allowed = (key_pos[None, :] <= query_pos[:, None]) & (key_pos[None, :] < length)
    return jnp.where(allowed[None], scores, NEG_BIG)


def attend_forward(queries, keys, values, lengths):
    slot_count, slot_len, heads_here, head_size = queries.shape
    block_len = min(512, slot_len)
    blocks = slot_len // block_len
    scale = 1.0 / math.sqrt(head_size)
    starts = jnp.arange(blocks, dtype=jnp.int32) * block_len

    def per_slot(item):
        slot_queries, slot_keys, slot_values, length = item

        def per_block(inner):
            query_block, start = inner
            scores = block_scores(query_block, slot_keys, start, length, scale)
            peak = jnp.max(scores, axis=-1, keepdims=True)
            raw_weights = jnp.exp(scores - peak)
            total = jnp.sum(raw_weights, axis=-1, keepdims=True)
            probs = raw_weights / total
            mixed = jnp.einsum(
                "hqk,khd->qhd",
                probs.astype(jnp.bfloat16),
                slot_values,
                preferred_element_type=jnp.float32,
            )
            return (mixed, (peak + jnp.log(total))[..., 0])

        mixed, log_totals = lax.map(
            per_block, (slot_queries.reshape(blocks, block_len, heads_here, head_size), starts)
        )
        return (mixed.reshape(slot_len, heads_here, head_size), log_totals)

    return lax.map(per_slot, (queries, keys, values, lengths))


def attend_backward(queries, keys, values, lengths, grad_mixed, log_totals):
    slot_count, slot_len, heads_here, head_size = queries.shape
    block_len = min(512, slot_len)
    blocks = slot_len // block_len
    scale = 1.0 / math.sqrt(head_size)
    starts = jnp.arange(blocks, dtype=jnp.int32) * block_len

    def per_slot(item):
        slot_queries, slot_keys, slot_values, length, slot_grads, slot_totals = item

        def per_block(carry, inner):
            key_grad, value_grad = carry
            query_block, grad_block, total_block, start = inner
            scores = block_scores(query_block, slot_keys, start, length, scale)
            probs = jnp.exp(scores - total_block[..., None])
            prob_grad = jnp.einsum(
                "qhd,khd->hqk", grad_block, slot_values, preferred_element_type=jnp.float32
            )
            center = jnp.sum(probs * prob_grad, axis=-1, keepdims=True)
            score_grad = (probs * (prob_grad - center)).astype(jnp.bfloat16)
            query_grad = (
                jnp.einsum(
                    "hqk,khd->qhd", score_grad, slot_keys, preferred_element_type=jnp.float32
                )
                * scale
            )
            key_grad = (
                key_grad
                + jnp.einsum(
                    "hqk,qhd->khd", score_grad, query_block, preferred_element_type=jnp.float32
                )
                * scale
            )
            value_grad = value_grad + jnp.einsum(
                "hqk,qhd->khd",
                probs.astype(jnp.bfloat16),
                grad_block,
                preferred_element_type=jnp.float32,
            )
            return ((key_grad, value_grad), query_grad)

        empty = jnp.zeros((slot_len, heads_here, head_size), jnp.float32)
        shaped_queries = slot_queries.reshape(blocks, block_len, heads_here, head_size)
        shaped_grads = slot_grads.reshape(blocks, block_len, heads_here, head_size)
        (key_grad, value_grad), query_grad = lax.scan(
            per_block, (empty, empty), (shaped_queries, shaped_grads, slot_totals, starts)
        )
        return (query_grad.reshape(slot_len, heads_here, head_size), key_grad, value_grad)

    return lax.map(per_slot, (queries, keys, values, lengths, grad_mixed, log_totals))


def row_valid(lengths, slot_len, start, count):
    index = start + jnp.arange(count, dtype=jnp.int32)
    slot_of = index // slot_len
    place = index % slot_len
    slot_ids = jnp.arange(lengths.shape[0], dtype=jnp.int32)
    limit = jnp.sum(jnp.where(slot_of[:, None] == slot_ids[None, :], lengths[None, :], 0), axis=1)
    return (place < limit).astype(jnp.float32)


def nesterov(grad, weight, moment, average, rate):
    moment_new = MOMENTUM * moment + grad
    weight_new = weight - rate * (grad + MOMENTUM * moment_new)
    average_new = AVERAGE_DECAY * average + (1.0 - AVERAGE_DECAY) * weight_new
    return (grad, moment_new, average_new, weight_new)


def shards_any(
    tokens,
    first_values,
    lengths,
    cotangent,
    w_qkv,
    w_out,
    w_gateup,
    w_down,
    gains,
    moment_qkv,
    moment_out,
    moment_gateup,
    moment_down,
    moment_gains,
    average_qkv,
    average_out,
    average_gateup,
    average_down,
    average_gains,
):
    local_rows, model = tokens.shape
    mp_count = lax.axis_size("mp")
    dp_count = lax.axis_size("dp")
    mp_index = lax.axis_index("mp")
    dp_index = lax.axis_index("dp")
    slot_count = lengths.shape[0]
    group_rows = local_rows * mp_count
    slot_len = group_rows // slot_count
    head_cols = w_qkv.shape[2]
    hidden_cols = w_gateup.shape[2]
    heads_here = head_cols // HEAD_DIM
    row_start = mp_index * local_rows
    all_tokens = group_rows * dp_count
    root_count = math.sqrt(all_tokens)
    qkv_bf = w_qkv.astype(jnp.bfloat16).reshape(model, 3 * head_cols)
    out_bf = w_out.astype(jnp.bfloat16)
    gateup_bf = w_gateup.astype(jnp.bfloat16).reshape(model, 2 * hidden_cols)
    down_bf = w_down.astype(jnp.bfloat16)
    gain_one = gains[0]
    gain_two = gains[1]
    valid_local = row_valid(lengths, slot_len, row_start, local_rows)
    x_local = tokens.astype(jnp.float32)
    x_group = lax.all_gather(tokens, "mp", axis=0, tiled=True).astype(jnp.float32)
    norm_one, unit_one, inverse_one = normalize(x_group, gain_one)
    norm_one_bf = norm_one.astype(jnp.bfloat16)
    qkv = jnp.dot(norm_one_bf, qkv_bf, preferred_element_type=jnp.float32)
    qkv = qkv.reshape(slot_count, slot_len, 3, heads_here, HEAD_DIM)
    cosine, sine = rope_tables(slot_len, HEAD_DIM)
    queries = rotate(qkv[:, :, 0], cosine, sine).astype(jnp.bfloat16)
    keys = rotate(qkv[:, :, 1], cosine, sine).astype(jnp.bfloat16)
    first_shaped = first_values.astype(jnp.float32).reshape(
        slot_count, slot_len, heads_here, HEAD_DIM
    )
    values = (HALF * qkv[:, :, 2] + HALF * first_shaped).astype(jnp.bfloat16)
    mixed, log_totals = attend_forward(queries, keys, values, lengths)
    mixed_bf = mixed.reshape(group_rows, head_cols).astype(jnp.bfloat16)
    resid_local = x_local + lax.psum_scatter(
        jnp.dot(mixed_bf, out_bf, preferred_element_type=jnp.float32),
        "mp",
        scatter_dimension=0,
        tiled=True,
    )
    norm_two_local, unit_two, inverse_two = normalize(resid_local, gain_two)
    norm_two_bf = lax.all_gather(norm_two_local.astype(jnp.bfloat16), "mp", axis=0, tiled=True)
    gateup = jnp.dot(norm_two_bf, gateup_bf, preferred_element_type=jnp.float32)
    gate_val = gateup[:, :hidden_cols]
    up_val = gateup[:, hidden_cols:]
    sigmoid_gate = jax.nn.sigmoid(gate_val)
    silu_gate = gate_val * sigmoid_gate
    hidden_bf = (silu_gate * up_val).astype(jnp.bfloat16)
    result_local = resid_local + lax.psum_scatter(
        jnp.dot(hidden_bf, down_bf, preferred_element_type=jnp.float32),
        "mp",
        scatter_dimension=0,
        tiled=True,
    )
    output = result_local.astype(jnp.bfloat16)
    grad_local = (cotangent.astype(jnp.float32) * valid_local[:, None]).astype(jnp.bfloat16)
    grad_group = lax.all_gather(grad_local, "mp", axis=0, tiled=True)
    grad_down = dot_first(hidden_bf, grad_group)
    grad_hidden = dot_last(grad_group, down_bf)
    grad_gate = grad_hidden * up_val * sigmoid_gate * (1.0 + gate_val * (1.0 - sigmoid_gate))
    grad_up = grad_hidden * silu_gate
    grad_gateup_bf = jnp.concatenate([grad_gate, grad_up], axis=1).astype(jnp.bfloat16)
    grad_gateup = dot_first(norm_two_bf, grad_gateup_bf)
    grad_norm_two = lax.psum_scatter(
        dot_last(grad_gateup_bf, gateup_bf), "mp", scatter_dimension=0, tiled=True
    )
    grad_resid_local = grad_local.astype(jnp.float32) + norm_back(
        grad_norm_two, gain_two, unit_two, inverse_two
    )
    gain_two_grad = jnp.sum(grad_norm_two * unit_two, axis=0)
    grad_resid_bf = lax.all_gather(grad_resid_local.astype(jnp.bfloat16), "mp", axis=0, tiled=True)
    grad_out = dot_first(mixed_bf, grad_resid_bf)
    grad_mixed = dot_last(grad_resid_bf, out_bf).astype(jnp.bfloat16)
    grad_mixed = grad_mixed.reshape(slot_count, slot_len, heads_here, HEAD_DIM)
    query_grad, key_grad, value_grad = attend_backward(
        queries, keys, values, lengths, grad_mixed, log_totals
    )
    first_values_grad = (HALF * value_grad).reshape(group_rows, head_cols)
    grad_qkv_bf = jnp.stack(
        [unrotate(query_grad, cosine, sine), unrotate(key_grad, cosine, sine), HALF * value_grad],
        axis=2,
    )
    grad_qkv_bf = grad_qkv_bf.reshape(group_rows, 3 * head_cols).astype(jnp.bfloat16)
    grad_qkv = dot_first(norm_one_bf, grad_qkv_bf)
    unit_local = lax.dynamic_slice_in_dim(unit_one, row_start, local_rows, 0)
    inverse_local = lax.dynamic_slice_in_dim(inverse_one, row_start, local_rows, 0)
    grad_norm_one = lax.psum_scatter(
        dot_last(grad_qkv_bf, qkv_bf).astype(jnp.bfloat16), "mp", scatter_dimension=0, tiled=True
    ).astype(jnp.float32)
    input_grad = grad_resid_local + norm_back(grad_norm_one, gain_one, unit_local, inverse_local)
    gain_one_grad = jnp.sum(grad_norm_one * unit_local, axis=0)
    sum_qkv, sum_out, sum_gateup, sum_down = (
        lax.psum_scatter(
            grad_qkv.reshape(model, 3, head_cols), "dp", scatter_dimension=0, tiled=True
        ),
        lax.psum_scatter(grad_out, "dp", scatter_dimension=1, tiled=True),
        lax.psum_scatter(
            grad_gateup.reshape(model, 2, hidden_cols), "dp", scatter_dimension=0, tiled=True
        ),
        lax.psum_scatter(grad_down, "dp", scatter_dimension=1, tiled=True),
    )
    gain_sum = lax.psum(jnp.stack([gain_one_grad, gain_two_grad], axis=0), ("dp", "mp"))
    share = model // dp_count
    own_qkv = lax.dynamic_slice_in_dim(w_qkv, dp_index * share, share, 0)
    own_out = lax.dynamic_slice_in_dim(w_out, dp_index * share, share, 1)
    own_gateup = lax.dynamic_slice_in_dim(w_gateup, dp_index * share, share, 0)
    own_down = lax.dynamic_slice_in_dim(w_down, dp_index * share, share, 1)
    qkv_set = nesterov(sum_qkv / root_count, own_qkv, moment_qkv, average_qkv, RATE_QKV)
    out_set = nesterov(sum_out / root_count, own_out, moment_out, average_out, RATE_OUT)
    gateup_set = nesterov(
        sum_gateup / root_count, own_gateup, moment_gateup, average_gateup, RATE_GATEUP
    )
    down_set = nesterov(sum_down / root_count, own_down, moment_down, average_down, RATE_DOWN)
    gains_set = nesterov(gain_sum / root_count, gains, moment_gains, average_gains, RATE_GAINS)
    return (
        output,
        input_grad,
        first_values_grad,
        qkv_set[0],
        qkv_set[1],
        qkv_set[2],
        qkv_set[3],
        out_set[0],
        out_set[1],
        out_set[2],
        out_set[3],
        gateup_set[0],
        gateup_set[1],
        gateup_set[2],
        gateup_set[3],
        down_set[0],
        down_set[1],
        down_set[2],
        down_set[3],
        gains_set[0],
        gains_set[1],
        gains_set[2],
        gains_set[3],
    )


F32 = jnp.float32
BF16 = jnp.bfloat16
LANES = 128
BLK = 256
ROWS = 256
PARTS = 3
SWAP = ((0, 1), (1, 0))
VMEM_MIB = 60


def nt(left, right):
    return lax.dot_general(left, right, (((1,), (1,)), ((), ())), preferred_element_type=F32)


def nn(left, right):
    return lax.dot_general(left, right, (((1,), (0,)), ((), ())), preferred_element_type=F32)


def tn(left, right):
    return lax.dot_general(left, right, (((0,), (0,)), ((), ())), preferred_element_type=F32)


def lane_of(rows):
    return lax.broadcasted_iota(jnp.int32, (rows, LANES), 1)


def params(mib):
    return pltpu.CompilerParams(vmem_limit_bytes=mib * 2**20)


def cost(flops, moved, exps=0):
    return pl.CostEstimate(flops=int(flops), bytes_accessed=int(moved), transcendentals=int(exps))


def partner_lanes(pair):
    lane = lane_of(pair.shape[0])
    return jnp.where((lane % HEAD_DIM) < HEAD_DIM // 2, pltpu.roll(pair, LANES - 32, 1), pltpu.roll(pair, 32, 1))


def pair_tables(length):
    cosine, sine = rope_tables(length, HEAD_DIM)
    cosine, sine = cosine[:, 0, :], sine[:, 0, :]
    wide_cos = jnp.concatenate([cosine] * 4, axis=1)
    wide_sin = jnp.concatenate([-sine, sine, -sine, sine], axis=1)
    return wide_cos, wide_sin


def qkv_kernel(base_ref, x_ref, first_ref, gain_ref, w_ref, cos_ref, sin_ref, *refs):
    n_ref, q_ref, k_ref, v_ref = refs[-4:]
    x = x_ref[...].astype(F32)
    inverse = lax.rsqrt(jnp.mean(x * x, axis=-1, keepdims=True) + EPS)
    norm = ((x * inverse) * gain_ref[...]).astype(BF16)
    n_ref[...] = norm
    cosine, sine = cos_ref[...], sin_ref[...]
    for part, out in ((0, q_ref), (1, k_ref)):
        flat = nn(norm, w_ref[:, part * q_ref.shape[1] : (part + 1) * q_ref.shape[1]])
        for c in range(flat.shape[1] // LANES):
            pair = flat[:, c * LANES : (c + 1) * LANES]
            turned = (pair * cosine + partner_lanes(pair) * sine).astype(BF16)
            if part == 0:
                turned = turned * jnp.asarray(0.125, BF16)
            out[:, c * LANES : (c + 1) * LANES] = turned
    v_ref[...] = (HALF * nn(norm, w_ref[:, 2 * q_ref.shape[1] :]) + HALF * first_ref[...].astype(F32)).astype(BF16)


def project_qkv(base, x, first, gain, w, cosine, sine, before):
    rows, model = x.shape
    slot_len, cols = first.shape
    here = lambda i, b: (i, 0)
    there = lambda i, b: (b[0] + i, 0)
    outs = (
        jax.ShapeDtypeStruct((slot_len, model), BF16),
        *(jax.ShapeDtypeStruct((slot_len, cols), BF16) for _ in range(3)),
    )
    before = () if before is None else tuple(before)
    return pl.pallas_call(
        qkv_kernel,
        out_shape=outs,
        grid_spec=pltpu.PrefetchScalarGridSpec(
            num_scalar_prefetch=1,
            grid=(rows // ROWS,),
            in_specs=[
                pl.BlockSpec((ROWS, model), here),
                pl.BlockSpec((ROWS, cols), there),
                pl.BlockSpec((1, model), lambda i, b: (0, 0)),
                pl.BlockSpec((model, PARTS * cols), lambda i, b: (0, 0)),
                pl.BlockSpec((ROWS, LANES), there),
                pl.BlockSpec((ROWS, LANES), there),
                *(pl.BlockSpec(memory_space=pl.ANY) for _ in before),
            ],
            out_specs=[pl.BlockSpec((ROWS, o.shape[1]), there) for o in outs],
        ),
        input_output_aliases={7 + n: n for n in range(len(before))},
        compiler_params=params(VMEM_MIB),
        cost_estimate=cost(2 * rows * model * cols * 3, 10e6),
        name="project_qkv",
    )(base, x, first, gain, w, cosine, sine, *before)


SAFE_SCORE = 60.0


def spare(head):
    return HEAD_DIM * (1 - head)


def own_lanes(lane, head):
    return (lane // HEAD_DIM) == head


def length_bias(slot_len, length):
    row = lax.broadcasted_iota(jnp.int32, (slot_len, LANES), 0)
    return jnp.where(row < length, 0.0, NEG_BIG).astype(BF16)


def causal_bias(mask_ref, query_axis):
    query = lax.broadcasted_iota(jnp.int32, (BLK, BLK), query_axis)
    key = lax.broadcasted_iota(jnp.int32, (BLK, BLK), 1 - query_axis)
    mask_ref[...] = jnp.where(key <= query, 0.0, NEG_BIG)


def largest_square(pair, both):
    flat = pair.astype(F32)
    return jnp.max(nn((flat * flat).astype(BF16), both))


def attend_fwd_kernel(scalar_ref, q_ref, k_ref, v_ref, *refs):
    o_ref, lse_ref, send_ref, ka, va, mask_ref = refs[-6:]
    slot_len = k_ref.shape[0]
    lane = lane_of(slot_len)
    bias = length_bias(slot_len, scalar_ref[0])
    for head in (0, 1):
        mine = own_lanes(lane, head)
        extra = jnp.where(lane == spare(head), bias, jnp.zeros_like(bias))
        ka[head] = jnp.where(mine, k_ref[...], extra)
        va[head] = jnp.where(mine, v_ref[...], jnp.ones_like(bias))
    causal_bias(mask_ref, 0)
    side = lambda axis: lax.broadcasted_iota(jnp.int32, (LANES, LANES), axis) // HEAD_DIM
    both = jnp.where(side(0) == side(1), 1.0, 0.0).astype(BF16)
    reach = largest_square(q_ref[...], both) * largest_square(k_ref[...], both)

    def rows_of(shifted):
        low = lane_of(BLK) < HEAD_DIM
        for i in range(slot_len // BLK):
            queries, seen = pl.ds(i * BLK, BLK), pl.ds(0, (i + 1) * BLK)
            before = i * BLK
            q = q_ref[queries, :]
            outs, peaks = [], []
            for head in (0, 1):
                one = jnp.where(lane_of(BLK) == spare(head), 1.0, 0.0).astype(BF16)
                scores = nt(jnp.where(own_lanes(lane_of(BLK), head), q, one), ka[head, seen, :])
                last = scores[:, before:] + mask_ref[...]
                scores = last if i == 0 else jnp.concatenate([scores[:, :before], last], axis=1)
                if shifted:
                    peak = jnp.max(scores, axis=1, keepdims=True)
                    scores = scores - peak
                    peaks.append(peak)
                outs.append(nn(jnp.exp(scores).astype(BF16), va[head, seen, :]))
            total = pltpu.roll(jnp.where(low, outs[1], outs[0]), HEAD_DIM, 1)
            o_ref[queries, :] = (jnp.where(low, outs[0], outs[1]) / total).astype(BF16)
            shift = jnp.where(low, peaks[0], peaks[1]) if shifted else 0.0
            lse_ref[queries, :] = shift + jnp.log(total)

    small = reach < (0.9 * SAFE_SCORE) ** 2

    @pl.when(small)
    def _():
        rows_of(False)

    @pl.when(jnp.logical_not(small))
    def _():
        rows_of(True)

    half = send_ref.shape[0]
    send_ref[...] = o_ref[pl.ds(pl.multiple_of(scalar_ref[1] * half, half), half), :]


def attend_pairs(first, count, scalars, q, k, v, before):
    slot_len, cols = q.shape
    full = pl.BlockSpec((slot_len, LANES), lambda p, n: (0, first + p))
    before = () if before is None else tuple(before)
    both = pltpu.VMEM((2, slot_len, LANES), BF16)
    return pl.pallas_call(
        attend_fwd_kernel,
        out_shape=(
            jax.ShapeDtypeStruct((slot_len, cols), BF16),
            jax.ShapeDtypeStruct((slot_len, cols), F32),
            jax.ShapeDtypeStruct((slot_len // 2, count * LANES), BF16),
        ),
        grid_spec=pltpu.PrefetchScalarGridSpec(
            num_scalar_prefetch=1,
            grid=(count,),
            in_specs=[full] * 3 + [pl.BlockSpec(memory_space=pl.ANY) for _ in before],
            out_specs=[full, full, pl.BlockSpec((slot_len // 2, LANES), lambda p, n: (0, p))],
            scratch_shapes=[both, both, pltpu.VMEM((BLK, BLK), F32)],
        ),
        input_output_aliases={4 + n: n for n in range(len(before))},
        compiler_params=params(VMEM_MIB),
        cost_estimate=cost(count * 2 * 2 * slot_len * slot_len * 256, 3e6 * count),
        name="attend_pairs",
    )(scalars, q, k, v, *before)


def split3(x):
    high = x.astype(BF16)
    rest = x - high.astype(F32)
    mid = rest.astype(BF16)
    return high, mid, (rest - mid.astype(F32)).astype(BF16)


def attend_back_kernel(scalar_ref, q_ref, k_ref, v_ref, o_ref, lse_ref, mine_ref, theirs_ref, cos_ref, sin_ref, *refs):
    fv_ref, grad_ref, send_ref, ka, va, kz, do_ref, mask_ref, dk_ref, dv_ref = refs[-10:]
    slot_len = k_ref.shape[0]
    half = slot_len // 2
    far_rows = pl.ds(pl.multiple_of(scalar_ref[1] * half, half), half)
    do_ref[pl.ds(pl.multiple_of((1 - scalar_ref[1]) * half, half), half), :] = mine_ref[...]
    do_ref[far_rows, :] = theirs_ref[...]
    lane = lane_of(slot_len)
    bias = length_bias(slot_len, scalar_ref[0])
    zero, minus = jnp.zeros_like(bias), jnp.full_like(bias, -1.0)
    for head in (0, 1):
        mine, at = own_lanes(lane, head), spare(head)
        ones = jnp.where((lane > at) & (lane < at + 4), minus, zero)
        ka[head] = jnp.where(mine, k_ref[...], jnp.where(lane == at, bias, ones))
        va[head] = jnp.where(mine, v_ref[...], ones)
        kz[head] = jnp.where(mine, k_ref[...], zero)
    causal_bias(mask_ref, 1)
    lane = lane_of(BLK)
    low = lane < HEAD_DIM
    zero = jnp.zeros((BLK, LANES), BF16)

    def unturn(grad, rows):
        return grad * cos_ref[rows, :] - partner_lanes(grad) * sin_ref[rows, :]

    for i in range(slot_len // BLK):
        queries, seen = pl.ds(i * BLK, BLK), pl.ds(0, (i + 1) * BLK)
        before = i * BLK
        q, do = q_ref[queries, :], do_ref[queries, :]
        prod = do.astype(F32) * o_ref[queries, :].astype(F32)
        center_low = jnp.sum(jnp.where(low, prod, 0.0), axis=1, keepdims=True)
        center_high = jnp.sum(jnp.where(low, 0.0, prod), axis=1, keepdims=True)
        centers = split3(jnp.where(low, center_high, center_low))
        totals = split3(pltpu.roll(lse_ref[queries, :], HEAD_DIM, 1))
        dq = dk = dv = None
        for head in (0, 1):
            mine = own_lanes(lane, head)

            def place(block, items):
                out = zero
                for n, item in enumerate(items):
                    out = jnp.where(lane == spare(head) + n, item, out)
                return jnp.where(mine, block, out)

            s = nt(ka[head, seen, :], place(q, [jnp.ones_like(zero), *totals]))
            last = s[before:] + mask_ref[...]
            p = jnp.exp(last if i == 0 else jnp.concatenate([s[:before], last], axis=0))
            ds = (p * nt(va[head, seen, :], place(do, [zero, *centers]))).astype(BF16)
            term = nn(p.astype(BF16), jnp.where(mine, do, zero))
            dv = term if dv is None else dv + term
            term = nn(ds, jnp.where(mine, q, zero))
            dk = term if dk is None else dk + term
            term = tn(ds, kz[head, seen, :])
            dq = term if dq is None else dq + term
        if i > 0:
            dv_ref[pl.ds(0, before), :] += dv[:before]
            dk_ref[pl.ds(0, before), :] += dk[:before]
        dv_ref[queries, :] = dv[before:]
        dk_ref[queries, :] = dk[before:]
        grad_ref[queries, 0:LANES] = unturn(dq * 0.125, queries).astype(BF16)
    for i in range(slot_len // BLK):
        keys = pl.ds(i * BLK, BLK)
        half_dv = HALF * dv_ref[keys, :]
        fv_ref[keys, :] = half_dv
        grad_ref[keys, 2 * LANES : 3 * LANES] = half_dv.astype(BF16)
        grad_ref[keys, LANES : 2 * LANES] = unturn(dk_ref[keys, :], keys).astype(BF16)
    send_ref[...] = grad_ref[far_rows, :]


def attend_back_pairs(first, count, scalars, q, k, v, o, lse, mine, theirs, cosine, sine, before):
    slot_len, cols = q.shape
    full = pl.BlockSpec((slot_len, LANES), lambda p, n: (0, first + p))
    own = pl.BlockSpec((slot_len, LANES), lambda p, n: (0, 0))
    before = () if before is None else tuple(before)
    both = pltpu.VMEM((2, slot_len, LANES), BF16)
    acc = pltpu.VMEM((slot_len, LANES), F32)
    wide = PARTS * LANES
    return pl.pallas_call(
        attend_back_kernel,
        out_shape=(
            jax.ShapeDtypeStruct((slot_len, cols), F32),
            jax.ShapeDtypeStruct((slot_len, PARTS * cols), BF16),
            jax.ShapeDtypeStruct((slot_len // 2, count * wide), BF16),
        ),
        grid_spec=pltpu.PrefetchScalarGridSpec(
            num_scalar_prefetch=1,
            grid=(count,),
            in_specs=[full] * 5
            + [
                pl.BlockSpec((slot_len // 2, LANES), lambda p, n: (0, first + p)),
                pl.BlockSpec((slot_len // 2, LANES), lambda p, n: (0, p)),
                own,
                own,
            ]
            + [pl.BlockSpec(memory_space=pl.ANY) for _ in before],
            out_specs=[
                full,
                pl.BlockSpec((slot_len, wide), lambda p, n: (0, first + p)),
                pl.BlockSpec((slot_len // 2, wide), lambda p, n: (0, p)),
            ],
            scratch_shapes=[both, both, both, pltpu.VMEM((slot_len, LANES), BF16),
                            pltpu.VMEM((BLK, BLK), F32), acc, acc],
        ),
        input_output_aliases={10 + n: n for n in range(len(before))},
        compiler_params=params(VMEM_MIB),
        cost_estimate=cost(count * (40 if first > 1 else 10) * slot_len * slot_len * 256, 6e6 * count),
        name="attend_back_pairs",
    )(scalars, q, k, v, o, lse, mine, theirs, cosine, sine, *before)


def resid_kernel(base_ref, x_ref, gain_ref, w_own_ref, w_far_ref, own_ref, *refs):
    own = own_ref[...]
    far = jnp.concatenate([r[...] for r in refs[:-3]], axis=1)
    h_ref, n_ref, o_ref = refs[-3:]
    h = x_ref[...].astype(F32) + (nn(own, w_own_ref[...]) + nn(far, w_far_ref[...]))
    inverse = lax.rsqrt(jnp.mean(h * h, axis=-1, keepdims=True) + EPS)
    h_ref[...] = h.astype(BF16)
    n_ref[...] = ((h * inverse) * gain_ref[...]).astype(BF16)
    cols = own.shape[1]
    o_ref[:, :cols] = far
    o_ref[:, cols:] = own


def resid_rows(base, x, gain, w_own, w_far, own, far):
    rows, model = x.shape
    cols = w_own.shape[0]
    wide = pl.BlockSpec((ROWS, model), lambda i, b: (i, 0))
    fixed = pl.BlockSpec((cols, model), lambda i, b: (0, 0))
    return pl.pallas_call(
        resid_kernel,
        out_shape=(
            jax.ShapeDtypeStruct((rows, model), BF16),
            jax.ShapeDtypeStruct((rows, model), BF16),
            jax.ShapeDtypeStruct((rows, 2 * cols), BF16),
        ),
        grid_spec=pltpu.PrefetchScalarGridSpec(
            num_scalar_prefetch=1,
            grid=(rows // ROWS,),
            in_specs=[
                wide,
                pl.BlockSpec((1, model), lambda i, b: (0, 0)),
                fixed,
                fixed,
                pl.BlockSpec((ROWS, cols), lambda i, b: (b[0] + i, 0)),
                *(pl.BlockSpec((ROWS, f.shape[1]), lambda i, b: (i, 0)) for f in far),
            ],
            out_specs=[wide, wide, pl.BlockSpec((ROWS, 2 * cols), lambda i, b: (i, 0))],
        ),
        compiler_params=params(VMEM_MIB),
        cost_estimate=cost(2 * rows * model * cols * 2, 14e6),
        name="resid_rows",
    )(base, x, gain, w_own, w_far, own, *far)


def weave_kernel(q_ref, gu_ref, d_ref, out_ref):
    cols = q_ref.shape[2]
    for part in range(PARTS):
        out_ref[:, part * cols : (part + 1) * cols] = q_ref[part].astype(BF16)
    down = d_ref[...].T
    for run in range(gu_ref.shape[2] // LANES):
        lanes = slice(run * LANES, (run + 1) * LANES)
        for part, piece in enumerate((gu_ref[:, 0, lanes], gu_ref[:, 1, lanes], down[:, lanes])):
            spot = PARTS * cols + (3 * run + part) * LANES
            out_ref[:, spot : spot + LANES] = piece.astype(BF16)


def weave(w_qkv, w_gateup, w_down):
    parts, model, cols = w_qkv.shape
    sides, hidden = w_gateup.shape[1:]
    rows = 128
    wide = parts * cols + 3 * hidden
    return pl.pallas_call(
        weave_kernel,
        out_shape=jax.ShapeDtypeStruct((model, wide), BF16),
        grid=(model // rows,),
        in_specs=[
            pl.BlockSpec((parts, rows, cols), lambda i: (0, i, 0)),
            pl.BlockSpec((rows, sides, hidden), lambda i: (i, 0, 0)),
            pl.BlockSpec((hidden, rows), lambda i: (0, i)),
        ],
        out_specs=pl.BlockSpec((rows, wide), lambda i: (i, 0)),
        compiler_params=params(VMEM_MIB),
        cost_estimate=cost(0, 6 * model * wide),
        name="weave",
    )(w_qkv, w_gateup, w_down)


def halve_rows(grad, core, x, keep, send):
    rows = grad.shape[0] // 16
    block = lambda z, i, c: grad[(z * 4 + i * 2 + c) * rows : (z * 4 + i * 2 + c + 1) * rows]
    for i in (0, 1):
        for z in range(4):
            spot = pl.ds((i * 4 + z) * rows, rows)
            same = [jnp.where(x == 0, block(z, i, c), block(z, 1 - i, c)) for c in (0, 1)]
            keep[spot, :] = jnp.where(core == 0, same[0], same[1])
            send[spot, :] = jnp.where(core == 0, same[1], same[0])


def runs(block, count, of, which):
    return jnp.concatenate(
        [block[:, (of * i + which) * LANES : (of * i + which + 1) * LANES] for i in range(count)], axis=1
    )


def swiglu_kernel(halved, place_ref, n_ref, dy_ref, w_ref, y_ref, dn_ref, *refs):
    y_acc, dn_acc = refs[-2:]
    step = pl.program_id(0)
    last = pl.num_programs(0) - 1

    def work(count, first):
        n = n_ref[...]
        dy = dy_ref[...]
        run = lambda i: w_ref[:, i * LANES : (i + 1) * LANES]
        wgu = jnp.concatenate([run(3 * i + j) for i in range(count) for j in (0, 1)], axis=1)
        wd = jnp.concatenate([run(3 * i + 2) for i in range(count)], axis=1)
        both = nn(n, wgu)
        gate, up = runs(both, count, 2, 0), runs(both, count, 2, 1)
        sig = jax.nn.sigmoid(gate)
        silu = gate * sig
        hid = (silu * up).astype(BF16)
        dhid = nn(dy, wd)
        dgate = (dhid * up * sig * (1.0 + gate * (1.0 - sig))).astype(BF16)
        dup = (dhid * silu).astype(BF16)
        dgu = jnp.concatenate(
            [d[:, i * LANES : (i + 1) * LANES] for i in range(count) for d in (dgate, dup)], axis=1
        )
        y = nt(hid, wd)
        dn = nt(dgu, wgu)
        if first:
            y_acc[...] = y
            dn_acc[...] = dn
        else:
            y_acc[...] += y
            dn_acc[...] += dn
        grad_gu = tn(n, dgu).astype(BF16)
        grad_d = tn(dy, hid).astype(BF16)
        for i in range(count):
            for part, grad in enumerate((grad_gu[:, 2 * i * LANES : (2 * i + 2) * LANES],
                                         grad_d[:, i * LANES : (i + 1) * LANES])):
                start = (3 * i + 2 * part) * LANES
                spot = slice(start, start + grad.shape[1])
                if halved:
                    halve_rows(grad, place_ref[0], place_ref[1], refs[0].at[:, spot], refs[1].at[:, spot])
                else:
                    refs[0][:, spot] = grad

    @pl.when(step == 0)
    def _():
        work(2, True)

    @pl.when((step > 0) & (step < last))
    def _():
        work(2, False)

    @pl.when(step == last)
    def _():
        work(1, False)
        y_ref[...] = y_acc[...].astype(BF16)
        dn_ref[...] = dn_acc[...].astype(BF16)


def swiglu_half(place, n, dy, w, first, width=None):
    rows, model = n.shape
    tile = 256
    skip = first // (3 * tile)
    hidden = (w.shape[1] - first) // 3
    held = pl.BlockSpec((rows, model), lambda t, p: (0, 0))
    cols = pl.BlockSpec((model, 3 * tile), lambda t, p: (0, t))
    source = pl.BlockSpec((model, 3 * tile), lambda t, p: (0, skip + t))
    half = pl.BlockSpec((model // 2, 3 * tile), lambda t, p: (0, t))
    grads = [(model, 3 * hidden)] if width is None else [(model // 2, width)] * 2
    return pl.pallas_call(
        functools.partial(swiglu_kernel, width is not None),
        out_shape=(
            *(jax.ShapeDtypeStruct((rows, model), BF16) for _ in range(2)),
            *(jax.ShapeDtypeStruct(g, BF16) for g in grads),
        ),
        grid_spec=pltpu.PrefetchScalarGridSpec(
            num_scalar_prefetch=1,
            grid=(-(-hidden // tile),),
            in_specs=[held, held, source],
            out_specs=[held, held] + ([cols] if width is None else [half, half]),
            scratch_shapes=[pltpu.VMEM((rows, model), F32)] * 2,
        ),
        compiler_params=params(VMEM_MIB),
        cost_estimate=cost(9 * 2 * rows * model * hidden, 36e6, rows * hidden),
        name="swiglu_half",
    )(place, n, dy, w)


def grad_out_kernel(place_ref, dhb_ref, o_ref, keep_ref, send_ref):
    grad = tn(dhb_ref[...], o_ref[...]).astype(BF16)
    halve_rows(grad, place_ref[0], place_ref[1], keep_ref, send_ref)


def grad_out_of(place, dhb, o_cat):
    rows, model = dhb.shape
    tile = 512
    out = pl.BlockSpec((model // 2, tile), lambda t, p: (0, t))
    return pl.pallas_call(
        grad_out_kernel,
        out_shape=[jax.ShapeDtypeStruct((model // 2, o_cat.shape[1]), BF16)] * 2,
        grid_spec=pltpu.PrefetchScalarGridSpec(
            num_scalar_prefetch=1,
            grid=(o_cat.shape[1] // tile,),
            in_specs=[
                pl.BlockSpec((rows, model), lambda t, p: (0, 0)),
                pl.BlockSpec((rows, tile), lambda t, p: (0, t)),
            ],
            out_specs=[out, out],
        ),
        compiler_params=params(VMEM_MIB),
        cost_estimate=cost(2 * rows * model * o_cat.shape[1], 7e6),
        name="grad_out",
    )(place, dhb, o_cat)


def grad_qkv_kernel(place_ref, n_ref, dqkv_ref, *refs):
    keep_ref, send_ref, t_ref = refs[-3:]
    grad = tn(n_ref[...], dqkv_ref[...])
    term = None
    for i in range(grad.shape[1] // LANES):
        weight = refs[i % PARTS][:, (i // PARTS) * LANES : (i // PARTS + 1) * LANES]
        piece = grad[:, i * LANES : (i + 1) * LANES] * weight.astype(F32)
        term = piece if term is None else term + piece
    t_ref[...] = term
    halve_rows(grad.astype(BF16), place_ref[0], place_ref[1], keep_ref, send_ref)


def grad_qkv_of(first, place, norm, dqkv, w, into):
    slot_len, model = norm.shape
    pairs = 2
    tile = pairs * PARTS * LANES
    steps = dqkv.shape[1] // tile
    at = first // pairs
    out = pl.BlockSpec((model // 2, tile), lambda t, p: (0, 0))
    into = () if into is None else tuple(into)
    width = into[0].shape[1] if into else tile
    return pl.pallas_call(
        grad_qkv_kernel,
        out_shape=(
            *(jax.ShapeDtypeStruct((model // 2, width), BF16) for _ in range(2)),
            jax.ShapeDtypeStruct((model, LANES), F32),
        ),
        grid_spec=pltpu.PrefetchScalarGridSpec(
            num_scalar_prefetch=1,
            grid=(1,),
            in_specs=[
                pl.BlockSpec((slot_len, model), lambda t, p: (0, 0)),
                pl.BlockSpec((slot_len, tile), lambda t, p: (0, at)),
                *(
                    pl.BlockSpec((model, pairs * LANES), lambda t, p, part=part: (0, part * steps + at))
                    for part in range(PARTS)
                ),
                *(pl.BlockSpec(memory_space=pl.ANY) for _ in into),
            ],
            out_specs=[out, out, pl.BlockSpec((model, LANES), lambda t, p: (0, 0))],
        ),
        input_output_aliases={6 + n: n for n in range(len(into))},
        compiler_params=params(VMEM_MIB),
        cost_estimate=cost(2 * slot_len * model * tile, 14e6),
        name="grad_qkv",
    )(place, norm, dqkv, *[w] * PARTS, *into)


def after_kernel(h_ref, y1_ref, y2_ref, d1_ref, d2_ref, dy_ref, gain_ref, w_own_ref, w_far_ref,
                 out_ref, dhb_ref, own_ref, far_ref, t_ref):
    h = h_ref[...].astype(F32)
    out_ref[...] = (h + (y1_ref[...].astype(F32) + y2_ref[...].astype(F32))).astype(BF16)
    inverse = lax.rsqrt(jnp.mean(h * h, axis=-1, keepdims=True) + EPS)
    unit = h * inverse
    dn = d1_ref[...].astype(F32) + d2_ref[...].astype(F32)
    e = dn * gain_ref[...]
    dh = dy_ref[...].astype(F32) + inverse * (e - unit * jnp.mean(e * unit, axis=-1, keepdims=True))
    dhb = dh.astype(BF16)
    dhb_ref[...] = dhb
    own_ref[...] = nt(dhb, w_own_ref[...]).astype(BF16)
    far_ref[...] = nt(dhb, w_far_ref[...]).astype(BF16)

    @pl.when(pl.program_id(0) == 0)
    def _():
        t_ref[...] = jnp.zeros_like(t_ref)

    t_ref[...] += jnp.sum(dn * unit, axis=0, keepdims=True)


def after_rows(h, y1, y2, d1, d2, dy, gain, w_own, w_far):
    rows, model = h.shape
    cols = w_own.shape[0]
    wide = pl.BlockSpec((ROWS, model), lambda i: (i, 0))
    fixed = pl.BlockSpec((cols, model), lambda i: (0, 0))
    slim = pl.BlockSpec((ROWS, cols), lambda i: (i, 0))
    one = pl.BlockSpec((1, model), lambda i: (0, 0))
    return pl.pallas_call(
        after_kernel,
        out_shape=(
            jax.ShapeDtypeStruct((rows, model), BF16),
            jax.ShapeDtypeStruct((rows, model), BF16),
            jax.ShapeDtypeStruct((rows, cols), BF16),
            jax.ShapeDtypeStruct((rows, cols), BF16),
            jax.ShapeDtypeStruct((1, model), F32),
        ),
        grid=(rows // ROWS,),
        in_specs=[wide] * 6 + [one, fixed, fixed],
        out_specs=[wide, wide, slim, slim, one],
        compiler_params=params(VMEM_MIB),
        cost_estimate=cost(2 * rows * model * cols * 2, 36e6),
        name="after_rows",
    )(h, y1, y2, d1, d2, dy, gain, w_own, w_far)


def input_kernel(base_ref, x_ref, dh_ref, gain_ref, w_own_ref, w_far_ref, *refs):
    out_ref = refs[-1]
    dn = None
    for weights, grads in ((w_own_ref, refs[:1]), (w_far_ref, refs[1:-1])):
        flat = jnp.concatenate([g[...] for g in grads], axis=1)
        count = flat.shape[1] // (PARTS * LANES)
        lanes = jnp.concatenate([runs(flat, count, PARTS, part) for part in range(PARTS)], axis=1)
        term = nt(lanes, weights[...])
        dn = term if dn is None else dn + term
    x = x_ref[...].astype(F32)
    inverse = lax.rsqrt(jnp.mean(x * x, axis=-1, keepdims=True) + EPS)
    unit = x * inverse
    e = dn * gain_ref[...]
    out_ref[...] = dh_ref[...].astype(F32) + inverse * (e - unit * jnp.mean(e * unit, axis=-1, keepdims=True))


def input_rows(base, x, dh, gain, w_own, w_far, own, far):
    rows, model = x.shape
    cols = own.shape[1] // PARTS
    wide = pl.BlockSpec((ROWS, model), lambda i, b: (i, 0))
    fixed = pl.BlockSpec((model, PARTS * cols), lambda i, b: (0, 0))
    return pl.pallas_call(
        input_kernel,
        out_shape=jax.ShapeDtypeStruct((rows, model), F32),
        grid_spec=pltpu.PrefetchScalarGridSpec(
            num_scalar_prefetch=1,
            grid=(rows // ROWS,),
            in_specs=[wide, wide, pl.BlockSpec((1, model), lambda i, b: (0, 0)), fixed, fixed]
            + [pl.BlockSpec((ROWS, own.shape[1]), lambda i, b: (b[0] + i, 0))]
            + [pl.BlockSpec((ROWS, f.shape[1]), lambda i, b: (i, 0)) for f in far],
            out_specs=wide,
        ),
        compiler_params=params(VMEM_MIB),
        cost_estimate=cost(8 * rows * model * cols * 6, 20e6),
        name="input_rows",
    )(base, x, dh, gain, w_own, w_far, own, *far)


def step_of(sum_grad, weight, moment, average, rate, root_count):
    return nesterov(sum_grad / root_count, weight, moment, average, rate)


def own_columns(place, wide):
    turned = wide.T
    half = turned.shape[0] // 2
    return jnp.where(place == 0, turned[:half], turned[half:])


def step_mlp_kernel(root_count, place_ref, sum_ref, got_ref, wgu_ref, mgu_ref, agu_ref, wd_ref, md_ref, ad_ref, *outs):
    total = sum_ref[...].astype(F32) + got_ref[:, : sum_ref.shape[1]].astype(F32)
    count = total.shape[1] // (3 * LANES)
    for side in (0, 1):
        grads = step_of(runs(total, count, 3, side), wgu_ref[:, side, :], mgu_ref[:, side, :],
                        agu_ref[:, side, :], RATE_GATEUP, root_count)
        for out, value in zip(outs[:4], grads):
            out[:, side, :] = value
    weight = own_columns(place_ref[1], wd_ref[...])
    grads = step_of(runs(total, count, 3, 2), weight, md_ref[...], ad_ref[...], RATE_DOWN, root_count)
    for out, value in zip(outs[4:], grads):
        out[...] = value


def step_mlp(dp_index, root_count, total, got, w_gateup, m_gu, a_gu, w_down, m_d, a_d):
    place = jnp.stack([dp_index, dp_index % 2, dp_index // 2]).astype(jnp.int32)
    share, sides, hidden = m_gu.shape
    cols = total.shape[1]
    gu = pl.BlockSpec((share, sides, hidden), lambda i, p: (0, 0, 0))
    d = pl.BlockSpec((share, hidden), lambda i, p: (0, 0))
    return pl.pallas_call(
        functools.partial(step_mlp_kernel, root_count),
        out_shape=(
            *(jax.ShapeDtypeStruct(m_gu.shape, F32) for _ in range(4)),
            *(jax.ShapeDtypeStruct((share, hidden), F32) for _ in range(4)),
        ),
        grid_spec=pltpu.PrefetchScalarGridSpec(
            num_scalar_prefetch=1,
            grid=(1,),
            in_specs=[
                pl.BlockSpec((share, cols), lambda i, p: (0, 0)),
                pl.BlockSpec(got.shape, lambda i, p: (0, 0)),
                pl.BlockSpec((share, sides, hidden), lambda i, p: (p[0], 0, 0)),
                gu,
                gu,
                pl.BlockSpec((hidden, LANES), lambda i, p: (0, p[2])),
                d,
                d,
            ],
            out_specs=[gu] * 4 + [d] * 4,
        ),
        compiler_params=params(VMEM_MIB),
        cost_estimate=cost(0, 14e6),
        name="step_mlp",
    )(place, total, got, w_gateup, m_gu, a_gu, w_down, m_d, a_d)


def step_attention_kernel(root_count, place_ref, mix_ref, last_ref, got_ref, wq_ref, mq_ref, aq_ref, wo_ref, mo_ref, ao_ref, *outs):
    cols = ao_ref.shape[1]
    early = mix_ref.shape[1] - 2 * cols
    total = jnp.concatenate([mix_ref[:, :early], last_ref[...]], axis=1)
    count = total.shape[1] // (PARTS * LANES)
    for part in range(PARTS):
        grads = step_of(runs(total, count, PARTS, part), wq_ref[part], mq_ref[part], aq_ref[part],
                        RATE_QKV, root_count)
        for out, value in zip(outs[:4], grads):
            out[part] = value
    weight = own_columns(place_ref[1], wo_ref[...])
    grads = step_of(mix_ref[:, early + cols :] + got_ref[...].astype(F32), weight, mo_ref[...],
                    ao_ref[...], RATE_OUT, root_count)
    for out, value in zip(outs[4:], grads):
        out[...] = value


def step_attention(dp_index, root_count, mix, last, got, w_qkv, m_q, a_q, w_out, m_o, a_o):
    place = jnp.stack([dp_index, dp_index % 2, dp_index // 2]).astype(jnp.int32)
    parts, share, cols = m_q.shape
    q = pl.BlockSpec((parts, share, cols), lambda i, p: (0, 0, 0))
    o = pl.BlockSpec((share, cols), lambda i, p: (0, 0))
    return pl.pallas_call(
        functools.partial(step_attention_kernel, root_count),
        out_shape=(
            *(jax.ShapeDtypeStruct(m_q.shape, F32) for _ in range(4)),
            *(jax.ShapeDtypeStruct((share, cols), F32) for _ in range(4)),
        ),
        grid_spec=pltpu.PrefetchScalarGridSpec(
            num_scalar_prefetch=1,
            grid=(1,),
            in_specs=[
                pl.BlockSpec(mix.shape, lambda i, p: (0, 0)),
                pl.BlockSpec(last.shape, lambda i, p: (0, 0)),
                o,
                pl.BlockSpec((parts, share, cols), lambda i, p: (0, p[0], 0)),
                q,
                q,
                pl.BlockSpec((cols, LANES), lambda i, p: (0, p[2])),
                o,
                o,
            ],
            out_specs=[q] * 4 + [o] * 4,
        ),
        compiler_params=params(VMEM_MIB),
        cost_estimate=cost(0, 6e6),
        name="step_attention",
    )(place, mix, last, got, w_qkv, m_q, a_q, w_out, m_o, a_o)


def dp_pairs(move):
    return tuple((i, move(i)) for i in range(16))


CORE = dp_pairs(lambda i: i ^ 1)
CROSS = dp_pairs(lambda i: i ^ 2)
Z_LINES = tuple(tuple(z * 4 + i for z in range(4)) for i in range(4))
NEAR = tuple(
    tuple((i, i ^ flip) for i in range(32)) for flip in (1, 2, 3)
)
ALONG = tuple(dp_pairs(lambda i, step=step: (i + 4 * step) % 16) for step in (1, 2, 3))


def move(x, pairs):
    return lax.ppermute(x, "dp", pairs)


def add(left, right):
    return left.astype(F32) + right.astype(F32)


def after_core(keep, got):
    half = keep.shape[0] // 2
    here = add(keep[:half], got[:half]).astype(BF16)
    away = add(keep[half:], got[half:]).astype(BF16)
    return here, away


def after_cross(here, got, z):
    total = add(here, got)
    rows = here.shape[0] // 4
    block = lambda step: lax.dynamic_slice_in_dim(total, lax.rem(z + step, 4) * rows, rows, 0)
    return block(0), tuple(block(step).astype(BF16) for step in (1, 2, 3))


def after_along(mine, got):
    for piece in got:
        mine = mine + piece.astype(F32)
    return mine


def tie(values, *others):
    return lax.optimization_barrier((values, others))[0]


def shards_pair(
    tokens,
    first_values,
    lengths,
    cotangent,
    w_qkv,
    w_out,
    w_gateup,
    w_down,
    gains,
    moment_qkv,
    moment_out,
    moment_gateup,
    moment_down,
    moment_gains,
    average_qkv,
    average_out,
    average_gateup,
    average_down,
    average_gains,
):
    rows, model = tokens.shape
    mp_index = lax.axis_index("mp")
    dp_index = lax.axis_index("dp")
    dp_count = lax.axis_size("dp")
    z, core = dp_index // 4, dp_index % 2
    place = jnp.stack([core, (dp_index // 2) % 2]).astype(jnp.int32)
    slot_len = 2 * rows
    head_cols = w_qkv.shape[2]
    hidden = w_gateup.shape[2]
    pairs = head_cols // LANES
    root_count = math.sqrt(slot_len * dp_count)
    row_start = mp_index * rows
    far_start = (1 - mp_index) * rows
    gain_one, gain_two = gains[0:1], gains[1:2]

    def swap(x):
        return lax.ppermute(x, "mp", SWAP)

    def chunk(x):
        part = x.shape[0] // dp_count
        return lax.dynamic_slice_in_dim(x, dp_index * part, part, 0)

    def gather(x):
        return lax.all_gather(x, "dp", axis=0, tiled=True)

    far_tokens = swap(tokens)
    out_bf = w_out.astype(BF16)
    woven = weave(w_qkv.transpose(1, 0, 2), w_gateup, w_down)
    cosine, sine = pair_tables(slot_len)
    block_of = lambda start: (start // ROWS).astype(jnp.int32)
    base, far_base = block_of(row_start).reshape(1), block_of(far_start).reshape(1)
    own_part = project_qkv(base, tokens, first_values, gain_one, woven, cosine, sine, None)
    place_row = row_start + jnp.arange(rows, dtype=jnp.int32)
    dy = jnp.where((place_row < lengths[0])[:, None], cotangent, jnp.zeros_like(cotangent))
    far_tokens, own_part, woven, dy, out_bf = lax.optimization_barrier(
        (far_tokens, own_part, woven, dy, out_bf)
    )
    woven_chunk = swap(chunk(woven))
    norm_one, q, k, v = project_qkv(
        far_base, far_tokens, first_values, gain_one, woven, cosine, sine, own_part
    )
    q, woven_chunk = lax.optimization_barrier((q, woven_chunk))
    woven_far = gather(woven_chunk)
    out_far = swap(tie(out_bf, woven_chunk))

    scalars = jnp.concatenate([lengths, (1 - mp_index).reshape(1).astype(jnp.int32)])
    early = pairs - 1
    o_all, lse_all, away = attend_pairs(0, early, scalars, q, k, v, None)
    o_far = [swap(away)]
    o_all, lse_all, away = attend_pairs(early, pairs - early, scalars, q, k, v, (o_all, lse_all))
    o_far.append(swap(away))
    h, norm_two, o_cat = resid_rows(base, tokens, gain_two, out_bf, out_far, o_all, o_far)

    y_own, dn_own, grads_own = swiglu_half(place, norm_two, dy, woven, PARTS * head_cols)
    sum_own = lax.psum_scatter(grads_own, "dp", scatter_dimension=0, tiled=True)
    norm_two, woven_far = tie((norm_two, woven_far), y_own)
    y_far, dn_far, keep_far, send_far = swiglu_half(
        place, norm_two, dy, woven_far, PARTS * head_cols, 3 * hidden
    )
    got_far = move(send_far, CORE)
    output, dhb, do_own, do_far, gain_two_part = after_rows(
        h, y_own, y_far, dn_own, dn_far, dy, gain_two, out_bf, out_far
    )
    theirs = [swap(do_far[:, :LANES])]
    theirs.append(swap(tie(do_far, theirs[0])[:, LANES:]))
    keep_out, send_out = grad_out_of(place, dhb, o_cat)
    here_far, away_far = after_core(keep_far, tie(got_far, keep_out))
    got_far = move(away_far, CROSS)
    got_out = move(send_out, CORE)

    dqkv_far = []

    def back(first, count, theirs, before):
        first_grad, dqkv, away = attend_back_pairs(
            first, count, scalars, q, k, v, o_all, lse_all, do_own, theirs, cosine, sine, before
        )
        dqkv_far.append(swap(away))
        return first_grad, dqkv

    done = back(0, 1, tie(theirs[0], keep_out, away_far), None)
    here_out, away_out = after_core(keep_out, tie(got_out, done))
    got_out = move(away_out, CROSS)
    done = back(1, pairs - 2, tie(theirs[1], away_out), done)
    done, dqkv_far[0] = lax.optimization_barrier((done, dqkv_far[0]))
    keep_two, send_two, gain_first = grad_qkv_of(0, place, norm_one, done[1], woven, None)
    got_two = move(send_two, CORE)
    total_far = add(here_far, tie(got_far, keep_two)).astype(BF16)
    total_far, sum_own = lax.optimization_barrier((total_far, sum_own))
    sum_far = lax.psum_scatter(
        total_far, "dp", scatter_dimension=0, tiled=True, axis_index_groups=Z_LINES
    )
    done = back(pairs - 1, 1, tie(theirs[1], total_far)[:, (pairs - 2) * LANES :], done)

    (first_grad, dqkv), got_two, got_out = lax.optimization_barrier((done, got_two, got_out))
    here_two, away_two = after_core(keep_two, got_two)
    got_two = move(away_two, CROSS)
    keep_qkv, send_qkv, gain_last = grad_qkv_of(
        2, place, norm_one, tie(dqkv, away_two), woven, None
    )
    got_qkv = move(send_qkv, CORE)
    gain_one_part = jnp.sum(gain_first + gain_last, axis=1) / gains[0]
    parts = jnp.stack([gain_one_part, gain_two_part[0]], axis=0)
    near = move(parts, CORE)
    got_qkv, near, got_two, dqkv_far[1] = lax.optimization_barrier(
        (got_qkv, near, got_two, dqkv_far[1])
    )
    here_qkv, away_qkv = after_core(keep_qkv, got_qkv)
    got_qkv = move(away_qkv, CROSS)
    parts = parts + near
    cross = move(parts, CROSS)
    mine_mix, blocks_mix = after_cross(
        jnp.concatenate([here_two, here_out], axis=1), jnp.concatenate([got_two, got_out], axis=1), z
    )
    got_mix = tuple(move(b, p) for b, p in zip(blocks_mix, ALONG))
    got_far = swap(tie(sum_far, blocks_mix))
    input_grad = input_rows(
        base, tokens, tie(dhb, away_qkv, parts, blocks_mix, sum_far), gain_one, woven, woven_far, dqkv, dqkv_far
    )
    got_qkv, cross, got_far, got_mix = tie((got_qkv, cross, got_far, got_mix), input_grad)
    mine_qkv, blocks_qkv = after_cross(here_qkv, got_qkv, z)
    got_qkv = tuple(move(b, p) for b, p in zip(blocks_qkv, ALONG))
    sum_mix = after_along(mine_mix, got_mix)
    early = keep_two.shape[1]
    got_out = swap(sum_mix[:, early : early + head_cols].astype(BF16))
    parts = parts + cross
    along = [move(parts, p) for p in ALONG]
    got_far = tie(got_far, blocks_qkv)

    gateup_down = step_mlp(
        dp_index, root_count, tie(sum_own, blocks_qkv, parts), got_far, w_gateup,
        moment_gateup, average_gateup, w_down, moment_down.T, average_down.T,
    )
    got_qkv, along, got_out = tie((got_qkv, along, got_out), gateup_down[0])
    parts = after_along(parts, along)
    gain_sum = parts + swap(parts)
    sum_qkv = after_along(mine_qkv, got_qkv)
    turn = lambda x: x.transpose(1, 0, 2)
    qkv_out = step_attention(
        dp_index, root_count, sum_mix, sum_qkv, got_out,
        turn(w_qkv), turn(moment_qkv), turn(average_qkv), w_out, moment_out.T, average_out.T,
    )
    gains_set = nesterov(gain_sum / root_count, gains, moment_gains, average_gains, RATE_GAINS)
    return (
        output,
        input_grad,
        first_grad,
        *(turn(x) for x in qkv_out[:4]),
        *(x.T for x in qkv_out[4:]),
        *gateup_down[:4],
        *(x.T for x in gateup_down[4:]),
        *gains_set,
    )


def solution(mesh):
    placed = (
        P(("dp", "mp"), None),
        P("dp", "mp"),
        P("dp"),
        P(("dp", "mp"), None),
        P(None, None, "mp"),
        P("mp", None),
        P(None, None, "mp"),
        P("mp", None),
        P(),
        P("dp", None, "mp"),
        P("mp", "dp"),
        P("dp", None, "mp"),
        P("mp", "dp"),
        P(),
        P("dp", None, "mp"),
        P("mp", "dp"),
        P("dp", None, "mp"),
        P("mp", "dp"),
        P(),
    )
    return jax.shard_map(
        shards_pair if (mesh.shape["dp"], mesh.shape["mp"]) == (16, 2) else shards_any,
        mesh=mesh,
        in_specs=placed,
        out_specs=(
            P(("dp", "mp"), None),
            P(("dp", "mp"), None),
            P("dp", "mp"),
            P("dp", None, "mp"),
            P("dp", None, "mp"),
            P("dp", None, "mp"),
            P("dp", None, "mp"),
            P("mp", "dp"),
            P("mp", "dp"),
            P("mp", "dp"),
            P("mp", "dp"),
            P("dp", None, "mp"),
            P("dp", None, "mp"),
            P("dp", None, "mp"),
            P("dp", None, "mp"),
            P("mp", "dp"),
            P("mp", "dp"),
            P("mp", "dp"),
            P("mp", "dp"),
            P(),
            P(),
            P(),
            P(),
        ),
        check_vma=False,
    )
```

```python
import functools
import math

import jax
import jax.numpy as jnp
from jax import lax
from jax.experimental import pallas as pl
from jax.experimental.pallas import tpu as pltpu
from jax.sharding import PartitionSpec as P

HEAD_DIM = 64


EPS = 1e-06
NEG_BIG = -1e30
HALF = 0.5
MOMENTUM = 0.5
AVERAGE_DECAY = 0.5
RATE_QKV = 0.05
RATE_OUT = 20.0
RATE_GATEUP = 0.12
RATE_DOWN = 0.04
RATE_GAINS = 0.6


def normalize(values, gain):
    inverse = lax.rsqrt(jnp.mean(values * values, axis=-1, keepdims=True) + EPS)
    unit = values * inverse
    return (unit * gain, unit, inverse)


def norm_back(grad_norm, gain, unit, inverse):
    scaled = grad_norm * gain
    return inverse * (scaled - unit * jnp.mean(scaled * unit, axis=-1, keepdims=True))


def rope_tables(length, head_size):
    half_size = head_size // 2
    freqs = jnp.power(10000.0, -2.0 * jnp.arange(half_size, dtype=jnp.float32) / head_size)
    angles = jnp.arange(length, dtype=jnp.float32)[:, None] * freqs[None, :]
    return (jnp.cos(angles)[:, None, :], jnp.sin(angles)[:, None, :])


def rotate(values, cosine, sine):
    half_size = values.shape[-1] // 2
    first_half = values[..., :half_size]
    second_half = values[..., half_size:]
    return jnp.concatenate(
        [first_half * cosine - second_half * sine, second_half * cosine + first_half * sine],
        axis=-1,
    )


def unrotate(grads, cosine, sine):
    half_size = grads.shape[-1] // 2
    first_half = grads[..., :half_size]
    second_half = grads[..., half_size:]
    return jnp.concatenate(
        [first_half * cosine + second_half * sine, second_half * cosine - first_half * sine],
        axis=-1,
    )


def dot_last(left, right):
    return lax.dot_general(
        left, right, (((1,), (1,)), ((), ())), preferred_element_type=jnp.float32
    )


def dot_first(left, right):
    return lax.dot_general(
        left, right, (((0,), (0,)), ((), ())), preferred_element_type=jnp.float32
    )


def block_scores(query_block, keys, start, length, scale):
    block_len = query_block.shape[0]
    key_len = keys.shape[0]
    scores = (
        jnp.einsum("qhd,khd->hqk", query_block, keys, preferred_element_type=jnp.float32) * scale
    )
    query_pos = start + jnp.arange(block_len, dtype=jnp.int32)
    key_pos = jnp.arange(key_len, dtype=jnp.int32)
    allowed = (key_pos[None, :] <= query_pos[:, None]) & (key_pos[None, :] < length)
    return jnp.where(allowed[None], scores, NEG_BIG)


def attend_forward(queries, keys, values, lengths):
    slot_count, slot_len, heads_here, head_size = queries.shape
    block_len = min(512, slot_len)
    blocks = slot_len // block_len
    scale = 1.0 / math.sqrt(head_size)
    starts = jnp.arange(blocks, dtype=jnp.int32) * block_len

    def per_slot(item):
        slot_queries, slot_keys, slot_values, length = item

        def per_block(inner):
            query_block, start = inner
            scores = block_scores(query_block, slot_keys, start, length, scale)
            peak = jnp.max(scores, axis=-1, keepdims=True)
            raw_weights = jnp.exp(scores - peak)
            total = jnp.sum(raw_weights, axis=-1, keepdims=True)
            probs = raw_weights / total
            mixed = jnp.einsum(
                "hqk,khd->qhd",
                probs.astype(jnp.bfloat16),
                slot_values,
                preferred_element_type=jnp.float32,
            )
            return (mixed, (peak + jnp.log(total))[..., 0])

        mixed, log_totals = lax.map(
            per_block, (slot_queries.reshape(blocks, block_len, heads_here, head_size), starts)
        )
        return (mixed.reshape(slot_len, heads_here, head_size), log_totals)

    return lax.map(per_slot, (queries, keys, values, lengths))


def attend_backward(queries, keys, values, lengths, grad_mixed, log_totals):
    slot_count, slot_len, heads_here, head_size = queries.shape
    block_len = min(512, slot_len)
    blocks = slot_len // block_len
    scale = 1.0 / math.sqrt(head_size)
    starts = jnp.arange(blocks, dtype=jnp.int32) * block_len

    def per_slot(item):
        slot_queries, slot_keys, slot_values, length, slot_grads, slot_totals = item

        def per_block(carry, inner):
            key_grad, value_grad = carry
            query_block, grad_block, total_block, start = inner
            scores = block_scores(query_block, slot_keys, start, length, scale)
            probs = jnp.exp(scores - total_block[..., None])
            prob_grad = jnp.einsum(
                "qhd,khd->hqk", grad_block, slot_values, preferred_element_type=jnp.float32
            )
            center = jnp.sum(probs * prob_grad, axis=-1, keepdims=True)
            score_grad = (probs * (prob_grad - center)).astype(jnp.bfloat16)
            query_grad = (
                jnp.einsum(
                    "hqk,khd->qhd", score_grad, slot_keys, preferred_element_type=jnp.float32
                )
                * scale
            )
            key_grad = (
                key_grad
                + jnp.einsum(
                    "hqk,qhd->khd", score_grad, query_block, preferred_element_type=jnp.float32
                )
                * scale
            )
            value_grad = value_grad + jnp.einsum(
                "hqk,qhd->khd",
                probs.astype(jnp.bfloat16),
                grad_block,
                preferred_element_type=jnp.float32,
            )
            return ((key_grad, value_grad), query_grad)

        empty = jnp.zeros((slot_len, heads_here, head_size), jnp.float32)
        shaped_queries = slot_queries.reshape(blocks, block_len, heads_here, head_size)
        shaped_grads = slot_grads.reshape(blocks, block_len, heads_here, head_size)
        (key_grad, value_grad), query_grad = lax.scan(
            per_block, (empty, empty), (shaped_queries, shaped_grads, slot_totals, starts)
        )
        return (query_grad.reshape(slot_len, heads_here, head_size), key_grad, value_grad)

    return lax.map(per_slot, (queries, keys, values, lengths, grad_mixed, log_totals))


def row_valid(lengths, slot_len, start, count):
    index = start + jnp.arange(count, dtype=jnp.int32)
    slot_of = index // slot_len
    place = index % slot_len
    slot_ids = jnp.arange(lengths.shape[0], dtype=jnp.int32)
    limit = jnp.sum(jnp.where(slot_of[:, None] == slot_ids[None, :], lengths[None, :], 0), axis=1)
    return (place < limit).astype(jnp.float32)


def nesterov(grad, weight, moment, average, rate):
    moment_new = MOMENTUM * moment + grad
    weight_new = weight - rate * (grad + MOMENTUM * moment_new)
    average_new = AVERAGE_DECAY * average + (1.0 - AVERAGE_DECAY) * weight_new
    return (grad, moment_new, average_new, weight_new)


def shards_any(
    tokens,
    first_values,
    lengths,
    cotangent,
    w_qkv,
    w_out,
    w_gateup,
    w_down,
    gains,
    moment_qkv,
    moment_out,
    moment_gateup,
    moment_down,
    moment_gains,
    average_qkv,
    average_out,
    average_gateup,
    average_down,
    average_gains,
):
    local_rows, model = tokens.shape
    mp_count = lax.axis_size("mp")
    dp_count = lax.axis_size("dp")
    mp_index = lax.axis_index("mp")
    dp_index = lax.axis_index("dp")
    slot_count = lengths.shape[0]
    group_rows = local_rows * mp_count
    slot_len = group_rows // slot_count
    head_cols = w_qkv.shape[2]
    hidden_cols = w_gateup.shape[2]
    heads_here = head_cols // HEAD_DIM
    row_start = mp_index * local_rows
    all_tokens = group_rows * dp_count
    root_count = math.sqrt(all_tokens)
    qkv_bf = w_qkv.astype(jnp.bfloat16).reshape(model, 3 * head_cols)
    out_bf = w_out.astype(jnp.bfloat16)
    gateup_bf = w_gateup.astype(jnp.bfloat16).reshape(model, 2 * hidden_cols)
    down_bf = w_down.astype(jnp.bfloat16)
    gain_one = gains[0]
    gain_two = gains[1]
    valid_local = row_valid(lengths, slot_len, row_start, local_rows)
    x_local = tokens.astype(jnp.float32)
    x_group = lax.all_gather(tokens, "mp", axis=0, tiled=True).astype(jnp.float32)
    norm_one, unit_one, inverse_one = normalize(x_group, gain_one)
    norm_one_bf = norm_one.astype(jnp.bfloat16)
    qkv = jnp.dot(norm_one_bf, qkv_bf, preferred_element_type=jnp.float32)
    qkv = qkv.reshape(slot_count, slot_len, 3, heads_here, HEAD_DIM)
    cosine, sine = rope_tables(slot_len, HEAD_DIM)
    queries = rotate(qkv[:, :, 0], cosine, sine).astype(jnp.bfloat16)
    keys = rotate(qkv[:, :, 1], cosine, sine).astype(jnp.bfloat16)
    first_shaped = first_values.astype(jnp.float32).reshape(
        slot_count, slot_len, heads_here, HEAD_DIM
    )
    values = (HALF * qkv[:, :, 2] + HALF * first_shaped).astype(jnp.bfloat16)
    mixed, log_totals = attend_forward(queries, keys, values, lengths)
    mixed_bf = mixed.reshape(group_rows, head_cols).astype(jnp.bfloat16)
    resid_local = x_local + lax.psum_scatter(
        jnp.dot(mixed_bf, out_bf, preferred_element_type=jnp.float32),
        "mp",
        scatter_dimension=0,
        tiled=True,
    )
    norm_two_local, unit_two, inverse_two = normalize(resid_local, gain_two)
    norm_two_bf = lax.all_gather(norm_two_local.astype(jnp.bfloat16), "mp", axis=0, tiled=True)
    gateup = jnp.dot(norm_two_bf, gateup_bf, preferred_element_type=jnp.float32)
    gate_val = gateup[:, :hidden_cols]
    up_val = gateup[:, hidden_cols:]
    sigmoid_gate = jax.nn.sigmoid(gate_val)
    silu_gate = gate_val * sigmoid_gate
    hidden_bf = (silu_gate * up_val).astype(jnp.bfloat16)
    result_local = resid_local + lax.psum_scatter(
        jnp.dot(hidden_bf, down_bf, preferred_element_type=jnp.float32),
        "mp",
        scatter_dimension=0,
        tiled=True,
    )
    output = result_local.astype(jnp.bfloat16)
    grad_local = (cotangent.astype(jnp.float32) * valid_local[:, None]).astype(jnp.bfloat16)
    grad_group = lax.all_gather(grad_local, "mp", axis=0, tiled=True)
    grad_down = dot_first(hidden_bf, grad_group)
    grad_hidden = dot_last(grad_group, down_bf)
    grad_gate = grad_hidden * up_val * sigmoid_gate * (1.0 + gate_val * (1.0 - sigmoid_gate))
    grad_up = grad_hidden * silu_gate
    grad_gateup_bf = jnp.concatenate([grad_gate, grad_up], axis=1).astype(jnp.bfloat16)
    grad_gateup = dot_first(norm_two_bf, grad_gateup_bf)
    grad_norm_two = lax.psum_scatter(
        dot_last(grad_gateup_bf, gateup_bf), "mp", scatter_dimension=0, tiled=True
    )
    grad_resid_local = grad_local.astype(jnp.float32) + norm_back(
        grad_norm_two, gain_two, unit_two, inverse_two
    )
    gain_two_grad = jnp.sum(grad_norm_two * unit_two, axis=0)
    grad_resid_bf = lax.all_gather(grad_resid_local.astype(jnp.bfloat16), "mp", axis=0, tiled=True)
    grad_out = dot_first(mixed_bf, grad_resid_bf)
    grad_mixed = dot_last(grad_resid_bf, out_bf).astype(jnp.bfloat16)
    grad_mixed = grad_mixed.reshape(slot_count, slot_len, heads_here, HEAD_DIM)
    query_grad, key_grad, value_grad = attend_backward(
        queries, keys, values, lengths, grad_mixed, log_totals
    )
    first_values_grad = (HALF * value_grad).reshape(group_rows, head_cols)
    grad_qkv_bf = jnp.stack(
        [unrotate(query_grad, cosine, sine), unrotate(key_grad, cosine, sine), HALF * value_grad],
        axis=2,
    )
    grad_qkv_bf = grad_qkv_bf.reshape(group_rows, 3 * head_cols).astype(jnp.bfloat16)
    grad_qkv = dot_first(norm_one_bf, grad_qkv_bf)
    unit_local = lax.dynamic_slice_in_dim(unit_one, row_start, local_rows, 0)
    inverse_local = lax.dynamic_slice_in_dim(inverse_one, row_start, local_rows, 0)
    grad_norm_one = lax.psum_scatter(
        dot_last(grad_qkv_bf, qkv_bf).astype(jnp.bfloat16), "mp", scatter_dimension=0, tiled=True
    ).astype(jnp.float32)
    input_grad = grad_resid_local + norm_back(grad_norm_one, gain_one, unit_local, inverse_local)
    gain_one_grad = jnp.sum(grad_norm_one * unit_local, axis=0)
    sum_qkv, sum_out, sum_gateup, sum_down = (
        lax.psum_scatter(
            grad_qkv.reshape(model, 3, head_cols), "dp", scatter_dimension=0, tiled=True
        ),
        lax.psum_scatter(grad_out, "dp", scatter_dimension=1, tiled=True),
        lax.psum_scatter(
            grad_gateup.reshape(model, 2, hidden_cols), "dp", scatter_dimension=0, tiled=True
        ),
        lax.psum_scatter(grad_down, "dp", scatter_dimension=1, tiled=True),
    )
    gain_sum = lax.psum(jnp.stack([gain_one_grad, gain_two_grad], axis=0), ("dp", "mp"))
    share = model // dp_count
    own_qkv = lax.dynamic_slice_in_dim(w_qkv, dp_index * share, share, 0)
    own_out = lax.dynamic_slice_in_dim(w_out, dp_index * share, share, 1)
    own_gateup = lax.dynamic_slice_in_dim(w_gateup, dp_index * share, share, 0)
    own_down = lax.dynamic_slice_in_dim(w_down, dp_index * share, share, 1)
    qkv_set = nesterov(sum_qkv / root_count, own_qkv, moment_qkv, average_qkv, RATE_QKV)
    out_set = nesterov(sum_out / root_count, own_out, moment_out, average_out, RATE_OUT)
    gateup_set = nesterov(
        sum_gateup / root_count, own_gateup, moment_gateup, average_gateup, RATE_GATEUP
    )
    down_set = nesterov(sum_down / root_count, own_down, moment_down, average_down, RATE_DOWN)
    gains_set = nesterov(gain_sum / root_count, gains, moment_gains, average_gains, RATE_GAINS)
    return (
        output,
        input_grad,
        first_values_grad,
        qkv_set[0],
        qkv_set[1],
        qkv_set[2],
        qkv_set[3],
        out_set[0],
        out_set[1],
        out_set[2],
        out_set[3],
        gateup_set[0],
        gateup_set[1],
        gateup_set[2],
        gateup_set[3],
        down_set[0],
        down_set[1],
        down_set[2],
        down_set[3],
        gains_set[0],
        gains_set[1],
        gains_set[2],
        gains_set[3],
    )


F32 = jnp.float32
BF16 = jnp.bfloat16
LANES = 128
BLK = 256
ROWS = 256
PARTS = 3
SWAP = ((0, 1), (1, 0))
VMEM_MIB = 60


def nt(left, right):
    return lax.dot_general(left, right, (((1,), (1,)), ((), ())), preferred_element_type=F32)


def nn(left, right):
    return lax.dot_general(left, right, (((1,), (0,)), ((), ())), preferred_element_type=F32)


def tn(left, right):
    return lax.dot_general(left, right, (((0,), (0,)), ((), ())), preferred_element_type=F32)


def lane_of(rows):
    return lax.broadcasted_iota(jnp.int32, (rows, LANES), 1)


def params(mib):
    return pltpu.CompilerParams(vmem_limit_bytes=mib * 2**20)


def cost(flops, moved, exps=0):
    return pl.CostEstimate(flops=int(flops), bytes_accessed=int(moved), transcendentals=int(exps))


def partner_lanes(pair):
    lane = lane_of(pair.shape[0])
    return jnp.where((lane % HEAD_DIM) < HEAD_DIM // 2, pltpu.roll(pair, LANES - 32, 1), pltpu.roll(pair, 32, 1))


def pair_tables(length):
    cosine, sine = rope_tables(length, HEAD_DIM)
    cosine, sine = cosine[:, 0, :], sine[:, 0, :]
    wide_cos = jnp.concatenate([cosine] * 4, axis=1)
    wide_sin = jnp.concatenate([-sine, sine, -sine, sine], axis=1)
    return wide_cos, wide_sin


def qkv_kernel(base_ref, x_ref, first_ref, gain_ref, w_ref, cos_ref, sin_ref, *refs):
    n_ref, q_ref, k_ref, v_ref = refs[-4:]
    x = x_ref[...].astype(F32)
    inverse = lax.rsqrt(jnp.mean(x * x, axis=-1, keepdims=True) + EPS)
    norm = ((x * inverse) * gain_ref[...]).astype(BF16)
    n_ref[...] = norm
    cosine, sine = cos_ref[...], sin_ref[...]
    for part, out in ((0, q_ref), (1, k_ref)):
        flat = nn(norm, w_ref[:, part * q_ref.shape[1] : (part + 1) * q_ref.shape[1]])
        for c in range(flat.shape[1] // LANES):
            pair = flat[:, c * LANES : (c + 1) * LANES]
            turned = (pair * cosine + partner_lanes(pair) * sine).astype(BF16)
            if part == 0:
                turned = turned * jnp.asarray(0.125, BF16)
            out[:, c * LANES : (c + 1) * LANES] = turned
    v_ref[...] = (HALF * nn(norm, w_ref[:, 2 * q_ref.shape[1] :]) + HALF * first_ref[...].astype(F32)).astype(BF16)


def project_qkv(base, x, first, gain, w, cosine, sine, before):
    rows, model = x.shape
    slot_len, cols = first.shape
    here = lambda i, b: (i, 0)
    there = lambda i, b: (b[0] + i, 0)
    outs = (
        jax.ShapeDtypeStruct((slot_len, model), BF16),
        *(jax.ShapeDtypeStruct((slot_len, cols), BF16) for _ in range(3)),
    )
    before = () if before is None else tuple(before)
    return pl.pallas_call(
        qkv_kernel,
        out_shape=outs,
        grid_spec=pltpu.PrefetchScalarGridSpec(
            num_scalar_prefetch=1,
            grid=(rows // ROWS,),
            in_specs=[
                pl.BlockSpec((ROWS, model), here),
                pl.BlockSpec((ROWS, cols), there),
                pl.BlockSpec((1, model), lambda i, b: (0, 0)),
                pl.BlockSpec((model, PARTS * cols), lambda i, b: (0, 0)),
                pl.BlockSpec((ROWS, LANES), there),
                pl.BlockSpec((ROWS, LANES), there),
                *(pl.BlockSpec(memory_space=pl.ANY) for _ in before),
            ],
            out_specs=[pl.BlockSpec((ROWS, o.shape[1]), there) for o in outs],
        ),
        input_output_aliases={7 + n: n for n in range(len(before))},
        compiler_params=params(VMEM_MIB),
        cost_estimate=cost(2 * rows * model * cols * 3, 10e6),
        name="project_qkv",
    )(base, x, first, gain, w, cosine, sine, *before)


SAFE_SCORE = 60.0


def spare(head):
    return HEAD_DIM * (1 - head)


def own_lanes(lane, head):
    return (lane // HEAD_DIM) == head


def length_bias(slot_len, length):
    row = lax.broadcasted_iota(jnp.int32, (slot_len, LANES), 0)
    return jnp.where(row < length, 0.0, NEG_BIG).astype(BF16)


def causal_bias(mask_ref, query_axis):
    query = lax.broadcasted_iota(jnp.int32, (BLK, BLK), query_axis)
    key = lax.broadcasted_iota(jnp.int32, (BLK, BLK), 1 - query_axis)
    mask_ref[...] = jnp.where(key <= query, 0.0, NEG_BIG)


def largest_square(pair, both):
    flat = pair.astype(F32)
    return jnp.max(nn((flat * flat).astype(BF16), both))


def attend_fwd_kernel(scalar_ref, q_ref, k_ref, v_ref, *refs):
    o_ref, lse_ref, send_ref, ka, va, mask_ref = refs[-6:]
    slot_len = k_ref.shape[0]
    lane = lane_of(slot_len)
    bias = length_bias(slot_len, scalar_ref[0])
    for head in (0, 1):
        mine = own_lanes(lane, head)
        extra = jnp.where(lane == spare(head), bias, jnp.zeros_like(bias))
        ka[head] = jnp.where(mine, k_ref[...], extra)
        va[head] = jnp.where(mine, v_ref[...], jnp.ones_like(bias))
    causal_bias(mask_ref, 0)
    side = lambda axis: lax.broadcasted_iota(jnp.int32, (LANES, LANES), axis) // HEAD_DIM
    both = jnp.where(side(0) == side(1), 1.0, 0.0).astype(BF16)
    reach = largest_square(q_ref[...], both) * largest_square(k_ref[...], both)

    def rows_of(shifted):
        low = lane_of(BLK) < HEAD_DIM
        for i in range(slot_len // BLK):
            queries, seen = pl.ds(i * BLK, BLK), pl.ds(0, (i + 1) * BLK)
            before = i * BLK
            q = q_ref[queries, :]
            outs, peaks = [], []
            for head in (0, 1):
                one = jnp.where(lane_of(BLK) == spare(head), 1.0, 0.0).astype(BF16)
                scores = nt(jnp.where(own_lanes(lane_of(BLK), head), q, one), ka[head, seen, :])
                last = scores[:, before:] + mask_ref[...]
                scores = last if i == 0 else jnp.concatenate([scores[:, :before], last], axis=1)
                if shifted:
                    peak = jnp.max(scores, axis=1, keepdims=True)
                    scores = scores - peak
                    peaks.append(peak)
                outs.append(nn(jnp.exp(scores).astype(BF16), va[head, seen, :]))
            total = pltpu.roll(jnp.where(low, outs[1], outs[0]), HEAD_DIM, 1)
            o_ref[queries, :] = (jnp.where(low, outs[0], outs[1]) / total).astype(BF16)
            shift = jnp.where(low, peaks[0], peaks[1]) if shifted else 0.0
            lse_ref[queries, :] = shift + jnp.log(total)

    small = reach < (0.9 * SAFE_SCORE) ** 2

    @pl.when(small)
    def _():
        rows_of(False)

    @pl.when(jnp.logical_not(small))
    def _():
        rows_of(True)

    half = send_ref.shape[0]
    send_ref[...] = o_ref[pl.ds(pl.multiple_of(scalar_ref[1] * half, half), half), :]


def attend_pairs(first, count, scalars, q, k, v, before):
    slot_len, cols = q.shape
    full = pl.BlockSpec((slot_len, LANES), lambda p, n: (0, first + p))
    before = () if before is None else tuple(before)
    both = pltpu.VMEM((2, slot_len, LANES), BF16)
    return pl.pallas_call(
        attend_fwd_kernel,
        out_shape=(
            jax.ShapeDtypeStruct((slot_len, cols), BF16),
            jax.ShapeDtypeStruct((slot_len, cols), F32),
            jax.ShapeDtypeStruct((slot_len // 2, count * LANES), BF16),
        ),
        grid_spec=pltpu.PrefetchScalarGridSpec(
            num_scalar_prefetch=1,
            grid=(count,),
            in_specs=[full] * 3 + [pl.BlockSpec(memory_space=pl.ANY) for _ in before],
            out_specs=[full, full, pl.BlockSpec((slot_len // 2, LANES), lambda p, n: (0, p))],
            scratch_shapes=[both, both, pltpu.VMEM((BLK, BLK), F32)],
        ),
        input_output_aliases={4 + n: n for n in range(len(before))},
        compiler_params=params(VMEM_MIB),
        cost_estimate=cost(count * 2 * 2 * slot_len * slot_len * 256, 3e6 * count),
        name="attend_pairs",
    )(scalars, q, k, v, *before)


def split3(x):
    high = x.astype(BF16)
    rest = x - high.astype(F32)
    mid = rest.astype(BF16)
    return high, mid, (rest - mid.astype(F32)).astype(BF16)


def attend_back_kernel(scalar_ref, q_ref, k_ref, v_ref, o_ref, lse_ref, mine_ref, theirs_ref, cos_ref, sin_ref, *refs):
    fv_ref, grad_ref, send_ref, ka, va, kz, do_ref, mask_ref, dk_ref, dv_ref = refs[-10:]
    slot_len = k_ref.shape[0]
    half = slot_len // 2
    far_rows = pl.ds(pl.multiple_of(scalar_ref[1] * half, half), half)
    do_ref[pl.ds(pl.multiple_of((1 - scalar_ref[1]) * half, half), half), :] = mine_ref[...]
    do_ref[far_rows, :] = theirs_ref[...]
    lane = lane_of(slot_len)
    bias = length_bias(slot_len, scalar_ref[0])
    zero, minus = jnp.zeros_like(bias), jnp.full_like(bias, -1.0)
    for head in (0, 1):
        mine, at = own_lanes(lane, head), spare(head)
        ones = jnp.where((lane > at) & (lane < at + 4), minus, zero)
        ka[head] = jnp.where(mine, k_ref[...], jnp.where(lane == at, bias, ones))
        va[head] = jnp.where(mine, v_ref[...], ones)
        kz[head] = jnp.where(mine, k_ref[...], zero)
    causal_bias(mask_ref, 1)
    lane = lane_of(BLK)
    low = lane < HEAD_DIM
    zero = jnp.zeros((BLK, LANES), BF16)

    def unturn(grad, rows):
        return grad * cos_ref[rows, :] - partner_lanes(grad) * sin_ref[rows, :]

    for i in range(slot_len // BLK):
        queries, seen = pl.ds(i * BLK, BLK), pl.ds(0, (i + 1) * BLK)
        before = i * BLK
        q, do = q_ref[queries, :], do_ref[queries, :]
        prod = do.astype(F32) * o_ref[queries, :].astype(F32)
        center_low = jnp.sum(jnp.where(low, prod, 0.0), axis=1, keepdims=True)
        center_high = jnp.sum(jnp.where(low, 0.0, prod), axis=1, keepdims=True)
        centers = split3(jnp.where(low, center_high, center_low))
        totals = split3(pltpu.roll(lse_ref[queries, :], HEAD_DIM, 1))
        dq = dk = dv = None
        for head in (0, 1):
            mine = own_lanes(lane, head)

            def place(block, items):
                out = zero
                for n, item in enumerate(items):
                    out = jnp.where(lane == spare(head) + n, item, out)
                return jnp.where(mine, block, out)

            s = nt(ka[head, seen, :], place(q, [jnp.ones_like(zero), *totals]))
            last = s[before:] + mask_ref[...]
            p = jnp.exp(last if i == 0 else jnp.concatenate([s[:before], last], axis=0))
            ds = (p * nt(va[head, seen, :], place(do, [zero, *centers]))).astype(BF16)
            term = nn(p.astype(BF16), jnp.where(mine, do, zero))
            dv = term if dv is None else dv + term
            term = nn(ds, jnp.where(mine, q, zero))
            dk = term if dk is None else dk + term
            term = tn(ds, kz[head, seen, :])
            dq = term if dq is None else dq + term
        if i > 0:
            dv_ref[pl.ds(0, before), :] += dv[:before]
            dk_ref[pl.ds(0, before), :] += dk[:before]
        dv_ref[queries, :] = dv[before:]
        dk_ref[queries, :] = dk[before:]
        grad_ref[queries, 0:LANES] = unturn(dq * 0.125, queries).astype(BF16)
    for i in range(slot_len // BLK):
        keys = pl.ds(i * BLK, BLK)
        half_dv = HALF * dv_ref[keys, :]
        fv_ref[keys, :] = half_dv
        grad_ref[keys, 2 * LANES : 3 * LANES] = half_dv.astype(BF16)
        grad_ref[keys, LANES : 2 * LANES] = unturn(dk_ref[keys, :], keys).astype(BF16)
    send_ref[...] = grad_ref[far_rows, :]


def attend_back_pairs(first, count, scalars, q, k, v, o, lse, mine, theirs, at, cosine, sine, before):
    slot_len, cols = q.shape
    full = pl.BlockSpec((slot_len, LANES), lambda p, n: (0, first + p))
    own = pl.BlockSpec((slot_len, LANES), lambda p, n: (0, 0))
    before = () if before is None else tuple(before)
    both = pltpu.VMEM((2, slot_len, LANES), BF16)
    acc = pltpu.VMEM((slot_len, LANES), F32)
    wide = PARTS * LANES
    return pl.pallas_call(
        attend_back_kernel,
        out_shape=(
            jax.ShapeDtypeStruct((slot_len, cols), F32),
            jax.ShapeDtypeStruct((slot_len, PARTS * cols), BF16),
            jax.ShapeDtypeStruct((slot_len // 2, count * wide), BF16),
        ),
        grid_spec=pltpu.PrefetchScalarGridSpec(
            num_scalar_prefetch=1,
            grid=(count,),
            in_specs=[full] * 5
            + [
                pl.BlockSpec((slot_len // 2, LANES), lambda p, n: (0, first + p)),
                pl.BlockSpec((slot_len // 2, LANES), lambda p, n: (0, at + p)),
                own,
                own,
            ]
            + [pl.BlockSpec(memory_space=pl.ANY) for _ in before],
            out_specs=[
                full,
                pl.BlockSpec((slot_len, wide), lambda p, n: (0, first + p)),
                pl.BlockSpec((slot_len // 2, wide), lambda p, n: (0, p)),
            ],
            scratch_shapes=[both, both, both, pltpu.VMEM((slot_len, LANES), BF16),
                            pltpu.VMEM((BLK, BLK), F32), acc, acc],
        ),
        input_output_aliases={10 + n: n for n in range(len(before))},
        compiler_params=params(VMEM_MIB),
        cost_estimate=cost(count * (40 if first > 1 else 10) * slot_len * slot_len * 256, 6e6 * count),
        name="attend_back_pairs",
    )(scalars, q, k, v, o, lse, mine, theirs, cosine, sine, *before)


def resid_kernel(base_ref, x_ref, gain_ref, w_own_ref, w_far_ref, own_ref, *refs):
    own = own_ref[...]
    far = jnp.concatenate([r[...] for r in refs[:-3]], axis=1)
    h_ref, n_ref, o_ref = refs[-3:]
    h = x_ref[...].astype(F32) + (nn(own, w_own_ref[...]) + nn(far, w_far_ref[...]))
    inverse = lax.rsqrt(jnp.mean(h * h, axis=-1, keepdims=True) + EPS)
    h_ref[...] = h.astype(BF16)
    n_ref[...] = ((h * inverse) * gain_ref[...]).astype(BF16)
    cols = own.shape[1]
    o_ref[:, :cols] = far
    o_ref[:, cols:] = own


def resid_rows(base, x, gain, w_own, w_far, own, far):
    rows, model = x.shape
    cols = w_own.shape[0]
    wide = pl.BlockSpec((ROWS, model), lambda i, b: (i, 0))
    fixed = pl.BlockSpec((cols, model), lambda i, b: (0, 0))
    return pl.pallas_call(
        resid_kernel,
        out_shape=(
            jax.ShapeDtypeStruct((rows, model), BF16),
            jax.ShapeDtypeStruct((rows, model), BF16),
            jax.ShapeDtypeStruct((rows, 2 * cols), BF16),
        ),
        grid_spec=pltpu.PrefetchScalarGridSpec(
            num_scalar_prefetch=1,
            grid=(rows // ROWS,),
            in_specs=[
                wide,
                pl.BlockSpec((1, model), lambda i, b: (0, 0)),
                fixed,
                fixed,
                pl.BlockSpec((ROWS, cols), lambda i, b: (b[0] + i, 0)),
                *(pl.BlockSpec((ROWS, f.shape[1]), lambda i, b: (i, 0)) for f in far),
            ],
            out_specs=[wide, wide, pl.BlockSpec((ROWS, 2 * cols), lambda i, b: (i, 0))],
        ),
        compiler_params=params(VMEM_MIB),
        cost_estimate=cost(2 * rows * model * cols * 2, 14e6),
        name="resid_rows",
    )(base, x, gain, w_own, w_far, own, *far)


def weave_kernel(q_ref, gu_ref, d_ref, out_ref):
    cols = q_ref.shape[2]
    for part in range(PARTS):
        out_ref[:, part * cols : (part + 1) * cols] = q_ref[part].astype(BF16)
    down = d_ref[...].T
    for run in range(gu_ref.shape[2] // LANES):
        lanes = slice(run * LANES, (run + 1) * LANES)
        for part, piece in enumerate((gu_ref[:, 0, lanes], gu_ref[:, 1, lanes], down[:, lanes])):
            spot = PARTS * cols + (3 * run + part) * LANES
            out_ref[:, spot : spot + LANES] = piece.astype(BF16)


def weave(w_qkv, w_gateup, w_down):
    parts, model, cols = w_qkv.shape
    sides, hidden = w_gateup.shape[1:]
    rows = 128
    wide = parts * cols + 3 * hidden
    return pl.pallas_call(
        weave_kernel,
        out_shape=jax.ShapeDtypeStruct((model, wide), BF16),
        grid=(model // rows,),
        in_specs=[
            pl.BlockSpec((parts, rows, cols), lambda i: (0, i, 0)),
            pl.BlockSpec((rows, sides, hidden), lambda i: (i, 0, 0)),
            pl.BlockSpec((hidden, rows), lambda i: (0, i)),
        ],
        out_specs=pl.BlockSpec((rows, wide), lambda i: (i, 0)),
        compiler_params=params(VMEM_MIB),
        cost_estimate=cost(0, 6 * model * wide),
        name="weave",
    )(w_qkv, w_gateup, w_down)


def halve_rows(grad, core, x, keep, send):
    rows = grad.shape[0] // 16
    block = lambda z, i, c: grad[(z * 4 + i * 2 + c) * rows : (z * 4 + i * 2 + c + 1) * rows]
    for i in (0, 1):
        for z in range(4):
            spot = pl.ds((i * 4 + z) * rows, rows)
            same = [jnp.where(x == 0, block(z, i, c), block(z, 1 - i, c)) for c in (0, 1)]
            keep[spot, :] = jnp.where(core == 0, same[0], same[1])
            send[spot, :] = jnp.where(core == 0, same[1], same[0])


def runs(block, count, of, which):
    return jnp.concatenate(
        [block[:, (of * i + which) * LANES : (of * i + which + 1) * LANES] for i in range(count)], axis=1
    )


def swiglu_kernel(halved, place_ref, n_ref, dy_ref, w_ref, y_ref, dn_ref, *refs):
    y_acc, dn_acc = refs[-2:]
    step = pl.program_id(0)
    last = pl.num_programs(0) - 1

    def work(count, first):
        n = n_ref[...]
        dy = dy_ref[...]
        run = lambda i: w_ref[:, i * LANES : (i + 1) * LANES]
        wgu = jnp.concatenate([run(3 * i + j) for i in range(count) for j in (0, 1)], axis=1)
        wd = jnp.concatenate([run(3 * i + 2) for i in range(count)], axis=1)
        both = nn(n, wgu)
        gate, up = runs(both, count, 2, 0), runs(both, count, 2, 1)
        sig = jax.nn.sigmoid(gate)
        silu = gate * sig
        hid = (silu * up).astype(BF16)
        dhid = nn(dy, wd)
        dgate = (dhid * up * sig * (1.0 + gate * (1.0 - sig))).astype(BF16)
        dup = (dhid * silu).astype(BF16)
        dgu = jnp.concatenate(
            [d[:, i * LANES : (i + 1) * LANES] for i in range(count) for d in (dgate, dup)], axis=1
        )
        y = nt(hid, wd)
        dn = nt(dgu, wgu)
        if first:
            y_acc[...] = y
            dn_acc[...] = dn
        else:
            y_acc[...] += y
            dn_acc[...] += dn
        grad_gu = tn(n, dgu).astype(BF16)
        grad_d = tn(dy, hid).astype(BF16)
        for i in range(count):
            for part, grad in enumerate((grad_gu[:, 2 * i * LANES : (2 * i + 2) * LANES],
                                         grad_d[:, i * LANES : (i + 1) * LANES])):
                start = (3 * i + 2 * part) * LANES
                spot = slice(start, start + grad.shape[1])
                if halved:
                    halve_rows(grad, place_ref[0], place_ref[1], refs[0].at[:, spot], refs[1].at[:, spot])
                else:
                    refs[0][:, spot] = grad

    @pl.when(step == 0)
    def _():
        work(2, True)

    @pl.when((step > 0) & (step < last))
    def _():
        work(2, False)

    @pl.when(step == last)
    def _():
        work(1, False)
        y_ref[...] = y_acc[...].astype(BF16)
        dn_ref[...] = dn_acc[...].astype(BF16)


def swiglu_half(place, n, dy, w, first, width=None):
    rows, model = n.shape
    tile = 256
    skip = first // (3 * tile)
    hidden = (w.shape[1] - first) // 3
    held = pl.BlockSpec((rows, model), lambda t, p: (0, 0))
    cols = pl.BlockSpec((model, 3 * tile), lambda t, p: (0, t))
    source = pl.BlockSpec((model, 3 * tile), lambda t, p: (0, skip + t))
    half = pl.BlockSpec((model // 2, 3 * tile), lambda t, p: (0, t))
    grads = [(model, 3 * hidden)] if width is None else [(model // 2, width)] * 2
    return pl.pallas_call(
        functools.partial(swiglu_kernel, width is not None),
        out_shape=(
            *(jax.ShapeDtypeStruct((rows, model), BF16) for _ in range(2)),
            *(jax.ShapeDtypeStruct(g, BF16) for g in grads),
        ),
        grid_spec=pltpu.PrefetchScalarGridSpec(
            num_scalar_prefetch=1,
            grid=(-(-hidden // tile),),
            in_specs=[held, held, source],
            out_specs=[held, held] + ([cols] if width is None else [half, half]),
            scratch_shapes=[pltpu.VMEM((rows, model), F32)] * 2,
        ),
        compiler_params=params(VMEM_MIB),
        cost_estimate=cost(9 * 2 * rows * model * hidden, 36e6, rows * hidden),
        name="swiglu_half",
    )(place, n, dy, w)


def grad_out_kernel(place_ref, dhb_ref, o_ref, keep_ref, send_ref):
    grad = tn(dhb_ref[...], o_ref[...]).astype(BF16)
    halve_rows(grad, place_ref[0], place_ref[1], keep_ref, send_ref)


def grad_out_of(place, dhb, o_cat):
    rows, model = dhb.shape
    tile = 512
    out = pl.BlockSpec((model // 2, tile), lambda t, p: (0, t))
    return pl.pallas_call(
        grad_out_kernel,
        out_shape=[jax.ShapeDtypeStruct((model // 2, o_cat.shape[1]), BF16)] * 2,
        grid_spec=pltpu.PrefetchScalarGridSpec(
            num_scalar_prefetch=1,
            grid=(o_cat.shape[1] // tile,),
            in_specs=[
                pl.BlockSpec((rows, model), lambda t, p: (0, 0)),
                pl.BlockSpec((rows, tile), lambda t, p: (0, t)),
            ],
            out_specs=[out, out],
        ),
        compiler_params=params(VMEM_MIB),
        cost_estimate=cost(2 * rows * model * o_cat.shape[1], 7e6),
        name="grad_out",
    )(place, dhb, o_cat)


def grad_qkv_kernel(place_ref, n_ref, dqkv_ref, *refs):
    keep_ref, send_ref, t_ref = refs[-3:]
    grad = tn(n_ref[...], dqkv_ref[...])
    term = None
    for i in range(grad.shape[1] // LANES):
        weight = refs[i % PARTS][:, (i // PARTS) * LANES : (i // PARTS + 1) * LANES]
        piece = grad[:, i * LANES : (i + 1) * LANES] * weight.astype(F32)
        term = piece if term is None else term + piece
    t_ref[...] = term
    halve_rows(grad.astype(BF16), place_ref[0], place_ref[1], keep_ref, send_ref)


def grad_qkv_of(first, place, norm, dqkv, w, into):
    slot_len, model = norm.shape
    pairs = 2
    tile = pairs * PARTS * LANES
    steps = dqkv.shape[1] // tile
    at = first // pairs
    out = pl.BlockSpec((model // 2, tile), lambda t, p: (0, 0))
    into = () if into is None else tuple(into)
    width = into[0].shape[1] if into else tile
    return pl.pallas_call(
        grad_qkv_kernel,
        out_shape=(
            *(jax.ShapeDtypeStruct((model // 2, width), BF16) for _ in range(2)),
            jax.ShapeDtypeStruct((model, LANES), F32),
        ),
        grid_spec=pltpu.PrefetchScalarGridSpec(
            num_scalar_prefetch=1,
            grid=(1,),
            in_specs=[
                pl.BlockSpec((slot_len, model), lambda t, p: (0, 0)),
                pl.BlockSpec((slot_len, tile), lambda t, p: (0, at)),
                *(
                    pl.BlockSpec((model, pairs * LANES), lambda t, p, part=part: (0, part * steps + at))
                    for part in range(PARTS)
                ),
                *(pl.BlockSpec(memory_space=pl.ANY) for _ in into),
            ],
            out_specs=[out, out, pl.BlockSpec((model, LANES), lambda t, p: (0, 0))],
        ),
        input_output_aliases={6 + n: n for n in range(len(into))},
        compiler_params=params(VMEM_MIB),
        cost_estimate=cost(2 * slot_len * model * tile, 14e6),
        name="grad_qkv",
    )(place, norm, dqkv, *[w] * PARTS, *into)


def after_kernel(h_ref, y1_ref, y2_ref, d1_ref, d2_ref, dy_ref, gain_ref, w_own_ref, w_far_ref,
                 out_ref, dhb_ref, own_ref, first_ref, second_ref, t_ref):
    h = h_ref[...].astype(F32)
    out_ref[...] = (h + (y1_ref[...].astype(F32) + y2_ref[...].astype(F32))).astype(BF16)
    inverse = lax.rsqrt(jnp.mean(h * h, axis=-1, keepdims=True) + EPS)
    unit = h * inverse
    dn = d1_ref[...].astype(F32) + d2_ref[...].astype(F32)
    e = dn * gain_ref[...]
    dh = dy_ref[...].astype(F32) + inverse * (e - unit * jnp.mean(e * unit, axis=-1, keepdims=True))
    dhb = dh.astype(BF16)
    dhb_ref[...] = dhb
    own_ref[...] = nt(dhb, w_own_ref[...]).astype(BF16)
    far = nt(dhb, w_far_ref[...]).astype(BF16)
    first_ref[...] = far[:, :LANES]
    second_ref[...] = far[:, LANES:]

    @pl.when(pl.program_id(0) == 0)
    def _():
        t_ref[...] = jnp.zeros_like(t_ref)

    t_ref[...] += jnp.sum(dn * unit, axis=0, keepdims=True)


def after_rows(h, y1, y2, d1, d2, dy, gain, w_own, w_far):
    rows, model = h.shape
    cols = w_own.shape[0]
    wide = pl.BlockSpec((ROWS, model), lambda i: (i, 0))
    fixed = pl.BlockSpec((cols, model), lambda i: (0, 0))
    slim = pl.BlockSpec((ROWS, cols), lambda i: (i, 0))
    first = pl.BlockSpec((ROWS, LANES), lambda i: (i, 0))
    second = pl.BlockSpec((ROWS, cols - LANES), lambda i: (i, 0))
    one = pl.BlockSpec((1, model), lambda i: (0, 0))
    return pl.pallas_call(
        after_kernel,
        out_shape=(
            jax.ShapeDtypeStruct((rows, model), BF16),
            jax.ShapeDtypeStruct((rows, model), BF16),
            jax.ShapeDtypeStruct((rows, cols), BF16),
            jax.ShapeDtypeStruct((rows, LANES), BF16),
            jax.ShapeDtypeStruct((rows, cols - LANES), BF16),
            jax.ShapeDtypeStruct((1, model), F32),
        ),
        grid=(rows // ROWS,),
        in_specs=[wide] * 6 + [one, fixed, fixed],
        out_specs=[wide, wide, slim, first, second, one],
        compiler_params=params(VMEM_MIB),
        cost_estimate=cost(2 * rows * model * cols * 2, 36e6),
        name="after_rows",
    )(h, y1, y2, d1, d2, dy, gain, w_own, w_far)


def by_part(flat):
    count = flat.shape[1] // (PARTS * LANES)
    return jnp.concatenate([runs(flat, count, PARTS, part) for part in range(PARTS)], axis=1)


def input_own_kernel(base_ref, grad_ref, w_ref, out_ref):
    out_ref[...] = nt(by_part(grad_ref[...]), w_ref[...]).astype(BF16)


def input_own(base, rows, dqkv, w):
    model = w.shape[0]
    return pl.pallas_call(
        input_own_kernel,
        out_shape=jax.ShapeDtypeStruct((rows, model), BF16),
        grid_spec=pltpu.PrefetchScalarGridSpec(
            num_scalar_prefetch=1,
            grid=(rows // ROWS,),
            in_specs=[
                pl.BlockSpec((ROWS, dqkv.shape[1]), lambda i, b: (b[0] + i, 0)),
                pl.BlockSpec((model, dqkv.shape[1]), lambda i, b: (0, 0)),
            ],
            out_specs=pl.BlockSpec((ROWS, model), lambda i, b: (i, 0)),
        ),
        compiler_params=params(VMEM_MIB),
        cost_estimate=cost(8 * rows * model * dqkv.shape[1], 8e6),
        name="input_own",
    )(base, dqkv, w)


def input_kernel(x_ref, dh_ref, gain_ref, part_ref, w_far_ref, *refs):
    out_ref = refs[-1]
    flat = jnp.concatenate([g[...] for g in refs[:-1]], axis=1)
    dn = part_ref[...].astype(F32) + nt(by_part(flat), w_far_ref[...])
    x = x_ref[...].astype(F32)
    inverse = lax.rsqrt(jnp.mean(x * x, axis=-1, keepdims=True) + EPS)
    unit = x * inverse
    e = dn * gain_ref[...]
    out_ref[...] = dh_ref[...].astype(F32) + inverse * (e - unit * jnp.mean(e * unit, axis=-1, keepdims=True))


def input_rows(x, dh, gain, part, w_far, far):
    rows, model = x.shape
    cols = sum(f.shape[1] for f in far)
    wide = pl.BlockSpec((ROWS, model), lambda i: (i, 0))
    return pl.pallas_call(
        input_kernel,
        out_shape=jax.ShapeDtypeStruct((rows, model), F32),
        grid=(rows // ROWS,),
        in_specs=[
            wide,
            wide,
            pl.BlockSpec((1, model), lambda i: (0, 0)),
            wide,
            pl.BlockSpec((model, cols), lambda i: (0, 0)),
            *(pl.BlockSpec((ROWS, f.shape[1]), lambda i: (i, 0)) for f in far),
        ],
        out_specs=wide,
        compiler_params=params(VMEM_MIB),
        cost_estimate=cost(8 * rows * model * cols, 20e6),
        name="input_rows",
    )(x, dh, gain, part, w_far, *far)


def step_of(sum_grad, weight, moment, average, rate, root_count):
    return nesterov(sum_grad / root_count, weight, moment, average, rate)


def own_columns(place, wide):
    turned = wide.T
    half = turned.shape[0] // 2
    return jnp.where(place == 0, turned[:half], turned[half:])


def step_mlp_kernel(root_count, place_ref, sum_ref, got_ref, wgu_ref, mgu_ref, agu_ref, wd_ref, md_ref, ad_ref, *outs):
    total = sum_ref[...].astype(F32) + got_ref[:, : sum_ref.shape[1]].astype(F32)
    count = total.shape[1] // (3 * LANES)
    for side in (0, 1):
        grads = step_of(runs(total, count, 3, side), wgu_ref[:, side, :], mgu_ref[:, side, :],
                        agu_ref[:, side, :], RATE_GATEUP, root_count)
        for out, value in zip(outs[:4], grads):
            out[:, side, :] = value
    weight = own_columns(place_ref[1], wd_ref[...])
    grads = step_of(runs(total, count, 3, 2), weight, md_ref[...], ad_ref[...], RATE_DOWN, root_count)
    for out, value in zip(outs[4:], grads):
        out[...] = value


def step_mlp(dp_index, root_count, total, got, w_gateup, m_gu, a_gu, w_down, m_d, a_d):
    place = jnp.stack([dp_index, dp_index % 2, dp_index // 2]).astype(jnp.int32)
    share, sides, hidden = m_gu.shape
    cols = total.shape[1]
    gu = pl.BlockSpec((share, sides, hidden), lambda i, p: (0, 0, 0))
    d = pl.BlockSpec((share, hidden), lambda i, p: (0, 0))
    return pl.pallas_call(
        functools.partial(step_mlp_kernel, root_count),
        out_shape=(
            *(jax.ShapeDtypeStruct(m_gu.shape, F32) for _ in range(4)),
            *(jax.ShapeDtypeStruct((share, hidden), F32) for _ in range(4)),
        ),
        grid_spec=pltpu.PrefetchScalarGridSpec(
            num_scalar_prefetch=1,
            grid=(1,),
            in_specs=[
                pl.BlockSpec((share, cols), lambda i, p: (0, 0)),
                pl.BlockSpec(got.shape, lambda i, p: (0, 0)),
                pl.BlockSpec((share, sides, hidden), lambda i, p: (p[0], 0, 0)),
                gu,
                gu,
                pl.BlockSpec((hidden, LANES), lambda i, p: (0, p[2])),
                d,
                d,
            ],
            out_specs=[gu] * 4 + [d] * 4,
        ),
        compiler_params=params(VMEM_MIB),
        cost_estimate=cost(0, 14e6),
        name="step_mlp",
    )(place, total, got, w_gateup, m_gu, a_gu, w_down, m_d, a_d)


def step_attention_kernel(root_count, place_ref, mix_ref, last_ref, got_ref, wq_ref, mq_ref, aq_ref, wo_ref, mo_ref, ao_ref, *outs):
    cols = ao_ref.shape[1]
    early = mix_ref.shape[1] - 2 * cols
    total = jnp.concatenate([mix_ref[:, :early], last_ref[...]], axis=1)
    count = total.shape[1] // (PARTS * LANES)
    for part in range(PARTS):
        grads = step_of(runs(total, count, PARTS, part), wq_ref[part], mq_ref[part], aq_ref[part],
                        RATE_QKV, root_count)
        for out, value in zip(outs[:4], grads):
            out[part] = value
    weight = own_columns(place_ref[1], wo_ref[...])
    grads = step_of(mix_ref[:, early + cols :] + got_ref[...].astype(F32), weight, mo_ref[...],
                    ao_ref[...], RATE_OUT, root_count)
    for out, value in zip(outs[4:], grads):
        out[...] = value


def step_attention(dp_index, root_count, mix, last, got, w_qkv, m_q, a_q, w_out, m_o, a_o):
    place = jnp.stack([dp_index, dp_index % 2, dp_index // 2]).astype(jnp.int32)
    parts, share, cols = m_q.shape
    q = pl.BlockSpec((parts, share, cols), lambda i, p: (0, 0, 0))
    o = pl.BlockSpec((share, cols), lambda i, p: (0, 0))
    return pl.pallas_call(
        functools.partial(step_attention_kernel, root_count),
        out_shape=(
            *(jax.ShapeDtypeStruct(m_q.shape, F32) for _ in range(4)),
            *(jax.ShapeDtypeStruct((share, cols), F32) for _ in range(4)),
        ),
        grid_spec=pltpu.PrefetchScalarGridSpec(
            num_scalar_prefetch=1,
            grid=(1,),
            in_specs=[
                pl.BlockSpec(mix.shape, lambda i, p: (0, 0)),
                pl.BlockSpec(last.shape, lambda i, p: (0, 0)),
                o,
                pl.BlockSpec((parts, share, cols), lambda i, p: (0, p[0], 0)),
                q,
                q,
                pl.BlockSpec((cols, LANES), lambda i, p: (0, p[2])),
                o,
                o,
            ],
            out_specs=[q] * 4 + [o] * 4,
        ),
        compiler_params=params(VMEM_MIB),
        cost_estimate=cost(0, 6e6),
        name="step_attention",
    )(place, mix, last, got, w_qkv, m_q, a_q, w_out, m_o, a_o)


def dp_pairs(move):
    return tuple((i, move(i)) for i in range(16))


CORE = dp_pairs(lambda i: i ^ 1)
CROSS = dp_pairs(lambda i: i ^ 2)
Z_LINES = tuple(tuple(z * 4 + i for z in range(4)) for i in range(4))
NEAR = tuple(
    tuple((i, i ^ flip) for i in range(32)) for flip in (1, 2, 3)
)
ALONG = tuple(dp_pairs(lambda i, step=step: (i + 4 * step) % 16) for step in (1, 2, 3))


def move(x, pairs):
    return lax.ppermute(x, "dp", pairs)


def add(left, right):
    return left.astype(F32) + right.astype(F32)


def after_core(keep, got):
    half = keep.shape[0] // 2
    here = add(keep[:half], got[:half]).astype(BF16)
    away = add(keep[half:], got[half:]).astype(BF16)
    return here, away


def after_cross(here, got, z):
    total = add(here, got)
    rows = here.shape[0] // 4
    block = lambda step: lax.dynamic_slice_in_dim(total, lax.rem(z + step, 4) * rows, rows, 0)
    return block(0), tuple(block(step).astype(BF16) for step in (1, 2, 3))


def after_along(mine, got):
    for piece in got:
        mine = mine + piece.astype(F32)
    return mine


def tie(values, *others):
    return lax.optimization_barrier((values, others))[0]


def shards_pair(
    tokens,
    first_values,
    lengths,
    cotangent,
    w_qkv,
    w_out,
    w_gateup,
    w_down,
    gains,
    moment_qkv,
    moment_out,
    moment_gateup,
    moment_down,
    moment_gains,
    average_qkv,
    average_out,
    average_gateup,
    average_down,
    average_gains,
):
    rows, model = tokens.shape
    mp_index = lax.axis_index("mp")
    dp_index = lax.axis_index("dp")
    dp_count = lax.axis_size("dp")
    z, core = dp_index // 4, dp_index % 2
    place = jnp.stack([core, (dp_index // 2) % 2]).astype(jnp.int32)
    slot_len = 2 * rows
    head_cols = w_qkv.shape[2]
    hidden = w_gateup.shape[2]
    pairs = head_cols // LANES
    root_count = math.sqrt(slot_len * dp_count)
    row_start = mp_index * rows
    far_start = (1 - mp_index) * rows
    gain_one, gain_two = gains[0:1], gains[1:2]

    def swap(x):
        return lax.ppermute(x, "mp", SWAP)

    def chunk(x):
        part = x.shape[0] // dp_count
        return lax.dynamic_slice_in_dim(x, dp_index * part, part, 0)

    def gather(x):
        return lax.all_gather(x, "dp", axis=0, tiled=True)

    far_tokens = swap(tokens)
    out_bf = w_out.astype(BF16)
    woven = weave(w_qkv.transpose(1, 0, 2), w_gateup, w_down)
    cosine, sine = pair_tables(slot_len)
    block_of = lambda start: (start // ROWS).astype(jnp.int32)
    base, far_base = block_of(row_start).reshape(1), block_of(far_start).reshape(1)
    own_part = project_qkv(base, tokens, first_values, gain_one, woven, cosine, sine, None)
    place_row = row_start + jnp.arange(rows, dtype=jnp.int32)
    dy = jnp.where((place_row < lengths[0])[:, None], cotangent, jnp.zeros_like(cotangent))
    far_tokens, own_part, woven, dy, out_bf = lax.optimization_barrier(
        (far_tokens, own_part, woven, dy, out_bf)
    )
    woven_chunk = swap(chunk(woven))
    norm_one, q, k, v = project_qkv(
        far_base, far_tokens, first_values, gain_one, woven, cosine, sine, own_part
    )
    scalars = jnp.concatenate([lengths, (1 - mp_index).reshape(1).astype(jnp.int32)])
    mixed, o_far = None, []
    for first, count in ((0, 1), (1, pairs - 2), (pairs - 1, 1)):
        o_all, lse_all, away = attend_pairs(first, count, scalars, q, k, v, mixed)
        if first == 0:
            o_all, woven_chunk = lax.optimization_barrier((o_all, woven_chunk))
            woven_far = gather(woven_chunk)
            out_far = swap(tie(out_bf, woven_chunk))
        mixed = o_all, lse_all
        o_far.append(swap(away))
    h, norm_two, o_cat = resid_rows(base, tokens, gain_two, out_bf, out_far, o_all, o_far)

    y_own, dn_own, grads_own = swiglu_half(place, norm_two, dy, woven, PARTS * head_cols)
    sum_own = lax.psum_scatter(grads_own, "dp", scatter_dimension=0, tiled=True)
    norm_two, woven_far = tie((norm_two, woven_far), y_own)
    y_far, dn_far, keep_far, send_far = swiglu_half(
        place, norm_two, dy, woven_far, PARTS * head_cols, 3 * hidden
    )
    got_far = move(send_far, CORE)
    output, dhb, do_own, *do_far, gain_two_part = after_rows(
        h, y_own, y_far, dn_own, dn_far, dy, gain_two, out_bf, out_far
    )
    theirs = [swap(do_far[0])]
    theirs.append(swap(tie(do_far[1], theirs[0])))
    keep_out, send_out = grad_out_of(place, dhb, o_cat)
    here_far, away_far = after_core(keep_far, tie(got_far, keep_out))
    got_far = move(away_far, CROSS)
    got_out = move(send_out, CORE)

    dqkv_far = []

    def back(first, count, theirs, at, before):
        first_grad, dqkv, away = attend_back_pairs(
            first, count, scalars, q, k, v, o_all, lse_all, do_own, theirs, at, cosine, sine, before
        )
        dqkv_far.append(swap(away))
        return first_grad, dqkv

    done = back(0, 1, tie(theirs[0], keep_out, away_far), 0, None)
    here_out, away_out = after_core(keep_out, tie(got_out, done))
    got_out = move(away_out, CROSS)
    done = back(1, pairs - 2, tie(theirs[1], away_out), 0, done)
    done, dqkv_far[0] = lax.optimization_barrier((done, dqkv_far[0]))
    keep_two, send_two, gain_first = grad_qkv_of(0, place, norm_one, done[1], woven, None)
    got_two = move(send_two, CORE)
    total_far = add(here_far, tie(got_far, keep_two)).astype(BF16)
    total_far, sum_own = lax.optimization_barrier((total_far, sum_own))
    sum_far = lax.psum_scatter(
        total_far, "dp", scatter_dimension=0, tiled=True, axis_index_groups=Z_LINES
    )
    done = back(pairs - 1, 1, tie(theirs[1], total_far), pairs - 2, done)
    (first_grad, dqkv), got_two, got_out = lax.optimization_barrier((done, got_two, got_out))

    here_two, away_two = after_core(keep_two, got_two)
    got_two = move(away_two, CROSS)
    keep_qkv, send_qkv, gain_last = grad_qkv_of(
        2, place, norm_one, tie(dqkv, away_two), woven, None
    )
    got_qkv = move(send_qkv, CORE)
    gain_one_part = jnp.sum(gain_first + gain_last, axis=1) / gains[0]
    parts = jnp.stack([gain_one_part, gain_two_part[0]], axis=0)
    near = move(parts, CORE)
    part = input_own(base, rows, tie(dqkv, keep_qkv), woven)
    got_qkv, near, got_two, dqkv_far[1], part = lax.optimization_barrier(
        (got_qkv, near, got_two, dqkv_far[1], part)
    )
    here_qkv, away_qkv = after_core(keep_qkv, got_qkv)
    got_qkv = move(away_qkv, CROSS)
    parts = parts + near
    cross = move(parts, CROSS)
    mine_mix, blocks_mix = after_cross(
        jnp.concatenate([here_two, here_out], axis=1), jnp.concatenate([got_two, got_out], axis=1), z
    )
    got_mix = tuple(move(b, p) for b, p in zip(blocks_mix, ALONG))
    got_far = swap(tie(sum_far, blocks_mix))
    input_grad = input_rows(
        tokens, tie(dhb, away_qkv, parts, blocks_mix, sum_far), gain_one, part, woven_far, dqkv_far
    )
    got_qkv, cross, got_far = tie((got_qkv, cross, got_far), input_grad)
    mine_qkv, blocks_qkv = after_cross(here_qkv, got_qkv, z)
    got_qkv = tuple(move(b, p) for b, p in zip(blocks_qkv, ALONG))
    sum_mix = after_along(mine_mix, tie(got_mix, blocks_qkv))
    early = keep_two.shape[1]
    got_out = swap(sum_mix[:, early : early + head_cols].astype(BF16))
    parts = parts + cross
    along = [move(parts, p) for p in ALONG]
    got_far = tie(got_far, blocks_qkv)

    gateup_down = step_mlp(
        dp_index, root_count, tie(sum_own, blocks_qkv, parts), got_far, w_gateup,
        moment_gateup, average_gateup, w_down, moment_down.T, average_down.T,
    )
    got_qkv, along, got_out = tie((got_qkv, along, got_out), gateup_down[0])
    parts = after_along(parts, along)
    gain_sum = parts + swap(parts)
    sum_qkv = after_along(mine_qkv, got_qkv)
    turn = lambda x: x.transpose(1, 0, 2)
    qkv_out = step_attention(
        dp_index, root_count, sum_mix, sum_qkv, got_out,
        turn(w_qkv), turn(moment_qkv), turn(average_qkv), w_out, moment_out.T, average_out.T,
    )
    gains_set = nesterov(gain_sum / root_count, gains, moment_gains, average_gains, RATE_GAINS)
    return (
        output,
        input_grad,
        first_grad,
        *(turn(x) for x in qkv_out[:4]),
        *(x.T for x in qkv_out[4:]),
        *gateup_down[:4],
        *(x.T for x in gateup_down[4:]),
        *gains_set,
    )


def solution(mesh):
    placed = (
        P(("dp", "mp"), None),
        P("dp", "mp"),
        P("dp"),
        P(("dp", "mp"), None),
        P(None, None, "mp"),
        P("mp", None),
        P(None, None, "mp"),
        P("mp", None),
        P(),
        P("dp", None, "mp"),
        P("mp", "dp"),
        P("dp", None, "mp"),
        P("mp", "dp"),
        P(),
        P("dp", None, "mp"),
        P("mp", "dp"),
        P("dp", None, "mp"),
        P("mp", "dp"),
        P(),
    )
    return jax.shard_map(
        shards_pair if (mesh.shape["dp"], mesh.shape["mp"]) == (16, 2) else shards_any,
        mesh=mesh,
        in_specs=placed,
        out_specs=(
            P(("dp", "mp"), None),
            P(("dp", "mp"), None),
            P("dp", "mp"),
            P("dp", None, "mp"),
            P("dp", None, "mp"),
            P("dp", None, "mp"),
            P("dp", None, "mp"),
            P("mp", "dp"),
            P("mp", "dp"),
            P("mp", "dp"),
            P("mp", "dp"),
            P("dp", None, "mp"),
            P("dp", None, "mp"),
            P("dp", None, "mp"),
            P("dp", None, "mp"),
            P("mp", "dp"),
            P("mp", "dp"),
            P("mp", "dp"),
            P("mp", "dp"),
            P(),
            P(),
            P(),
            P(),
        ),
        check_vma=False,
    )
```
